32 devices in a mesh: ctx: 8 (over y, x, core), wt: 4 (over z).
Axes of the slice: x: 2, y: 2, z: 4, core: 2. Of those that a mesh axis runs over, the one named last changes fastest.
Arguments:
- tokens: bfloat16 [4, 4096, 768], P('wt', 'ctx'), may hold values from -6 to 6
- cotangent: bfloat16 [4, 4096, 768], P('wt', 'ctx'), may hold values from -6 to 6
- lengths: int32 [4], P('wt'), may hold values from 1024 to 4096, as said below
- rand_blocks: int32 [4, 64, 12, 3], P('wt', 'ctx'), may hold values from 0 to 63, as said below
- query_weight: bfloat16 [768, 768], P('wt'), may hold values from -0.4375 to 0.4375
- key_weight: bfloat16 [768, 768], P('wt'), may hold values from -0.21875 to 0.21875
- value_weight: bfloat16 [768, 768], P('wt'), may hold values from -0.21875 to 0.21875
- output_weight: bfloat16 [768, 768], P('wt'), may hold values from -0.875 to 0.875
- expand_weight: bfloat16 [768, 3072], P('wt'), may hold values from -0.21875 to 0.21875
- contract_weight: bfloat16 [3072, 768], P('wt'), may hold values from -0.15625 to 0.15625
- query_bias: bfloat16 [768], P('wt'), may hold values from -3 to 3
- value_bias: bfloat16 [768], P('wt'), may hold values from -3 to 3
- output_bias: bfloat16 [768], P('wt'), may hold values from -2 to 2
- expand_bias: bfloat16 [3072], P('wt'), may hold values from -2 to 2
- contract_bias: bfloat16 [768], P('wt'), may hold values from -2 to 2
- attn_gain: bfloat16 [768], P('wt'), may hold values from 0.5 to 1.5
- attn_shift: bfloat16 [768], P('wt'), may hold values from -2 to 2
- ffn_gain: bfloat16 [768], P('wt'), may hold values from 0.5 to 1.5
- ffn_shift: bfloat16 [768], P('wt'), may hold values from -2 to 2
Outputs:
- layer_out: bfloat16 [4, 4096, 768], P('wt', 'ctx')
- input_grad: float32 [4, 4096, 768], P('wt', 'ctx')
- query_wgrad: float32 [768, 768], P('wt')
- key_wgrad: float32 [768, 768], P('wt')
- value_wgrad: float32 [768, 768], P('wt')
- output_wgrad: float32 [768, 768], P('wt')
- expand_wgrad: float32 [768, 3072], P('wt')
- contract_wgrad: float32 [3072, 768], P('wt')
- query_bgrad: float32 [768], P('wt')
- value_bgrad: float32 [768], P('wt')
- output_bgrad: float32 [768], P('wt')
- expand_bgrad: float32 [3072], P('wt')
- contract_bgrad: float32 [768], P('wt')
- attn_ggrad: float32 [768], P('wt')
- attn_sgrad: float32 [768], P('wt')
- ffn_ggrad: float32 [768], P('wt')
- ffn_sgrad: float32 [768], P('wt')
The draws below stay inside these ranges and needn't reach their ends.
Inputs may be any that keep to these rules, and one draw needn't show every extreme that they name: `lengths`: one sequence has exactly 4096 tokens. `rand_blocks`: entries of the row blocks of shard k (blocks k*8 .. k*8 + 7), for one head, are 24 blocks that lie, in a drawn order, one each on the shards k+1, k+2, ..., k+24, counted cyclically over the 8 shards; the block within that shard is drawn uniformly. So over all heads at most 36 entries of one shard lie on any one shard, and exactly 36 lie on the next shard. Entries of the first 2 row blocks are not used.
All inputs are finite; a program needn't handle non-finite values.
Results may differ from the reference program's by a relative error of at most 0.02.
Values may be sent and summed in bfloat16 or wider, within the bound.
No kernel may reach another device: no remote copies, remote signals or barrier semaphores. Data moves between devices by JAX's collectives and lax.ppermute only.
A program may use at most 384 MiB of HBM per device.

```python
import jax
import jax.numpy as jnp
from jax import lax

D = 768
H = 12
HD = 64
FF = 3072
BLOCK = 64
GLOB = 2
RAND = 3
RB = 8
SEQ_LEN = 4096
NB = 64
NSEQ = 4
LEN_MIN = 1024


def draw_lengths(key, part):
    key_draw = jax.random.fold_in(key, 11)
    key_pick = jax.random.fold_in(key, 12)
    draws_raw = jax.random.randint(key_draw, (NSEQ,), LEN_MIN, SEQ_LEN + 1)
    chosen = jax.random.randint(key_pick, (), 0, NSEQ)
    return jnp.where(jnp.arange(NSEQ) == chosen, SEQ_LEN, draws_raw).astype(jnp.int32)


def draw_rand_blocks(key, part):
    shards = NB // RB
    request_count = RAND * RB
    key_order = jax.random.fold_in(key, 21)
    key_local = jax.random.fold_in(key, 22)
    scores = jax.random.randint(key_order, (NSEQ, shards, H, request_count), 0, 1 << 20) * request_count
    scores = scores + jnp.arange(request_count, dtype=jnp.int32)
    ranking = jnp.argsort(scores, axis=-1).astype(jnp.int32)
    shard_ids = jnp.arange(shards, dtype=jnp.int32)[None, :, None, None]
    owners = (shard_ids + 1 + ranking) % shards
    within = jax.random.randint(key_local, (NSEQ, shards, H, request_count), 0, RB)
    blocks = (owners * RB + within).reshape(NSEQ, shards, H, RB, RAND)
    return jnp.transpose(blocks, (0, 1, 3, 2, 4)).reshape(NSEQ, NB, H, RAND).astype(jnp.int32)


def shard_levels(stream_key, shape, pieces, least, top_value):
    factor_of = 1.0
    for axis_at, parts in pieces:
        draws = jax.random.uniform(jax.random.fold_in(jax.random.fold_in(stream_key, 6), axis_at), (parts,), jnp.float32, least / len(pieces), top_value / len(pieces))
        factor_of = factor_of * jnp.repeat(jnp.exp(draws), shape[axis_at] // parts).reshape((-1,) + (1,) * (len(shape) - 1 - axis_at))
    return factor_of


def bell_draw(key, shape, spread, limit, cuts=(), kind=jnp.bfloat16):
    array = jax.random.normal(key, shape, jnp.float32) * spread
    if len(cuts) > 0:
        array = shard_levels(key, shape, cuts, -0.22, 0.18) * array
    return jnp.clip(array, min=-limit, max=limit).astype(kind)


def setup_inputs(seed: int = 0) -> dict:
    keys = jax.random.split(jax.random.key(seed), 20)
    tokens = bell_draw(keys[0], (NSEQ, SEQ_LEN, D), 1.0, 6.0, ((0, 4), (1, 8)))
    cotangent = bell_draw(keys[1], (NSEQ, SEQ_LEN, D), 1.0, 6.0, ((0, 4), (1, 8)))
    lengths = draw_lengths(jax.random.fold_in(keys[19], 71), 0)
    rand_blocks = draw_rand_blocks(jax.random.fold_in(keys[19], 71), 0)
    query_weight = bell_draw(keys[4], (D, D), (D // 4) ** -0.5, 0.4375, ((0, 4),))
    key_weight = bell_draw(keys[5], (D, D), D ** -0.5, 0.21875, ((0, 4),))
    value_weight = bell_draw(keys[6], (D, D), D ** -0.5, 0.21875, ((0, 4),))
    output_weight = bell_draw(keys[7], (D, D), (D // 16) ** -0.5, 0.875, ((0, 4),))
    expand_weight = bell_draw(keys[8], (D, FF), D ** -0.5, 0.21875, ((0, 4),))
    contract_weight = bell_draw(keys[9], (FF, D), (FF // 2) ** -0.5, 0.15625, ((0, 4),))
    query_bias = bell_draw(keys[10], (D,), 0.5, 3.0, ((0, 4),))
    value_bias = bell_draw(keys[11], (D,), 0.5, 3.0, ((0, 4),))
    output_bias = bell_draw(keys[12], (D,), 0.3, 2.0, ((0, 4),))
    expand_bias = bell_draw(keys[13], (FF,), 0.3, 2.0, ((0, 4),))
    contract_bias = bell_draw(keys[14], (D,), 0.3, 2.0, ((0, 4),))
    attn_gain = jnp.clip(1.0 + 0.1 * jax.random.normal(keys[15], (D,), jnp.float32), 0.5, 1.5).astype(jnp.bfloat16)
    attn_shift = bell_draw(keys[16], (D,), 0.3, 2.0, ((0, 4),))
    ffn_gain = jnp.clip(1.0 + 0.1 * jax.random.normal(keys[17], (D,), jnp.float32), 0.5, 1.5).astype(jnp.bfloat16)
    ffn_shift = bell_draw(keys[18], (D,), 0.3, 2.0, ((0, 4),))
    return dict(tokens=tokens, cotangent=cotangent, lengths=lengths, rand_blocks=rand_blocks, query_weight=query_weight, key_weight=key_weight, value_weight=value_weight, output_weight=output_weight, expand_weight=expand_weight, contract_weight=contract_weight, query_bias=query_bias, value_bias=value_bias, output_bias=output_bias, expand_bias=expand_bias, contract_bias=contract_bias, attn_gain=attn_gain, attn_shift=attn_shift, ffn_gain=ffn_gain, ffn_shift=ffn_shift)


PRECISE = lax.Precision.HIGHEST
EPSILON = 1e-12
NEGATIVE = -1e+30

@jax.custom_vjp
def low(v):
    return lax.optimization_barrier(v.astype(jnp.bfloat16)).astype(jnp.float32)

@jax.custom_vjp
def low_back(v):
    return v

def low_keep(v):
    return (low(v), None)

def low_pass(kept, grad):
    return (grad,)

def back_keep(v):
    return (v, None)

def back_low(kept, grad):
    return (low(grad),)
low.defvjp(low_keep, low_pass)
low_back.defvjp(back_keep, back_low)

def matmul(left_side, right_side):
    return jnp.dot(left_side, right_side, precision=PRECISE, preferred_element_type=jnp.float32)

def layer_norm(values, norm_gain, norm_shift):
    centered = values - lax.optimization_barrier(jnp.mean(values, axis=-1, keepdims=True))
    variance = lax.optimization_barrier(jnp.mean(centered * centered, axis=-1, keepdims=True))
    return centered * lax.rsqrt(variance + EPSILON) * norm_gain + norm_shift

def masked_softmax(scores, allowed):
    guarded = jnp.where(allowed, scores, NEGATIVE)
    summit = lax.optimization_barrier(jnp.max(guarded, axis=-1, keepdims=True))
    raised = jnp.where(allowed, jnp.exp(guarded - summit), 0.0)
    return raised / lax.optimization_barrier(jnp.sum(raised, axis=-1, keepdims=True))

def window_attention(queries, key_rows, values, usable, block_table):
    factor = HD ** (-0.5)
    listed_count = GLOB + 3 + RAND
    query_blocks = queries.reshape(NB, BLOCK, H, HD)
    key_heads = jnp.transpose(key_rows.reshape(NB, BLOCK, H, HD), (2, 0, 1, 3))
    value_heads = jnp.transpose(values.reshape(NB, BLOCK, H, HD), (2, 0, 1, 3))
    usable_blocks = usable.reshape(NB, BLOCK)
    head_index = jnp.arange(H, dtype=jnp.int32)[None, :, None]

    def one_group(group_index):
        start = (group_index * RB).astype(jnp.int32)
        blocks = start + jnp.arange(RB, dtype=jnp.int32)
        common = jnp.concatenate([jnp.broadcast_to(jnp.arange(GLOB, dtype=jnp.int32)[None, :], (RB, GLOB)), blocks[:, None] + jnp.arange(-1, 2, dtype=jnp.int32)[None, :]], axis=1)
        listed = jnp.concatenate([jnp.broadcast_to(common[:, None, :], (RB, H, GLOB + 3)), lax.dynamic_slice_in_dim(block_table, start, RB, 0).astype(jnp.int32)], axis=2)
        inside = (listed >= 0) & (listed < NB)
        clipped = jnp.clip(listed, 0, NB - 1).astype(jnp.int32)
        chosen_keys = key_heads[head_index, clipped]
        chosen_values = value_heads[head_index, clipped]
        allowed = inside[..., None] & usable_blocks[clipped]
        query_rows = lax.dynamic_slice_in_dim(query_blocks, start, RB, 0)
        scores = jnp.einsum('bqhd,bhjrd->bhqjr', query_rows, chosen_keys, precision=PRECISE) * factor
        scores = low_back(scores.reshape(RB, H, BLOCK, listed_count * BLOCK))
        weights = low(masked_softmax(scores, allowed.reshape(RB, H, 1, listed_count * BLOCK)))
        output = jnp.einsum('bhqjr,bhjrd->bqhd', weights.reshape(RB, H, BLOCK, listed_count, BLOCK), chosen_values, precision=PRECISE)
        return output.reshape(RB * BLOCK, H * HD)
    grouped = lax.map(jax.checkpoint(one_group), jnp.arange(NB // RB, dtype=jnp.int32))
    return grouped.reshape(SEQ_LEN, H * HD)

def global_attention(queries, key_rows, values, usable):
    factor = HD ** (-0.5)
    global_count = GLOB * BLOCK
    global_queries = queries[:global_count].reshape(global_count, H, HD)
    scores = jnp.einsum('qhd,khd->hqk', global_queries, key_rows.reshape(SEQ_LEN, H, HD), precision=PRECISE) * factor
    weights = masked_softmax(low_back(scores), usable[None, None, :])
    output = jnp.einsum('hqk,khd->qhd', weights, values.reshape(SEQ_LEN, H, HD), precision=PRECISE)
    return output.reshape(global_count, H * HD)

def sequence_forward(params, seq_tokens, seq_length, block_table):
    query_weight, key_weight, value_weight, output_weight, expand_weight, contract_weight, query_bias, value_bias, output_bias, expand_bias, contract_bias, attn_gain, attn_shift, ffn_gain, ffn_shift = params
    usable = jnp.arange(SEQ_LEN, dtype=jnp.int32) < seq_length
    queries = low(low_back(matmul(seq_tokens, query_weight) + query_bias))
    key_rows = low(low_back(matmul(seq_tokens, key_weight)))
    values = low(low_back(matmul(seq_tokens, value_weight) + value_bias))
    window_out = window_attention(queries, key_rows, values, usable, block_table)
    global_out = global_attention(queries, key_rows, values, usable)
    attended = jnp.concatenate([global_out, window_out[GLOB * BLOCK:]], axis=0)
    rounded = low(low_back(attended))
    branch = low_back(matmul(rounded, output_weight) + output_bias)
    normed_one = layer_norm(seq_tokens + branch, attn_gain, attn_shift)
    expand = low_back(matmul(low(normed_one), expand_weight) + expand_bias)
    hidden = low(jax.nn.gelu(expand, approximate=True))
    second = low_back(matmul(hidden, contract_weight) + contract_bias)
    result = layer_norm(normed_one + second, ffn_gain, ffn_shift)
    return jnp.where(usable[:, None], result, 0.0)

def reference(tokens, cotangent, lengths, rand_blocks, query_weight, key_weight, value_weight, output_weight, expand_weight, contract_weight, query_bias, value_bias, output_bias, expand_bias, contract_bias, attn_gain, attn_shift, ffn_gain, ffn_shift):
    params = tuple((member.astype(jnp.float32) for member in (query_weight, key_weight, value_weight, output_weight, expand_weight, contract_weight, query_bias, value_bias, output_bias, expand_bias, contract_bias, attn_gain, attn_shift, ffn_gain, ffn_shift)))
    inputs = tokens.astype(jnp.float32)
    cotangents = cotangent.astype(jnp.float32)

    def one_sequence(running, slices):
        seq_tokens, seq_cot, seq_length, block_table = slices

        def forward(params_in, tokens_in):
            return sequence_forward(params_in, tokens_in, seq_length, block_table)
        result, pullback = jax.vjp(forward, params, seq_tokens)
        param_grads, token_grad = pullback(seq_cot)
        running = jax.tree.map(lambda running_sum, addition: running_sum + addition, running, param_grads)
        return (running, (result.astype(jnp.bfloat16), token_grad))
    starting = tuple((jnp.zeros_like(member) for member in params))
    totals, (outputs, input_grads) = lax.scan(one_sequence, starting, (inputs, cotangents, lengths, rand_blocks))
    return (outputs, input_grads, totals[0], totals[1], totals[2], totals[3], totals[4], totals[5], totals[6], totals[7], totals[8], totals[9], totals[10], totals[11], totals[12], totals[13], totals[14])
```

```python
from functools import partial

import jax
import jax.numpy as jnp
from jax import lax
from jax.experimental import pallas as pl
from jax.experimental.pallas import tpu as pltpu
from jax.sharding import PartitionSpec as P

H = 12
HD = 64
BLOCK = 64
GLOB = 2
RAND = 3
PAIR = 2 * HD
PIECES = 8
NEGATIVE = -1e30
EPSILON = 1e-12
FACTOR = HD ** (-0.5)
F32 = jnp.float32
BF16 = jnp.bfloat16


def groups_of(shards):
    return [list(range(s, s + PIECES)) for s in range(0, shards, PIECES)]


def across_groups(shards):
    return [list(range(s, shards, PIECES)) for s in range(PIECES)]


def dot(a, b):
    return jnp.dot(a, b, preferred_element_type=F32)


def dot_t(a, b):
    return lax.dot_general(a, b, (((1,), (1,)), ((), ())), preferred_element_type=F32)


def t_dot(a, b):
    return lax.dot_general(a, b, (((0,), (0,)), ((), ())), preferred_element_type=F32)


def listed_rows(table, meta, pair, head, block, seq_blocks):
    length, first = meta[0], meta[1]
    own = first + block
    starts, limits = [], []
    for step in (-1, 0, 1):
        at = own + step
        inside = (at >= 0) & (at < seq_blocks)
        at = jnp.clip(at, 0, seq_blocks - 1)
        starts.append(pl.multiple_of(at * BLOCK, BLOCK))
        limits.append(jnp.where(inside, length - at * BLOCK, 0))
    for slot in range(RAND):
        at = table[(block * H + 2 * pair + head) * RAND + slot]
        starts.append(pl.multiple_of(at * BLOCK, BLOCK))
        limits.append(length - at * BLOCK)
    return starts, limits


def gathered(kv_ref, starts, columns):
    parts = [kv_ref[0 : GLOB * BLOCK, columns]]
    parts += [kv_ref[pl.ds(at, BLOCK), columns] for at in starts]
    return jnp.concatenate(parts, axis=0)


def forward_kernel(table, meta, q_ref, kv_ref, out_ref, p_ref, pg_ref, *, row_blocks, extra):
    pair = pl.program_id(0)
    rows = row_blocks * BLOCK
    seq = kv_ref.shape[0]
    listed = (GLOB + 3 + RAND) * BLOCK
    low = lax.broadcasted_iota(jnp.int32, (1, PAIR), 1) < HD
    lane = lax.broadcasted_iota(jnp.int32, (1, listed), 1)
    group = lane // BLOCK
    within = lane % BLOCK

    def one_block(block, carry):
        at = pl.multiple_of(block * BLOCK, BLOCK)
        q_both = q_ref[pl.ds(at, BLOCK), :]
        zero = jnp.zeros_like(q_both)
        outs = []
        for head in range(2):
            columns = slice(head * PAIR, (head + 1) * PAIR)
            q = jnp.where(low, zero, q_both) if head == 0 else jnp.where(low, q_both, zero)
            starts, limits = listed_rows(table, meta, pair, head, block, seq // BLOCK)
            kv = gathered(kv_ref, starts, columns)
            limit = jnp.full((1, listed), BLOCK, jnp.int32)
            for i, value in enumerate(limits):
                limit = jnp.where(group == GLOB + i, value, limit)
            scores = dot_t(q, kv) + jnp.where(within < limit, 0.0, NEGATIVE)
            raised = jnp.exp(scores - jnp.max(scores, axis=1, keepdims=True))
            probs = (raised / jnp.sum(raised, axis=1, keepdims=True)).astype(BF16)
            p_ref[block, head] = probs
            outs.append(dot(probs, kv))
        out_ref[pl.ds(at, BLOCK), :] = jnp.where(low, outs[0], outs[1]).astype(BF16)
        return carry

    lax.fori_loop(0, row_blocks, one_block, 0)

    q_both = q_ref[rows : rows + extra, :]
    zero = jnp.zeros_like(q_both)
    wide = jnp.concatenate(
        [
            jnp.concatenate([jnp.where(low, zero, q_both), zero], axis=1),
            jnp.concatenate([zero, jnp.where(low, q_both, zero)], axis=1),
        ],
        axis=0,
    )
    position = lax.broadcasted_iota(jnp.int32, (1, seq), 1)
    scores = dot_t(wide, kv_ref[...]) + jnp.where(position < meta[0], 0.0, NEGATIVE)
    raised = jnp.exp(scores - jnp.max(scores, axis=1, keepdims=True))
    probs = (raised / jnp.sum(raised, axis=1, keepdims=True)).astype(BF16)
    pg_ref[0] = probs
    out = dot(probs, kv_ref[...])
    out_ref[rows : rows + extra, :] = jnp.where(
        low, out[:extra, :PAIR], out[extra:, PAIR:]
    ).astype(BF16)


def backward_kernel(
    table, meta, q_ref, do_ref, kv_ref, p_ref, pg_ref, dq_ref, dkv_ref, acc, *, row_blocks, extra
):
    pair = pl.program_id(0)
    rows = row_blocks * BLOCK
    seq = kv_ref.shape[0]
    low = lax.broadcasted_iota(jnp.int32, (1, PAIR), 1) < HD

    q_both = q_ref[rows : rows + extra, :]
    do_both = do_ref[rows : rows + extra, :]
    zero = jnp.zeros_like(q_both)
    wide_q = jnp.concatenate(
        [
            jnp.concatenate([jnp.where(low, zero, q_both), zero], axis=1),
            jnp.concatenate([zero, jnp.where(low, q_both, zero)], axis=1),
        ],
        axis=0,
    )
    wide_do = jnp.concatenate(
        [
            jnp.concatenate([jnp.where(low, do_both, zero), zero], axis=1),
            jnp.concatenate([zero, jnp.where(low, zero, do_both)], axis=1),
        ],
        axis=0,
    )
    probs = pg_ref[0]
    wide = probs.astype(F32)
    dp = dot_t(wide_do, kv_ref[...])
    ds = (wide * (dp - jnp.sum(wide * dp, axis=1, keepdims=True))).astype(BF16)
    dq = dot(ds, kv_ref[...])
    dq_ref[rows : rows + extra, :] = (
        jnp.where(low, dq[extra:, PAIR:], dq[:extra, :PAIR]) * FACTOR
    ).astype(BF16)
    acc[...] = t_dot(
        jnp.concatenate([probs, ds], axis=0), jnp.concatenate([wide_do, wide_q], axis=0)
    )

    def one_block(block, carry):
        at = pl.multiple_of(block * BLOCK, BLOCK)
        q_both = q_ref[pl.ds(at, BLOCK), :]
        do_both = do_ref[pl.ds(at, BLOCK), :]
        zero = jnp.zeros_like(q_both)
        dqs = []
        for head in range(2):
            columns = slice(head * PAIR, (head + 1) * PAIR)
            q = jnp.where(low, zero, q_both) if head == 0 else jnp.where(low, q_both, zero)
            do = jnp.where(low, do_both, zero) if head == 0 else jnp.where(low, zero, do_both)
            starts, _ = listed_rows(table, meta, pair, head, block, seq // BLOCK)
            kv = gathered(kv_ref, starts, columns)
            probs = p_ref[block, head]
            wide = probs.astype(F32)
            dp = dot_t(do, kv)
            ds = (wide * (dp - jnp.sum(wide * dp, axis=1, keepdims=True))).astype(BF16)
            dqs.append(dot(ds, kv))
            dkv = t_dot(jnp.concatenate([probs, ds], axis=0), jnp.concatenate([do, q], axis=0))
            acc[0 : GLOB * BLOCK, columns] += dkv[: GLOB * BLOCK]
            for i, start in enumerate(starts):
                here = dkv[(GLOB + i) * BLOCK : (GLOB + i + 1) * BLOCK]
                acc[pl.ds(start, BLOCK), columns] += here
        dq_ref[pl.ds(at, BLOCK), :] = (jnp.where(low, dqs[1], dqs[0]) * FACTOR).astype(BF16)
        return carry

    lax.fori_loop(0, row_blocks, one_block, 0)
    dkv_ref[...] = acc[...].astype(BF16)


def attention_forward(table, meta, q, kv, row_blocks, extra):
    rows, seq, pairs = q.shape[0], kv.shape[0], H // 2
    listed = (GLOB + 3 + RAND) * BLOCK
    return pl.pallas_call(
        partial(forward_kernel, row_blocks=row_blocks, extra=extra),
        grid_spec=pltpu.PrefetchScalarGridSpec(
            num_scalar_prefetch=2,
            grid=(pairs,),
            in_specs=[
                pl.BlockSpec((rows, PAIR), lambda p, *_: (0, p)),
                pl.BlockSpec((seq, 2 * PAIR), lambda p, *_: (0, p)),
            ],
            out_specs=[
                pl.BlockSpec((rows, PAIR), lambda p, *_: (0, p)),
                pl.BlockSpec((row_blocks, 2, BLOCK, listed), lambda p, *_: (0, p, 0, 0)),
                pl.BlockSpec((1, 2 * extra, seq), lambda p, *_: (p, 0, 0)),
            ],
        ),
        out_shape=[
            jax.ShapeDtypeStruct((rows, H * HD), BF16),
            jax.ShapeDtypeStruct((row_blocks, H, BLOCK, listed), BF16),
            jax.ShapeDtypeStruct((pairs, 2 * extra, seq), BF16),
        ],
        compiler_params=pltpu.CompilerParams(vmem_limit_bytes=50 * 2**20),
        name="attention_forward",
    )(table, meta, q, kv)


def attention_backward(table, meta, q, do, kv, probs, global_probs, row_blocks, extra):
    rows, seq, pairs = q.shape[0], kv.shape[0], H // 2
    listed = (GLOB + 3 + RAND) * BLOCK
    tile = pl.BlockSpec((rows, PAIR), lambda p, *_: (0, p))
    wide = pl.BlockSpec((seq, 2 * PAIR), lambda p, *_: (0, p))
    return pl.pallas_call(
        partial(backward_kernel, row_blocks=row_blocks, extra=extra),
        grid_spec=pltpu.PrefetchScalarGridSpec(
            num_scalar_prefetch=2,
            grid=(pairs,),
            in_specs=[
                tile,
                tile,
                wide,
                pl.BlockSpec((row_blocks, 2, BLOCK, listed), lambda p, *_: (0, p, 0, 0)),
                pl.BlockSpec((1, 2 * extra, seq), lambda p, *_: (p, 0, 0)),
            ],
            out_specs=[tile, wide],
            scratch_shapes=[pltpu.VMEM((seq, 2 * PAIR), F32)],
        ),
        out_shape=[
            jax.ShapeDtypeStruct((rows, H * HD), BF16),
            jax.ShapeDtypeStruct((seq, 2 * H * HD), BF16),
        ],
        compiler_params=pltpu.CompilerParams(vmem_limit_bytes=58 * 2**20),
        name="attention_backward",
    )(table, meta, q, do, kv, probs, global_probs)


def swap_heads(columns):
    lead = columns.shape[:-1]
    split = columns.reshape(*lead, H // 2, 2, HD)
    return jnp.concatenate([split[..., 1, :], split[..., 0, :]], axis=-1).reshape(*lead, H * HD)


def interleave(keys, values):
    lead = keys.shape[:-1]
    k, v = (a.reshape(*lead, H // 2, 2, HD) for a in (keys, values))
    parts = [v[..., 0, :], k[..., 0, :], k[..., 1, :], v[..., 1, :]]
    return jnp.concatenate(parts, axis=-1).reshape(*lead, 2 * H * HD)


def separate(columns):
    lead = columns.shape[:-1]
    split = columns.reshape(*lead, H // 2, 4, HD)
    keys = jnp.concatenate([split[..., 1, :], split[..., 2, :]], axis=-1)
    values = jnp.concatenate([split[..., 0, :], split[..., 3, :]], axis=-1)
    return keys.reshape(*lead, H * HD), values.reshape(*lead, H * HD)


def in_pieces(grad, parts, width):
    rows, columns = grad.shape
    split = grad.reshape(parts, PIECES, rows // parts // PIECES, columns // width, width)
    return jnp.transpose(split, (1, 0, 3, 2, 4)).reshape(PIECES, parts, -1, width)


def from_pieces(pieces, columns, width):
    split = pieces.reshape(PIECES, columns // width, -1, width)
    return jnp.transpose(split, (0, 2, 1, 3)).reshape(-1, columns)


def reduced(pieces, shards):
    mine = lax.psum_scatter(
        pieces, "ctx", scatter_dimension=0, axis_index_groups=groups_of(shards), tiled=False
    )
    if shards > PIECES:
        mine = lax.psum(mine, "ctx", axis_index_groups=across_groups(shards))
    mine = lax.psum_scatter(mine, "wt", scatter_dimension=0, tiled=False)
    return lax.all_gather(mine, "ctx", axis_index_groups=groups_of(shards))


def body(
    tokens,
    cotangent,
    lengths,
    rand_blocks,
    query_weight,
    key_weight,
    value_weight,
    output_weight,
    expand_weight,
    contract_weight,
    query_bias,
    value_bias,
    output_bias,
    expand_bias,
    contract_bias,
    attn_gain,
    attn_shift,
    ffn_gain,
    ffn_shift,
):
    shards = lax.axis_size("ctx")
    parts = lax.axis_size("wt")
    c = lax.axis_index("ctx")
    rows, width = tokens.shape[1], tokens.shape[2]
    row_blocks = rows // BLOCK
    global_count = GLOB * BLOCK
    extra = 16 * (-(-global_count // (16 * shards)))
    hidden_width = expand_weight.shape[1]
    length = lengths[0]
    inputs = tokens[0]

    everything = lax.all_gather(inputs, "ctx", axis=0, tiled=True)
    qkv_shard = jnp.concatenate(
        [swap_heads(query_weight), interleave(key_weight, value_weight)], axis=1
    )
    w_qkv = lax.all_gather(qkv_shard, "wt", axis=0, tiled=True)
    w_query, w_kv = w_qkv[:, :width], w_qkv[:, width:]

    small = jnp.concatenate(
        [
            query_bias,
            value_bias,
            output_bias,
            contract_bias,
            attn_gain,
            attn_shift,
            ffn_gain,
            ffn_shift,
            expand_bias,
        ]
    ).reshape(1, -1)
    small = lax.all_gather(small, "wt", axis=0, tiled=True)
    each = width // parts
    b_query, b_value, b_output, b_contract, g_attn, s_attn, g_ffn, s_ffn = (
        small[:, i * each : (i + 1) * each].reshape(-1).astype(F32) for i in range(8)
    )
    b_expand = small[:, 8 * each :].reshape(-1).astype(F32)

    others = jnp.concatenate(
        [
            in_pieces(output_weight, 1, width)[:, 0],
            in_pieces(expand_weight, 1, width)[:, 0],
            in_pieces(contract_weight, 1, width)[:, 0],
        ],
        axis=1,
    )
    others = lax.dynamic_index_in_dim(others, c % PIECES, 0, keepdims=False)
    others = lax.all_gather(others, "wt")
    others = lax.all_gather(others, "ctx", axis_index_groups=groups_of(shards))
    n_out = width // parts // PIECES
    n_exp = n_out * (hidden_width // width)

    def whole(pieces, columns):
        pieces = jnp.transpose(pieces, (1, 0, 2, 3))
        return jax.vmap(lambda a: from_pieces(a, columns, width))(pieces).reshape(-1, columns)

    w_output = whole(others[:, :, :n_out], width)
    w_expand = whole(others[:, :, n_out : n_out + n_exp], hidden_width)
    w_contract = whole(others[:, :, n_out + n_exp :], width)

    start = jnp.minimum(c * extra, everything.shape[0] - extra)
    x = jnp.concatenate([inputs, lax.dynamic_slice_in_dim(everything, start, extra, 0)], axis=0)
    first_cot = jnp.where(c == 0, cotangent[0, :global_count], jnp.zeros((), BF16))
    first_cot = lax.psum(first_cot, "ctx")
    first_cot = jnp.pad(first_cot, ((0, max(0, shards * extra - global_count)), (0, 0)))
    cot = jnp.concatenate(
        [cotangent[0], lax.dynamic_slice_in_dim(first_cot, c * extra, extra, 0)], axis=0
    )
    index = jnp.arange(rows + extra, dtype=jnp.int32)
    position = jnp.where(index < rows, c * rows + index, c * extra + index - rows)
    is_global = position < global_count
    usable = (position < length) & (is_global == (index >= rows))

    q = ((dot(x, w_query) + swap_heads(b_query)).astype(BF16) * FACTOR).astype(BF16)
    kv = (dot(everything, w_kv) + interleave(jnp.zeros_like(b_value), b_value)).astype(BF16)
    table = rand_blocks.reshape(-1)
    meta = jnp.stack([length, c * row_blocks]).astype(jnp.int32)
    attended, probs, global_probs = attention_forward(table, meta, q, kv, row_blocks, extra)

    residual = x.astype(F32) + dot(attended, w_output) + b_output
    centered = residual - jnp.mean(residual, axis=1, keepdims=True)
    root_one = lax.rsqrt(jnp.mean(centered * centered, axis=1, keepdims=True) + EPSILON)
    norm_one = centered * root_one
    normed_one = norm_one * g_attn + s_attn
    normed_low = normed_one.astype(BF16)
    expand = dot(normed_low, w_expand) + b_expand
    hidden = jax.nn.gelu(expand, approximate=True).astype(BF16)
    second = normed_one + dot(hidden, w_contract) + b_contract
    centered = second - jnp.mean(second, axis=1, keepdims=True)
    root_two = lax.rsqrt(jnp.mean(centered * centered, axis=1, keepdims=True) + EPSILON)
    norm_two = centered * root_two
    result = norm_two * g_ffn + s_ffn
    layer_out = jnp.where(usable[:, None], result, 0.0).astype(BF16)

    grad_result = jnp.where(usable[:, None], cot.astype(F32), 0.0)
    ffn_ggrad = jnp.sum(grad_result * norm_two, axis=0)
    ffn_sgrad = jnp.sum(grad_result, axis=0)
    e = g_ffn * grad_result
    grad_two = root_two * (
        e
        - jnp.mean(e, axis=1, keepdims=True)
        - norm_two * jnp.mean(e * norm_two, axis=1, keepdims=True)
    )
    grad_second = grad_two.astype(BF16)
    contract_grad = t_dot(hidden, grad_second)
    contract_bgrad = jnp.sum(grad_second.astype(F32), axis=0)
    grad_hidden = dot_t(grad_second, w_contract)
    gelu_back = jax.vjp(partial(jax.nn.gelu, approximate=True), expand)[1]
    grad_expand = gelu_back(grad_hidden)[0].astype(BF16)
    expand_grad = t_dot(normed_low, grad_expand)
    expand_bgrad = jnp.sum(grad_expand.astype(F32), axis=0)
    grad_first = grad_two + dot_t(grad_expand, w_expand)
    attn_ggrad = jnp.sum(grad_first * norm_one, axis=0)
    attn_sgrad = jnp.sum(grad_first, axis=0)
    e = g_attn * grad_first
    grad_one = root_one * (
        e
        - jnp.mean(e, axis=1, keepdims=True)
        - norm_one * jnp.mean(e * norm_one, axis=1, keepdims=True)
    )
    grad_branch = grad_one.astype(BF16)
    output_grad = t_dot(attended, grad_branch)
    output_bgrad = jnp.sum(grad_branch.astype(F32), axis=0)
    grad_attended = dot_t(grad_branch, w_output).astype(BF16)

    early = reduced(
        jnp.concatenate(
            [
                in_pieces(contract_grad.astype(BF16), parts, width),
                in_pieces(expand_grad.astype(BF16), parts, width),
                in_pieces(output_grad.astype(BF16), parts, width),
            ],
            axis=2,
        ),
        shards,
    ).astype(F32)
    n_con = hidden_width // parts // PIECES
    contract_wgrad = from_pieces(early[:, :n_con], width, width)
    expand_wgrad = from_pieces(early[:, n_con : n_con + n_exp], hidden_width, width)
    output_wgrad = from_pieces(early[:, n_con + n_exp :], width, width)

    dq, dkv = attention_backward(
        table, meta, q, grad_attended, kv, probs, global_probs, row_blocks, extra
    )
    qkv_grad = jnp.concatenate([t_dot(x, dq), t_dot(everything, dkv)], axis=1).astype(BF16)
    query_bgrad = swap_heads(jnp.sum(dq.astype(F32), axis=0))
    _, value_bgrad = separate(jnp.sum(dkv.astype(F32), axis=0))
    vectors = jnp.concatenate(
        [
            a.reshape(parts, -1)
            for a in (
                query_bgrad,
                value_bgrad,
                output_bgrad,
                contract_bgrad,
                attn_ggrad,
                attn_sgrad,
                ffn_ggrad,
                ffn_sgrad,
                expand_bgrad,
            )
        ],
        axis=1,
    )
    vector_rows = -(-vectors.shape[1] // (PIECES * width))
    vectors = jnp.pad(vectors, ((0, 0), (0, vector_rows * PIECES * width - vectors.shape[1])))
    vectors = vectors.reshape(parts, PIECES, vector_rows, width).transpose(1, 0, 2, 3)
    late = reduced(
        jnp.concatenate([in_pieces(qkv_grad, parts, width), vectors.astype(BF16)], axis=2), shards
    ).astype(F32)
    qkv_wgrad = from_pieces(late[:, :-vector_rows], 3 * width, width)
    query_wgrad = swap_heads(qkv_wgrad[:, :width])
    key_wgrad, value_wgrad = separate(qkv_wgrad[:, width:])
    vectors = late[:, -vector_rows:].reshape(-1)
    small_grads = [vectors[i * each : (i + 1) * each] for i in range(8)]
    expand_bias_grad = vectors[8 * each : 8 * each + hidden_width // parts]

    grad_x = dot_t(dkv, w_kv)
    own = grad_one + dot_t(dq, w_query)
    share = jnp.where(c * extra < global_count, own[rows:], 0.0)
    here = lax.dynamic_slice_in_dim(grad_x, start, extra, 0)
    grad_x = lax.dynamic_update_slice_in_dim(grad_x, here + share, start, 0)
    input_grad = own[:rows] + lax.psum_scatter(
        grad_x.astype(BF16), "ctx", scatter_dimension=0, tiled=True
    ).astype(F32)

    finished = lax.all_gather(layer_out[rows:], "ctx", axis=0, tiled=True)
    on_first = (c == 0) & (index[:rows] < global_count)
    finished = jnp.pad(finished[:global_count], ((0, rows - global_count), (0, 0)))
    layer_out = jnp.where(on_first[:, None], finished, layer_out[:rows])

    return (
        layer_out[None],
        input_grad[None],
        query_wgrad,
        key_wgrad,
        value_wgrad,
        output_wgrad,
        expand_wgrad,
        contract_wgrad,
        small_grads[0],
        small_grads[1],
        small_grads[2],
        expand_bias_grad,
        small_grads[3],
        small_grads[4],
        small_grads[5],
        small_grads[6],
        small_grads[7],
    )


def solution(mesh):
    tokens, weight, vector = P("wt", "ctx", None), P("wt", None), P("wt")
    return jax.shard_map(
        body,
        mesh=mesh,
        in_specs=(tokens, tokens, vector, P("wt", "ctx", None, None)) + (weight,) * 6 + (vector,) * 9,
        out_specs=(tokens, tokens) + (weight,) * 6 + (vector,) * 9,
        check_vma=False,
    )
```

```python
from functools import partial, reduce

import jax
import jax.numpy as jnp
from jax import lax
from jax.experimental import pallas as pl
from jax.experimental.pallas import tpu as pltpu
from jax.sharding import PartitionSpec as P

H = 12
HD = 64
BLOCK = 64
GLOB = 2
RAND = 3
PAIR = 2 * HD
PAIRS = H // 2
AHEAD = 2
GROUPS = ((0, AHEAD), (AHEAD, PAIRS - AHEAD))
BACK = ((0, 0, 2), (1, 0, 2), (1, 2, 1), (1, 3, 1))
BACK_COST = (8, 8, 8, 20)
MOVING = 3 + RAND
UNROLL = 2
LISTED = (GLOB + MOVING) * BLOCK
PIECES = 8
NEGATIVE = -1e30
EPSILON = 1e-12
FACTOR = HD ** (-0.5)
SLOPE = (2.0 / jnp.pi) ** 0.5
CUBIC = 0.044715
F32 = jnp.float32
BF16 = jnp.bfloat16
MIB = 2**20


def taking(microseconds):
    return pl.CostEstimate(
        flops=int(microseconds * 10**9), bytes_accessed=10**6, transcendentals=0
    )


def groups_of(shards):
    return [list(range(s, s + PIECES)) for s in range(0, shards, PIECES)]


def across_groups(shards):
    return [list(range(s, shards, PIECES)) for s in range(PIECES)]


def dot(a, b):
    return jnp.dot(a, b, preferred_element_type=F32)


def dot_t(a, b):
    return lax.dot_general(a, b, (((1,), (1,)), ((), ())), preferred_element_type=F32)


def t_dot(a, b):
    return lax.dot_general(a, b, (((0,), (0,)), ((), ())), preferred_element_type=F32)


def after(value, *earlier):
    return pl.pallas_call(
        lambda *refs: None,
        in_specs=[pl.BlockSpec(memory_space=pl.ANY)] * (1 + len(earlier)),
        out_specs=pl.BlockSpec(memory_space=pl.ANY),
        out_shape=jax.ShapeDtypeStruct(value.shape, value.dtype),
        input_output_aliases={0: 0},
        name="after",
    )(value, *earlier)


def by_head(both, low, inner):
    zero = jnp.zeros_like(both)
    first, second = jnp.where(low, both, zero), jnp.where(low, zero, both)
    if inner:
        first, second = second, first
    return jnp.concatenate(
        [jnp.concatenate([first, zero], axis=1), jnp.concatenate([zero, second], axis=1)], axis=0
    )


def listed_keys(starts, spot, top, kv_ref):
    rows = [
        [pl.multiple_of(starts[spot + head * MOVING + i], BLOCK) for i in range(MOVING)]
        for head in range(2)
    ]
    parts = [kv_ref[pl.ds(top, GLOB * BLOCK), :]]
    parts += [kv_ref[pl.ds(at, BLOCK), :] for at in rows[0][:3]]
    parts += [
        jnp.concatenate(
            [kv_ref[pl.ds(first, BLOCK), :PAIR], kv_ref[pl.ds(second, BLOCK), PAIR:]], axis=1
        )
        for first, second in zip(rows[0][3:], rows[1][3:])
    ]
    return jnp.concatenate(parts, axis=0), rows


def loader(refs, streamed):
    if not streamed:
        return lambda i: refs[i][...]
    buffer, semaphore = streamed

    def load(i):
        copy = pltpu.make_async_copy(refs[i], buffer, semaphore)
        copy.start()
        copy.wait()
        return buffer[...]

    return load


def softmax(scores):
    raised = jnp.exp(scores - jnp.max(scores, axis=0, keepdims=True))
    return (raised * (1.0 / jnp.sum(raised, axis=0, keepdims=True))).astype(BF16)


def by_core(grad, core, parts):
    half = grad.shape[0] // parts // 2
    halves = [
        jnp.concatenate([grad[at : at + half] for at in range(i * half, grad.shape[0], 2 * half)])
        for i in range(2)
    ]
    first = core == 0
    return jnp.where(first, halves[0], halves[1]), jnp.where(first, halves[1], halves[0])


def forward_kernel(
    starts, limits, x_ref, w_ref, b_ref, *rest, first, row_blocks, extra, shards, waits
):
    seen_refs = rest[:shards]
    q_ref, kv_ref, out_ref, p_ref, pg_ref = rest[shards + waits :][:5]
    tokens = loader(seen_refs, rest[shards + waits + 5 :])
    top = pl.multiple_of(starts[row_blocks * H * MOVING], BLOCK)
    pair = first + pl.program_id(0)
    rows = row_blocks * BLOCK
    low = lax.broadcasted_iota(jnp.int32, (1, PAIR), 1) < HD
    within = lax.broadcasted_iota(jnp.int32, (BLOCK, PAIR), 0)

    queries = dot(x_ref[...], w_ref[:, :PAIR]) + b_ref[0, :, :PAIR]
    q_ref[...] = (queries.astype(BF16).astype(F32) * FACTOR).astype(BF16)

    for i in range(shards):
        kv = dot(tokens(i), w_ref[:, PAIR:]) + b_ref[0, :, PAIR:]
        kv_ref[i * rows : (i + 1) * rows, :] = kv.astype(BF16)

    def one_block(block, carry):
        at = pl.ds(pl.multiple_of(block * BLOCK, BLOCK), BLOCK)
        spot = (block * H + 2 * pair) * MOVING
        kv, _ = listed_keys(starts, spot, top, kv_ref)
        scores = dot_t(kv, by_head(q_ref[at, :], low, True))
        masked = [scores[: GLOB * BLOCK]]
        for i in range(MOVING):
            limit = jnp.where(low, limits[spot + i], limits[spot + MOVING + i])
            here = scores[(GLOB + i) * BLOCK : (GLOB + i + 1) * BLOCK]
            masked.append(jnp.where(within < limit, here, NEGATIVE))
        probs = softmax(jnp.concatenate(masked, axis=0))
        p_ref[block, 0] = probs
        out = t_dot(probs, kv)
        out_ref[at, :] = jnp.where(low, out[:BLOCK, :PAIR], out[BLOCK:, PAIR:]).astype(BF16)
        return carry

    lax.fori_loop(0, row_blocks, one_block, 0, unroll=UNROLL)

    wide = by_head(q_ref[rows : rows + extra, :], low, True)
    within = lax.broadcasted_iota(jnp.int32, (rows, 2 * extra), 0)
    scores = []
    for i in range(shards):
        limit = limits[row_blocks * H * MOVING + i]
        here = dot_t(kv_ref[i * rows : (i + 1) * rows, :], wide)
        scores.append(jnp.where(within < limit, here, NEGATIVE))
    summit = jnp.max(reduce(jnp.maximum, scores), axis=0, keepdims=True)
    raised = [jnp.exp(here - summit) for here in scores]
    share = 1.0 / jnp.sum(reduce(jnp.add, raised), axis=0, keepdims=True)
    out = None
    for i in range(shards):
        here = slice(i * rows, (i + 1) * rows)
        probs = (raised[i] * share).astype(BF16)
        pg_ref[0, here, :] = probs
        term = t_dot(probs, kv_ref[here, :])
        out = term if out is None else out + term
    out_ref[rows : rows + extra, :] = jnp.where(
        low, out[:extra, :PAIR], out[extra:, PAIR:]
    ).astype(BF16)


def backward_kernel(
    starts,
    x_ref,
    q_ref,
    do_ref,
    kv_ref,
    p_ref,
    pg_ref,
    *rest,
    first,
    row_blocks,
    extra,
    shards,
    parts,
    waits,
):
    seen_refs = rest[:shards]
    dq_ref, dkv_ref, near_ref, away_ref, qsum_ref, vsum_ref, acc = rest[shards + waits :][:7]
    tokens = loader(seen_refs, rest[shards + waits + 7 :])
    core = starts[row_blocks * H * MOVING + 1]
    top = pl.multiple_of(starts[row_blocks * H * MOVING], BLOCK)
    pair = first + pl.program_id(0)
    rows = row_blocks * BLOCK
    low = lax.broadcasted_iota(jnp.int32, (1, PAIR), 1) < HD

    def back(kv, probs, q_both, do_both):
        count = q_both.shape[0]
        wide_do = by_head(do_both, low, False)
        wide = probs.astype(F32)
        dp = dot_t(kv, wide_do)
        ds = (wide * (dp - jnp.sum(wide * dp, axis=0, keepdims=True))).astype(BF16)
        dq = t_dot(ds, kv)
        dq = (jnp.where(low, dq[count:, PAIR:], dq[:count, :PAIR]) * FACTOR).astype(BF16)
        rows_in = jnp.concatenate([wide_do, by_head(q_both, low, True)], axis=0)
        return dq, dot(jnp.concatenate([probs, ds], axis=1), rows_in)

    last = slice(rows, rows + extra)
    wide_do = by_head(do_ref[last, :], low, False)
    cuts = [slice(i * rows, (i + 1) * rows) for i in range(shards)]
    dps = [dot_t(kv_ref[here, :], wide_do) for here in cuts]
    terms = [pg_ref[0, here, :].astype(F32) * dp for here, dp in zip(cuts, dps)]
    delta = jnp.sum(reduce(jnp.add, terms), axis=0, keepdims=True)
    rows_in = jnp.concatenate([wide_do, by_head(q_ref[last, :], low, True)], axis=0)
    dq = None
    for here, dp in zip(cuts, dps):
        probs = pg_ref[0, here, :]
        ds = (probs.astype(F32) * (dp - delta)).astype(BF16)
        term = t_dot(ds, kv_ref[here, :])
        dq = term if dq is None else dq + term
        acc[here, :] = dot(jnp.concatenate([probs, ds], axis=1), rows_in)
    dq = jnp.where(low, dq[extra:, PAIR:], dq[:extra, :PAIR]) * FACTOR
    dq_ref[last, :] = dq.astype(BF16)

    def one_block(block, carry):
        at = pl.ds(pl.multiple_of(block * BLOCK, BLOCK), BLOCK)
        spot = (block * H + 2 * pair) * MOVING
        kv, places = listed_keys(starts, spot, top, kv_ref)
        dq_ref[at, :], dkv = back(kv, p_ref[block, 0], q_ref[at, :], do_ref[at, :])
        acc[pl.ds(top, GLOB * BLOCK), :] += dkv[: GLOB * BLOCK]
        for i in range(MOVING):
            here = dkv[(GLOB + i) * BLOCK : (GLOB + i + 1) * BLOCK]
            if i < 3:
                acc[pl.ds(places[0][i], BLOCK), :] += here
            else:
                acc[pl.ds(places[0][i], BLOCK), :PAIR] += here[:, :PAIR]
                acc[pl.ds(places[1][i], BLOCK), PAIR:] += here[:, PAIR:]
        return carry

    lax.fori_loop(0, row_blocks, one_block, 0, unroll=UNROLL)
    dkv_ref[...] = acc[...].astype(BF16)
    total = jnp.sum(acc[...], axis=0, keepdims=True)
    vsum_ref[0] = jnp.where(low, total[:, :PAIR], total[:, PAIR:])
    total = jnp.sum(dq_ref[...].astype(F32), axis=0, keepdims=True)
    qsum_ref[0] = jnp.concatenate([total[:, HD:], total[:, :HD]], axis=1)
    near, away = by_core(t_dot(x_ref[...], dq_ref[...]), core, parts)
    near_ref[:, :PAIR], away_ref[:, :PAIR] = near.astype(BF16), away.astype(BF16)
    total = None
    for i in range(shards):
        term = t_dot(tokens(i), dkv_ref[i * rows : (i + 1) * rows, :])
        total = term if total is None else total + term
    near, away = by_core(total, core, parts)
    near_ref[:, PAIR:], away_ref[:, PAIR:] = near.astype(BF16), away.astype(BF16)


def piece_specs(rows, width, shards):
    if shards > PIECES:
        scratch = [pltpu.VMEM((rows, width), BF16), pltpu.SemaphoreType.DMA]
        return [pl.BlockSpec(memory_space=pl.ANY)] * shards, scratch
    spec = pl.BlockSpec((rows, width), lambda p, *_: (0, 0), pipeline_mode=pl.Buffered(1))
    return [spec] * shards, []


def long_spec(shape, place, shards):
    if shards > PIECES:
        return pl.BlockSpec(shape, place, pipeline_mode=pl.Buffered(1))
    return pl.BlockSpec(shape, place)


def attention_forward(starts, limits, x, pieces, weights, b_qkv, waits, first, count, extra):
    rows, width, shards = x.shape[0], x.shape[1], len(pieces)
    seq = shards * (rows - extra)
    row_blocks = (rows - extra) // BLOCK
    specs, scratch = piece_specs(rows - extra, width, shards)
    return pl.pallas_call(
        partial(
            forward_kernel,
            first=first,
            row_blocks=row_blocks,
            extra=extra,
            shards=shards,
            waits=len(waits),
        ),
        grid_spec=pltpu.PrefetchScalarGridSpec(
            num_scalar_prefetch=2,
            grid=(count,),
            in_specs=[
                pl.BlockSpec((rows, width), lambda p, *_: (0, 0)),
                pl.BlockSpec((width, 3 * PAIR), lambda p, *_: (0, p)),
                pl.BlockSpec((1, 1, 3 * PAIR), lambda p, *_: (first + p, 0, 0)),
            ]
            + specs
            + [pl.BlockSpec(memory_space=pl.ANY)] * len(waits),
            out_specs=[
                pl.BlockSpec((rows, PAIR), lambda p, *_: (0, p)),
                long_spec((seq, 2 * PAIR), lambda p, *_: (0, p), shards),
                pl.BlockSpec((rows, PAIR), lambda p, *_: (0, p)),
                pl.BlockSpec((row_blocks, 1, LISTED, PAIR), lambda p, *_: (0, p, 0, 0)),
                long_spec((1, seq, 2 * extra), lambda p, *_: (p, 0, 0), shards),
            ],
            scratch_shapes=scratch,
        ),
        out_shape=[
            jax.ShapeDtypeStruct((rows, count * PAIR), BF16),
            jax.ShapeDtypeStruct((seq, 2 * count * PAIR), BF16),
            jax.ShapeDtypeStruct((rows, count * PAIR), BF16),
            jax.ShapeDtypeStruct((row_blocks, count, LISTED, PAIR), BF16),
            jax.ShapeDtypeStruct((count, seq, 2 * extra), BF16),
        ],
        compiler_params=pltpu.CompilerParams(vmem_limit_bytes=58 * MIB),
        cost_estimate=taking(10 * count),
        name="attention_forward",
    )(starts, limits, x, weights, b_qkv, *pieces, *waits)


def attention_backward(
    starts, x, pieces, q, do, kv, probs, global_probs, waits, first, offset, count, cost, extra
):
    rows, seq, width, shards = q.shape[0], kv.shape[0], x.shape[1], len(pieces)
    parts = lax.axis_size("wt")
    row_blocks = (rows - extra) // BLOCK
    specs, scratch = piece_specs(rows - extra, width, shards)
    return pl.pallas_call(
        partial(
            backward_kernel,
            first=first,
            row_blocks=row_blocks,
            extra=extra,
            shards=shards,
            parts=parts,
            waits=len(waits),
        ),
        grid_spec=pltpu.PrefetchScalarGridSpec(
            num_scalar_prefetch=1,
            grid=(count,),
            in_specs=[
                pl.BlockSpec((rows, width), lambda p, *_: (0, 0)),
                pl.BlockSpec((rows, PAIR), lambda p, *_: (0, offset + p)),
                pl.BlockSpec((rows, PAIR), lambda p, *_: (0, first + p)),
                long_spec((seq, 2 * PAIR), lambda p, *_: (0, offset + p), shards),
                pl.BlockSpec((row_blocks, 1, LISTED, PAIR), lambda p, *_: (0, offset + p, 0, 0)),
                long_spec((1, seq, 2 * extra), lambda p, *_: (offset + p, 0, 0), shards),
            ]
            + specs
            + [pl.BlockSpec(memory_space=pl.ANY)] * len(waits),
            out_specs=[
                pl.BlockSpec((rows, PAIR), lambda p, *_: (0, p)),
                long_spec((seq, 2 * PAIR), lambda p, *_: (0, p), shards),
                pl.BlockSpec((width // 2, 3 * PAIR), lambda p, *_: (0, p)),
                pl.BlockSpec((width // 2, 3 * PAIR), lambda p, *_: (0, p)),
                pl.BlockSpec((1, 1, PAIR), lambda p, *_: (p, 0, 0)),
                pl.BlockSpec((1, 1, PAIR), lambda p, *_: (p, 0, 0)),
            ],
            scratch_shapes=[pltpu.VMEM((seq, 2 * PAIR), F32), *scratch],
        ),
        out_shape=[
            jax.ShapeDtypeStruct((rows, count * PAIR), BF16),
            jax.ShapeDtypeStruct((seq, 2 * count * PAIR), BF16),
            jax.ShapeDtypeStruct((width // 2, 3 * count * PAIR), BF16),
            jax.ShapeDtypeStruct((width // 2, 3 * count * PAIR), BF16),
            jax.ShapeDtypeStruct((count, 1, PAIR), F32),
            jax.ShapeDtypeStruct((count, 1, PAIR), F32),
        ],
        compiler_params=pltpu.CompilerParams(vmem_limit_bytes=60 * MIB),
        cost_estimate=taking(cost),
        name="attention_backward",
    )(starts, x, q, do, kv, probs, global_probs, *pieces, *waits)


def centered_root(value):
    centered = value - jnp.mean(value, axis=1, keepdims=True)
    root = lax.rsqrt(jnp.mean(centered * centered, axis=1, keepdims=True) + EPSILON)
    return centered * root, root


def norm_back(grad, normed, root):
    mean = jnp.mean(grad, axis=1, keepdims=True)
    return root * (grad - mean - normed * jnp.mean(grad * normed, axis=1, keepdims=True))


def expand_piece(ref, piece):
    half = ref.shape[3] // 2
    blocks = []
    for part in range(ref.shape[1]):
        blocks += [ref[piece, part, :, :half], ref[piece, part, :, half:]]
    return jnp.concatenate(blocks, axis=0)


def contract_piece(ref, piece):
    return jnp.concatenate([ref[piece, part] for part in range(ref.shape[1])], axis=0)


def layer_kernel(
    me,
    x_ref,
    att0_ref,
    att1_ref,
    cot_ref,
    keep_ref,
    wo_ref,
    we_ref,
    wc_ref,
    be_ref,
    vec_ref,
    out_ref,
    one_ref,
    do_ref,
    wok_ref,
    woa_ref,
    ck_ref,
    ca_ref,
    ek_ref,
    ea_ref,
    beg_ref,
    vecg_ref,
    norm_ref,
    root_ref,
    low_ref,
    slope_ref,
    hid_ref,
    acc_ref,
    two_ref,
):
    step = pl.program_id(0)
    core = me[0] % 2
    row = lambda i: vec_ref[i : i + 1, :]

    @pl.when(step == 0)
    def _():
        cut = att0_ref.shape[1]
        branch = dot(att0_ref[...], wo_ref[:cut]) + dot(att1_ref[...], wo_ref[cut:])
        normed, root = centered_root(x_ref[...].astype(F32) + branch + row(0))
        norm_ref[...] = normed
        root_ref[...] = root
        normed = normed * row(1) + row(2)
        low_ref[...] = normed.astype(BF16)
        acc_ref[...] = normed + row(3)

    @pl.when(step < 4)
    def _():
        for i, piece in enumerate((core, 1 - core)):
            u = dot(low_ref[...], expand_piece(we_ref, piece)) + be_ref[piece]
            square = u * u
            t = jnp.tanh(SLOPE * u * (1.0 + CUBIC * square))
            half = 0.5 * (1.0 + t)
            hidden = (u * half).astype(BF16)
            slope_ref[step, i] = half + (0.5 * SLOPE) * u * (1.0 - t * t) * (
                1.0 + (3.0 * CUBIC) * square
            )
            hid_ref[step, i] = hidden
            acc_ref[...] += dot(hidden, contract_piece(wc_ref, piece))

    @pl.when(step == 4)
    def _():
        normed, root = centered_root(acc_ref[...])
        out_ref[...] = (keep_ref[...] * (normed * row(4) + row(5))).astype(BF16)
        cot = cot_ref[...].astype(F32)
        vecg_ref[4:5, :] = jnp.sum(cot * normed, axis=0, keepdims=True)
        vecg_ref[5:6, :] = jnp.sum(cot, axis=0, keepdims=True)
        two = norm_back(cot * row(4), normed, root)
        acc_ref[...] = two
        two = two.astype(BF16)
        two_ref[...] = two
        vecg_ref[3:4, :] = jnp.sum(two.astype(F32), axis=0, keepdims=True)

    @pl.when(step >= 4)
    def _():
        at = step - 4
        for i, (piece, c_ref, e_ref) in enumerate(
            ((core, ck_ref, ek_ref), (1 - core, ca_ref, ea_ref))
        ):
            c_ref[0] = t_dot(hid_ref[at, i], two_ref[...]).astype(BF16)
            grad = (dot_t(two_ref[...], contract_piece(wc_ref, piece)) * slope_ref[at, i]).astype(BF16)
            e_ref[0] = t_dot(low_ref[...], grad).astype(BF16)
            beg_ref[piece] = jnp.sum(grad.astype(F32), axis=0, keepdims=True)
            acc_ref[...] += dot_t(grad, expand_piece(we_ref, piece))

    @pl.when(step == 7)
    def _():
        first = acc_ref[...]
        normed = norm_ref[...]
        vecg_ref[1:2, :] = jnp.sum(first * normed, axis=0, keepdims=True)
        vecg_ref[2:3, :] = jnp.sum(first, axis=0, keepdims=True)
        one = norm_back(first * row(1), normed, root_ref[...])
        one_ref[...] = one
        one = one.astype(BF16)
        vecg_ref[0:1, :] = jnp.sum(one.astype(F32), axis=0, keepdims=True)
        vecg_ref[6:8, :] = jnp.zeros((2, one.shape[1]), F32)
        grad = [t_dot(att_ref[...], one) for att_ref in (att0_ref, att1_ref)]
        near, away = by_core(jnp.concatenate(grad, axis=0), core, we_ref.shape[1])
        wok_ref[...], woa_ref[...] = near.astype(BF16), away.astype(BF16)
        do_ref[...] = dot_t(one, wo_ref[...]).astype(BF16)


def layer(c, x, attended, cot, keep, w_output, w_hidden, b_expand, vectors):
    rows, width = x.shape
    parts, piece = w_hidden.shape[1], b_expand.shape[2]
    each = piece // parts
    steps = PIECES // 2
    whole = lambda *shape: pl.BlockSpec(shape, lambda s, me: (0,) * len(shape))
    chip = lambda s, me: (s % steps) ^ ((me[0] % PIECES) // 2)
    sent = lambda *shape: pl.BlockSpec((1, *shape), lambda s, me: (jnp.maximum(s - steps, 0), 0, 0))
    return pl.pallas_call(
        layer_kernel,
        grid_spec=pltpu.PrefetchScalarGridSpec(
            num_scalar_prefetch=1,
            grid=(2 * steps,),
            in_specs=[
                whole(rows, width),
                *[whole(*a.shape) for a in attended],
                whole(rows, width),
                whole(rows, 1),
                whole(width, width),
                pl.BlockSpec((2, parts, each, width), lambda s, me: (chip(s, me), 0, 0, 0)),
                pl.BlockSpec((2, parts, each, width), lambda s, me: (chip(s, me), 0, 1, 0)),
                pl.BlockSpec((2, 1, piece), lambda s, me: (chip(s, me), 0, 0)),
                whole(8, width),
            ],
            out_specs=[
                whole(rows, width),
                whole(rows, width),
                whole(rows, width),
                whole(width // 2, width),
                whole(width // 2, width),
                sent(piece, width),
                sent(piece, width),
                sent(width, piece),
                sent(width, piece),
                pl.BlockSpec((2, 1, piece), lambda s, me: (chip(jnp.maximum(s - steps, 0), me), 0, 0)),
                whole(8, width),
            ],
            scratch_shapes=[
                pltpu.VMEM((rows, width), F32),
                pltpu.VMEM((rows, 1), F32),
                pltpu.VMEM((rows, width), BF16),
                pltpu.VMEM((steps, 2, rows, piece), F32),
                pltpu.VMEM((steps, 2, rows, piece), BF16),
                pltpu.VMEM((rows, width), F32),
                pltpu.VMEM((rows, width), BF16),
            ],
        ),
        out_shape=[
            jax.ShapeDtypeStruct((rows, width), BF16),
            jax.ShapeDtypeStruct((rows, width), F32),
            jax.ShapeDtypeStruct((rows, width), BF16),
            jax.ShapeDtypeStruct((width // 2, width), BF16),
            jax.ShapeDtypeStruct((width // 2, width), BF16),
            jax.ShapeDtypeStruct((steps, piece, width), BF16),
            jax.ShapeDtypeStruct((steps, piece, width), BF16),
            jax.ShapeDtypeStruct((steps, width, piece), BF16),
            jax.ShapeDtypeStruct((steps, width, piece), BF16),
            jax.ShapeDtypeStruct((PIECES, 1, piece), F32),
            jax.ShapeDtypeStruct((8, width), F32),
        ],
        compiler_params=pltpu.CompilerParams(vmem_limit_bytes=58 * MIB),
        cost_estimate=taking(35),
        name="layer",
    )(
        jnp.reshape(c, (1,)).astype(jnp.int32),
        x,
        *attended,
        cot,
        keep,
        w_output,
        w_hidden,
        w_hidden,
        b_expand,
        vectors,
    )


def pair_sum(grad_refs, weight_refs, columns, at):
    total = None
    for (group, offset, count), ref in zip(BACK, grad_refs):
        for pair in range(count):
            start = 3 * PAIR * (offset + pair) + at
            term = dot_t(
                ref[:, pair * columns : (pair + 1) * columns],
                weight_refs[group][:, start : start + columns],
            )
            total = term if total is None else total + term
    return total


def token_kernel(me, *refs, away, extra, count):
    sides = len(BACK)
    dkv_refs, w_refs = refs[:sides], refs[sides : sides + 2]
    c, step = me[0], pl.program_id(0)
    piece = 2 * step + (1 if away else 0)
    half = dkv_refs[0].shape[0] // 2
    if away:
        dq_refs, one_ref = refs[sides + 2 : 2 * sides + 2], refs[2 * sides + 2]
        above_ref, below_ref, share_ref = refs[-3:]

        @pl.when(step == 0)
        def _():
            share_ref[...] = one_ref[...] + pair_sum(dq_refs, w_refs, PAIR, 0)

        share = lambda: share_ref[2 * half : 2 * half + extra, :]
    else:
        share_ref, above_ref, below_ref = refs[sides + 2], *refs[-2:]
        share = lambda: share_ref[...]
    total = pair_sum(dkv_refs, w_refs, 2 * PAIR, PAIR).astype(BF16)
    above_ref[0], below_ref[0] = total[:half], total[half:]

    @pl.when((piece == c) & (c < count))
    def _():
        at = pl.ds(pl.multiple_of(c * extra, extra), extra)
        above_ref[0, at, :] = (above_ref[0, at, :].astype(F32) + share()).astype(BF16)


def token_share(c, dkvs, weights, more, away, waits, rows, extra, count):
    seq, width = dkvs[0].shape[0], weights[0].shape[0]
    chips = seq // rows // 2
    other = 1 if away else 0
    full = lambda a: pl.BlockSpec(a.shape, lambda j, me: (0,) * a.ndim)
    out_specs = [pl.BlockSpec((1, rows // 2, width), lambda j, me: (j, 0, 0))] * 2
    out_shape = [jax.ShapeDtypeStruct((chips, rows // 2, width), BF16)] * 2
    if away:
        out_specs.append(pl.BlockSpec((rows + extra, width), lambda j, me: (0, 0)))
        out_shape.append(jax.ShapeDtypeStruct((rows + extra, width), F32))
    return pl.pallas_call(
        partial(token_kernel, away=away, extra=extra, count=count),
        grid_spec=pltpu.PrefetchScalarGridSpec(
            num_scalar_prefetch=1,
            grid=(chips,),
            in_specs=[
                pl.BlockSpec((rows, a.shape[1]), lambda j, me: (2 * j + other, 0))
                for a in dkvs
            ]
            + [full(a) for a in (*weights, *more)]
            + [pl.BlockSpec(memory_space=pl.ANY)] * len(waits),
            out_specs=out_specs,
        ),
        out_shape=out_shape,
        compiler_params=pltpu.CompilerParams(vmem_limit_bytes=48 * MIB),
        cost_estimate=taking(3),
        name="token_share",
    )(jnp.reshape(c, (1,)).astype(jnp.int32), *dkvs, *weights, *more, *waits)


def by_pair(queries, keys, values):
    count = queries.shape[0]
    together = [a.reshape(count, PAIRS, PAIR) for a in (queries, keys, values)]
    together = jnp.concatenate(together, axis=2).reshape(count * PAIRS, 3 * PAIR)
    places = jnp.arange(3 * PAIR, dtype=jnp.int32)
    source = jnp.array((1, 0, 4, 2, 3, 5), jnp.int32)[places // HD] * HD + places % HD
    return ordered(together, source).astype(BF16).reshape(count, PAIRS * 3 * PAIR)


def column_places(pairs):
    start = jnp.arange(pairs, dtype=jnp.int32)[:, None, None] * (3 * PAIR)
    inner = jnp.arange(HD, dtype=jnp.int32)
    for spots in ((1, 0), (3, 4), (2, 5)):
        yield (start + jnp.array(spots, jnp.int32)[:, None] * HD + inner).reshape(-1)


def swapped(value, bit):
    shards = lax.axis_size("ctx")
    return lax.ppermute(value, "ctx", [(i, i ^ bit) for i in range(shards)])


def own_bit(bit):
    return (lax.axis_index("ctx") // bit) % 2


def added(keep, came):
    return (keep.astype(F32) + came.astype(F32)).astype(BF16)


def halved(value, axis, bit):
    mine = own_bit(bit)
    away = lax.dynamic_index_in_dim(value, 1 - mine, axis, keepdims=False)
    keep = lax.dynamic_index_in_dim(value, mine, axis, keepdims=False)
    return added(keep, swapped(away, bit))


def doubled(value, bit):
    other = swapped(value, bit)
    mine = own_bit(bit) == 0
    return jnp.stack([jnp.where(mine, value, other), jnp.where(mine, other, value)])


def plane_gather(value):
    value = value[None]
    for bit in (1, 2, 4):
        value = doubled(value, bit)
        value = value.reshape(-1, *value.shape[2:])
    return value


def line_step(value, bit):
    parts = lax.axis_size("wt")
    other = lax.ppermute(value, "wt", [(i, i ^ bit) for i in range(parts)])
    mine = lax.axis_index("wt") // bit % 2 == 0
    return jnp.concatenate([jnp.where(mine, value, other), jnp.where(mine, other, value)])


def line_gather(value, bit=1):
    while bit < lax.axis_size("wt"):
        value = line_step(value, bit)
        bit *= 2
    return value


def token_gather(own):
    shards, half = lax.axis_size("ctx"), own.shape[0] // 2
    along_x, along_y = swapped(own, 2), swapped(own, 4)
    far = jnp.concatenate([swapped(along_y[:half], 2), swapped(along_x[half:], 4)], axis=0)
    pieces = []
    for piece in (own, along_x, along_y, far):
        pieces += [piece, swapped(piece, 1)]
    bit = PIECES
    while bit < shards:
        pieces += [swapped(piece, bit) for piece in pieces]
        bit *= 2
    return pieces


def far_sum(value, shards):
    if shards == PIECES:
        return value
    return lax.psum(value, "ctx", axis_index_groups=across_groups(shards))


def same_core(shards, block):
    return [list(range(s + k, s + block, 2)) for s in range(0, shards, block) for k in range(2)]


def rows_start(near, came):
    parts, columns = lax.axis_size("wt"), near.shape[1]
    near, came = (a.reshape(parts, PIECES // 2, -1, columns) for a in (near, came))
    return jnp.transpose(added(near, came), (1, 0, 2, 3)).reshape(parts * PIECES // 2, -1, columns)


def rows_sum(sums):
    shards, parts = lax.axis_size("ctx"), lax.axis_size("wt")
    sums = far_sum(sums, shards)
    groups = [[i * parts + w for i in g for w in range(parts)] for g in same_core(shards, PIECES)]
    sums = lax.all_to_all(
        sums, ("ctx", "wt"), split_axis=0, concat_axis=0, axis_index_groups=groups, tiled=True
    )
    return jnp.sum(sums.astype(F32), axis=0).astype(BF16)


def ordered(value, source):
    rows = jnp.arange(value.shape[1], dtype=jnp.int32)
    return dot(value, (rows[:, None] == source[None, :]).astype(BF16))


def vector_kernel(*refs, parts):
    sides = len(BACK)
    joined = lambda some: jnp.concatenate([r[i] for r in some for i in range(r.shape[0])], axis=1)
    grads_ref, expand_ref, _, out_ref = refs[2 * sides :]
    rows = [joined(refs[:sides]), joined(refs[sides : 2 * sides])]
    rows += [grads_ref[i : i + 1, :] for i in (0, 3, 1, 2, 4, 5)]
    width = out_ref.shape[1]
    share, run = width // parts, expand_ref.shape[2] // parts
    out = []
    for part in range(parts):
        cuts = [row[:, part * share : (part + 1) * share] for row in rows]
        out += [jnp.concatenate(cuts[i : i + parts], axis=1) for i in range(0, len(cuts), parts)]
        cuts = [expand_ref[p, :, part * run : (part + 1) * run] for p in range(PIECES)]
        out.append(jnp.concatenate(cuts, axis=1))
        out.append(jnp.zeros((PIECES - len(rows) // parts - 1, width), F32))
    out_ref[...] = jnp.concatenate(out, axis=0).astype(BF16)


def vector_rows(q_sums, v_sums, grads, expand_grads, wait, parts):
    return pl.pallas_call(
        partial(vector_kernel, parts=parts),
        in_specs=[pl.BlockSpec(memory_space=pltpu.VMEM)] * (2 * len(BACK) + 2)
        + [pl.BlockSpec(memory_space=pl.ANY)],
        out_shape=jax.ShapeDtypeStruct((parts * PIECES, grads.shape[1]), BF16),
        cost_estimate=taking(1),
        name="vector_rows",
    )(*q_sums, *v_sums, grads, expand_grads, wait)


def expand_kernel(in_ref, out_ref):
    pieces, half, run = in_ref.shape[0], in_ref.shape[1], in_ref.shape[2] // 2
    parts = out_ref.shape[1] // in_ref.shape[2]
    count = run // parts
    for lower in range(2):
        for part in range(parts):
            at = lower * run + part * count
            runs = [in_ref[p, :, at : at + count].astype(F32) for p in range(pieces)]
            out_ref[
                lower * half : (lower + 1) * half, part * 2 * run : (part + 1) * 2 * run
            ] = jnp.concatenate(runs, axis=1)


def expand_columns(gathered, each_piece, parts):
    width = gathered.shape[2]
    return pl.pallas_call(
        expand_kernel,
        grid=(1,),
        in_specs=[pl.BlockSpec((PIECES, each_piece, width), lambda i: (0, 1, 0))],
        out_specs=pl.BlockSpec((2 * each_piece, parts * width), lambda i: (0, 0)),
        out_shape=jax.ShapeDtypeStruct((2 * each_piece, parts * width), F32),
        compiler_params=pltpu.CompilerParams(vmem_limit_bytes=24 * MIB),
        cost_estimate=taking(2),
        name="expand_columns",
    )(gathered)


def body(
    tokens,
    cotangent,
    lengths,
    rand_blocks,
    query_weight,
    key_weight,
    value_weight,
    output_weight,
    expand_weight,
    contract_weight,
    query_bias,
    value_bias,
    output_bias,
    expand_bias,
    contract_bias,
    attn_gain,
    attn_shift,
    ffn_gain,
    ffn_shift,
):
    shards = lax.axis_size("ctx")
    parts = lax.axis_size("wt")
    c = lax.axis_index("ctx")
    rows, width = tokens.shape[1], tokens.shape[2]
    row_blocks = rows // BLOCK
    seq = shards * rows
    global_count = GLOB * BLOCK
    extra = 16 * (-(-global_count // (16 * shards)))
    hidden_width = expand_weight.shape[1]
    part = expand_weight.shape[0]
    piece = hidden_width // PIECES
    length = lengths[0]
    inputs = tokens[0]

    pieces = token_gather(inputs)
    small = jnp.concatenate(
        [
            query_bias,
            value_bias,
            output_bias,
            contract_bias,
            attn_gain,
            attn_shift,
            ffn_gain,
            ffn_shift,
            expand_bias,
        ]
    )
    half = part // 2
    bundles = [
        lax.dynamic_slice_in_dim(w, own_bit(1) * half, half, 0)
        for w in (query_weight, key_weight, value_weight)
    ]
    bundles = by_pair(*bundles)
    ahead = AHEAD * 3 * PAIR
    small_rows = 8 * (-(-small.shape[0] // (8 * ahead)))
    padded = jnp.pad(small, (0, small_rows * ahead - small.shape[0])).reshape(small_rows, ahead)
    early_lead = line_step(jnp.concatenate([bundles[:, :ahead], padded], axis=0)[None], 1)
    leading = line_gather(early_lead, 2)
    vectors = leading[:, half:].reshape(parts, -1)[:, : small.shape[0]]
    leading = leading[:, :half]

    def joined(bundle):
        return jnp.transpose(doubled(bundle, 1), (1, 0, 2, 3)).reshape(width, -1)

    weights = [joined(leading)]
    behind = bundles[:, ahead:]
    behind = jnp.concatenate([behind[:, :width], behind[:, width:]], axis=0)
    each = width // parts
    b_query, b_value, b_output, b_contract, g_attn, s_attn, g_ffn, s_ffn = (
        vectors[:, i * each : (i + 1) * each].reshape(-1).astype(F32) for i in range(8)
    )
    b_expand = vectors[:, 8 * each :].reshape(parts, PIECES, -1)
    b_expand = jnp.transpose(b_expand, (1, 0, 2)).reshape(PIECES, 1, piece).astype(F32)

    p = c % PIECES
    each_piece = piece // parts
    e_piece = lax.dynamic_index_in_dim(
        expand_weight.reshape(part, parts, PIECES, -1), p, 2, keepdims=False
    ).reshape(part, piece)
    e_piece = jnp.concatenate([e_piece[:each_piece], e_piece[each_piece:]], axis=1)
    c_piece = lax.dynamic_slice_in_dim(contract_weight, p * each_piece, each_piece, 0)
    o_rows = part // PIECES
    o_piece = lax.dynamic_slice_in_dim(output_weight, p * o_rows, o_rows, 0)
    w_hidden = jnp.concatenate([e_piece, c_piece, o_piece, behind], axis=0)
    w_hidden = after(w_hidden, pieces[1])
    w_hidden = lax.all_gather(w_hidden, "wt")
    mixed = 2 * each_piece + o_rows
    following = w_hidden[:, mixed:].reshape(parts, 2, half, width)
    following = jnp.concatenate([following[:, 0], following[:, 1]], axis=2)

    start = jnp.minimum(c * extra, global_count - extra)
    more = lax.dynamic_slice_in_dim(pieces[0], start, extra, 0)
    for i in range(1, shards):
        other = lax.dynamic_slice_in_dim(pieces[i], start, extra, 0)
        more = jnp.where(c == i, other, more)
    x = jnp.concatenate([inputs, more], axis=0)
    index = jnp.arange(rows + extra, dtype=jnp.int32)
    position = jnp.where(index < rows, c * rows + index, c * extra + index - rows)
    is_global = position < global_count
    usable = ((position < length) & (is_global == (index >= rows)))[:, None]
    own = c * row_blocks + jnp.arange(row_blocks, dtype=jnp.int32)
    beside = own[:, None, None] + jnp.arange(-1, 2, dtype=jnp.int32)
    listed = jnp.concatenate(
        [jnp.broadcast_to(beside, (row_blocks, H, 3)), rand_blocks[0]], axis=2
    )
    blocks = seq // BLOCK
    inside = (listed >= 0) & (listed < blocks)
    listed = jnp.clip(listed, 0, blocks - 1)
    limits = jnp.where(inside, length - listed * BLOCK, 0).reshape(-1)
    order = jnp.arange(shards, dtype=jnp.int32) ^ c
    limits = jnp.concatenate([limits, length - order * rows])
    starts = (listed // row_blocks ^ c) * rows + listed % row_blocks * BLOCK
    starts = jnp.concatenate([starts.reshape(-1), jnp.stack([c * rows, c % 2])])

    given = jnp.where(c == 0, cotangent[0, :global_count], jnp.zeros((), BF16))
    given = jnp.pad(given, ((0, shards * extra - global_count), (0, 0)))
    given = given.reshape(shards, extra, width)
    given = lax.all_to_all(given, "ctx", split_axis=0, concat_axis=0, tiled=True)
    cot = jnp.concatenate([cotangent[0], given[0]], axis=0)
    cot = jnp.where(usable, cot, jnp.zeros((), BF16))

    b_qkv = by_pair(*(b.astype(BF16)[None] for b in (b_query, jnp.zeros_like(b_value), b_value)))
    b_qkv = b_qkv.astype(F32).reshape(PAIRS, 1, 3 * PAIR)
    zero = jnp.zeros_like(b_output)
    vectors = jnp.stack([b_output, g_attn, s_attn, b_contract, g_ffn, s_ffn, zero, zero])
    keep = usable.astype(F32)
    w_hidden = after(
        w_hidden[:, :mixed], *pieces, weights[0], cot, starts, limits, b_qkv, vectors, b_expand, keep, x
    )
    w_hidden = lax.all_gather(w_hidden, "ctx", axis_index_groups=groups_of(shards))
    w_output = jnp.transpose(w_hidden[:, :, 2 * each_piece :], (1, 0, 2, 3)).reshape(width, width)
    forward = partial(attention_forward, starts, limits, x, pieces)
    kept = [forward(weights[0], b_qkv, (cot,), *GROUPS[0], extra)]
    weights.append(joined(following))
    kept.append(forward(weights[1], b_qkv, (), *GROUPS[1], extra))

    (
        layer_out,
        grad_one,
        grad_attended,
        o_keep,
        o_away,
        c_keep,
        c_away,
        e_keep,
        e_away,
        expand_bgrad,
        vector_grads,
    ) = layer(
        c,
        x,
        [k[2] for k in kept],
        cot,
        keep,
        w_output,
        w_hidden,
        b_expand,
        vectors,
    )

    def attention_back(side, *waits):
        group, offset, count = BACK[side]
        q, kv, _, probs, global_probs = kept[group]
        first = GROUPS[group][0] + offset
        return attention_backward(
            starts,
            x,
            pieces,
            q,
            grad_attended,
            kv,
            probs,
            global_probs,
            waits,
            first,
            offset,
            count,
            BACK_COST[side],
            extra,
        )

    c_came, e_came = swapped(c_away, 1), swapped(e_away, 1)
    early = [rows_start(o_keep, swapped(o_away, 1))]
    backs = [attention_back(0)]
    steps = PIECES // 2
    c_keep, c_came = (a.reshape(2, 2, piece, width) for a in (c_keep, c_came))
    e_keep, e_came = (a.reshape(2, 2, width, piece) for a in (e_keep, e_came))
    c_away = added(c_keep[:, 1], c_came[:, 1])
    e_away = added(e_keep[1], e_came[1])
    c_came_on, e_came_on = swapped(c_away, 2), swapped(e_away, 4)
    c_keep = added(c_keep[:, 0], c_came[:, 0])
    e_keep = added(e_keep[0], e_came[0])

    early.append(rows_start(backs[0][2], swapped(backs[0][3], 1)))
    early = jnp.concatenate(early, axis=1)
    backs.append(attention_back(1, c_away, e_away, early))
    early = rows_sum(early)
    c_away, e_away = added(c_keep[1], c_came_on[1]), added(e_keep[1], e_came_on[1])
    c_last, e_last = swapped(c_away, 4), swapped(e_away, 2)
    c_keep, e_keep = added(c_keep[0], c_came_on[0]), added(e_keep[0], e_came_on[0])

    middle = rows_start(backs[1][2], swapped(backs[1][3], 1))
    backs.append(attention_back(2, c_away, e_away, early, middle))
    middle = rows_sum(middle)
    c_mine = far_sum(added(c_keep, c_last), shards).reshape(parts, -1, width)
    e_mine = far_sum(added(e_keep, e_last), shards).reshape(parts, 2, -1, piece)
    e_mine = jnp.concatenate([e_mine[:, 0], e_mine[:, 1]], axis=2)
    hidden_sums = jnp.concatenate([c_mine, e_mine], axis=1)
    both = lax.all_to_all(hidden_sums, "wt", split_axis=0, concat_axis=0, tiled=True)
    backs.append(attention_back(3, hidden_sums, middle))

    share = partial(token_share, c, [b[1] for b in backs], weights)
    count = global_count // extra
    above_away, below_away, own = share(
        [b[0] for b in backs] + [grad_one], True, (both,), rows, extra, count
    )
    both = jnp.sum(both.astype(F32), axis=0).astype(BF16)
    both = jnp.concatenate([both, early, middle, layer_out[rows:]], axis=0)
    above, below = share([own[rows:]], False, (above_away, both), rows, extra, count)

    def by_chip(keep, came):
        chips = shards // 2
        if chips > 4:
            keep = added(keep, came)
            while chips > 4:
                keep = added(keep[: chips // 2], swapped(keep[chips // 2 :], chips))
                chips //= 2
            came = jnp.zeros_like(keep)
        return [a.reshape(2, 2, rows // 2, width) for a in (keep, came)]

    above = by_chip(above, swapped(above_away, 1))
    below = by_chip(below, swapped(below_away, 1))
    above_sent = added(above[0][:, 1], above[1][:, 1])
    below_sent = added(below[0][1], below[1][1])
    above_came, below_came = swapped(above_sent, 2), swapped(below_sent, 4)
    above = added(above[0][:, 0], above[1][:, 0])
    below = added(below[0][0], below[1][0])

    hidden_rows = 2 * each_piece
    gathered = lax.all_gather(both, "ctx", axis_index_groups=groups_of(shards))

    contract_wgrad = gathered[:, :each_piece].reshape(-1, width).astype(F32)
    expand_wgrad = expand_columns(gathered, each_piece, parts)
    finished = gathered[:, -extra:].reshape(-1, width)
    on_first = (c == 0) & (index[:rows] < global_count)
    finished = jnp.pad(finished[:global_count], ((0, rows - global_count), (0, 0)))
    layer_out = jnp.where(on_first[:, None], finished, layer_out[:rows])

    above_came = after(above_came, contract_wgrad, expand_wgrad, layer_out)
    below_came = after(below_came, contract_wgrad, expand_wgrad, layer_out)

    small = vector_rows([b[4] for b in backs], [b[5] for b in backs], vector_grads, expand_bgrad, above_sent, parts)
    small = small.reshape(parts, 2, -1, width)
    near = jnp.concatenate([backs[2][2], backs[3][2]], axis=1).reshape(parts, PIECES // 2, -1, width)
    near = jnp.concatenate(
        [near, lax.dynamic_index_in_dim(small, own_bit(1), 1, keepdims=False)[:, :, None]], axis=2
    )
    far = jnp.concatenate([backs[2][3], backs[3][3]], axis=1).reshape(parts, PIECES // 2, -1, width)
    far = jnp.concatenate(
        [far, lax.dynamic_index_in_dim(small, 1 - own_bit(1), 1, keepdims=False)[:, :, None]], axis=2
    )
    late = rows_start(near.reshape(-1, width), swapped(far, 1))
    late = rows_sum(late)

    above_sent = added(above[1], above_came[1])
    below_sent = added(below[1], below_came[1])
    above_last, below_last = swapped(above_sent, 4), swapped(below_sent, 2)
    above = above[0].astype(F32) + above_came[0].astype(F32) + above_last.astype(F32)
    below = below[0].astype(F32) + below_came[0].astype(F32) + below_last.astype(F32)
    input_grad = own[:rows] + jnp.concatenate([above, below], axis=0)

    late = plane_gather(after(late, above_sent, below_sent))
    kinds = [gathered[:, hidden_rows:-extra].reshape(PIECES, 3, -1, width)]
    kinds.append(late[:, None, :-1])
    mine = jnp.concatenate(kinds, axis=1).reshape(PIECES // 2, 2, 4, -1, width)
    mine = jnp.transpose(mine, (2, 1, 0, 3, 4)).reshape(4, part, width)
    small = jnp.transpose(late[:, -1].reshape(PIECES // 2, 2, width), (1, 0, 2)).reshape(-1, width)
    small = small.astype(F32)
    small_grads = [small[i // parts, i % parts * each :][:each] for i in range(8)]
    expand_bias_grad = small[2]
    output_wgrad = mine[0].astype(F32)
    query_wgrad, key_wgrad, value_wgrad = (
        jnp.concatenate([ordered(g, places) for g in (mine[1], mine[2], mine[3])], axis=1)
        for places in column_places(AHEAD)
    )

    return (
        layer_out[None],
        input_grad[None],
        query_wgrad,
        key_wgrad,
        value_wgrad,
        output_wgrad,
        expand_wgrad,
        contract_wgrad,
        small_grads[0],
        small_grads[1],
        small_grads[2],
        expand_bias_grad,
        small_grads[3],
        small_grads[4],
        small_grads[5],
        small_grads[6],
        small_grads[7],
    )


def solution(mesh):
    tokens, weight, vector = P("wt", "ctx", None), P("wt", None), P("wt")
    return jax.shard_map(
        body,
        mesh=mesh,
        in_specs=(tokens, tokens, vector, P("wt", "ctx", None, None)) + (weight,) * 6 + (vector,) * 9,
        out_specs=(tokens, tokens) + (weight,) * 6 + (vector,) * 9,
        check_vma=False,
    )
```

```python
from functools import partial, reduce

import jax
import jax.numpy as jnp
from jax import lax
from jax.experimental import pallas as pl
from jax.experimental.pallas import tpu as pltpu
from jax.sharding import PartitionSpec as P

H = 12
HD = 64
BLOCK = 64
GLOB = 2
RAND = 3
PAIR = 2 * HD
PAIRS = H // 2
AHEAD = 2
GROUPS = ((0, AHEAD), (AHEAD, PAIRS - AHEAD))
BACK = ((0, 0, 2), (1, 0, 2), (1, 2, 1), (1, 3, 1))
BACK_COST = (8, 8, 8, 20)
MOVING = 3 + RAND
TOGETHER = 8
LISTED = (GLOB + MOVING) * BLOCK
PIECES = 8
NEGATIVE = -1e30
EPSILON = 1e-12
FACTOR = HD ** (-0.5)
SLOPE = (2.0 / jnp.pi) ** 0.5
CUBIC = 0.044715
F32 = jnp.float32
BF16 = jnp.bfloat16
MIB = 2**20


def taking(microseconds):
    return pl.CostEstimate(
        flops=int(microseconds * 10**9), bytes_accessed=10**6, transcendentals=0
    )


def groups_of(shards):
    return [list(range(s, s + PIECES)) for s in range(0, shards, PIECES)]


def across_groups(shards):
    return [list(range(s, shards, PIECES)) for s in range(PIECES)]


def dot(a, b):
    return jnp.dot(a, b, preferred_element_type=F32)


def dot_t(a, b):
    return lax.dot_general(a, b, (((1,), (1,)), ((), ())), preferred_element_type=F32)


def t_dot(a, b):
    return lax.dot_general(a, b, (((0,), (0,)), ((), ())), preferred_element_type=F32)


def after(value, *earlier):
    return pl.pallas_call(
        lambda *refs: None,
        in_specs=[pl.BlockSpec(memory_space=pl.ANY)] * (1 + len(earlier)),
        out_specs=pl.BlockSpec(memory_space=pl.ANY),
        out_shape=jax.ShapeDtypeStruct(value.shape, value.dtype),
        input_output_aliases={0: 0},
        name="after",
    )(value, *earlier)


def by_head(both, low, inner):
    zero = jnp.zeros_like(both)
    first, second = jnp.where(low, both, zero), jnp.where(low, zero, both)
    if inner:
        first, second = second, first
    return jnp.concatenate(
        [jnp.concatenate([first, zero], axis=1), jnp.concatenate([zero, second], axis=1)], axis=0
    )


def listed_keys(starts, spot, top, kv_ref):
    rows = [
        [pl.multiple_of(starts[spot + head * MOVING + i], BLOCK) for i in range(MOVING)]
        for head in range(2)
    ]
    parts = [kv_ref[pl.ds(top, GLOB * BLOCK), :]]
    parts += [kv_ref[pl.ds(at, BLOCK), :] for at in rows[0][:3]]
    parts += [
        jnp.concatenate(
            [kv_ref[pl.ds(first, BLOCK), :PAIR], kv_ref[pl.ds(second, BLOCK), PAIR:]], axis=1
        )
        for first, second in zip(rows[0][3:], rows[1][3:])
    ]
    return jnp.concatenate(parts, axis=0), rows


def loader(refs, streamed):
    if not streamed:
        return lambda i: refs[i][...]
    buffer, semaphore = streamed

    def load(i):
        copy = pltpu.make_async_copy(refs[i], buffer, semaphore)
        copy.start()
        copy.wait()
        return buffer[...]

    return load


def softmax(scores):
    raised = jnp.exp(scores - jnp.max(scores, axis=0, keepdims=True))
    return (raised * (1.0 / jnp.sum(raised, axis=0, keepdims=True))).astype(BF16)


def by_core(grad, core, parts):
    half = grad.shape[0] // parts // 2
    halves = [
        jnp.concatenate([grad[at : at + half] for at in range(i * half, grad.shape[0], 2 * half)])
        for i in range(2)
    ]
    first = core == 0
    return jnp.where(first, halves[0], halves[1]), jnp.where(first, halves[1], halves[0])


def forward_kernel(
    starts, limits, x_ref, w_ref, b_ref, *rest, first, row_blocks, extra, shards, waits
):
    seen_refs = rest[:shards]
    q_ref, kv_ref, out_ref, p_ref, pg_ref = rest[shards + waits :][:5]
    tokens = loader(seen_refs, rest[shards + waits + 5 :])
    top = pl.multiple_of(starts[row_blocks * H * MOVING], BLOCK)
    pair = first + pl.program_id(0)
    rows = row_blocks * BLOCK
    low = lax.broadcasted_iota(jnp.int32, (1, PAIR), 1) < HD
    within = lax.broadcasted_iota(jnp.int32, (BLOCK, PAIR), 0)

    queries = dot(x_ref[...], w_ref[:, :PAIR]) + b_ref[0, :, :PAIR]
    q_ref[...] = (queries.astype(BF16).astype(F32) * FACTOR).astype(BF16)

    for i in range(shards):
        kv = dot(tokens(i), w_ref[:, PAIR:]) + b_ref[0, :, PAIR:]
        kv_ref[i * rows : (i + 1) * rows, :] = kv.astype(BF16)

    def some_blocks(group, carry):
        blocks = [group * TOGETHER + i for i in range(TOGETHER)]
        ats = [pl.ds(pl.multiple_of(block * BLOCK, BLOCK), BLOCK) for block in blocks]
        spots = [(block * H + 2 * pair) * MOVING for block in blocks]
        kvs = [listed_keys(starts, spot, top, kv_ref)[0] for spot in spots]
        scores = [dot_t(kv, by_head(q_ref[at, :], low, True)) for kv, at in zip(kvs, ats)]
        probs = []
        for some, spot in zip(scores, spots):
            masked = [some[: GLOB * BLOCK]]
            for i in range(MOVING):
                limit = jnp.where(low, limits[spot + i], limits[spot + MOVING + i])
                here = some[(GLOB + i) * BLOCK : (GLOB + i + 1) * BLOCK]
                masked.append(jnp.where(within < limit, here, NEGATIVE))
            probs.append(softmax(jnp.concatenate(masked, axis=0)))
        outs = [t_dot(some, kv) for some, kv in zip(probs, kvs)]
        for block, at, some, out in zip(blocks, ats, probs, outs):
            p_ref[block, 0] = some
            out_ref[at, :] = jnp.where(low, out[:BLOCK, :PAIR], out[BLOCK:, PAIR:]).astype(BF16)
        return carry

    lax.fori_loop(0, row_blocks // TOGETHER, some_blocks, 0)

    wide = by_head(q_ref[rows : rows + extra, :], low, True)
    within = lax.broadcasted_iota(jnp.int32, (rows, 2 * extra), 0)
    scores = []
    for i in range(shards):
        limit = limits[row_blocks * H * MOVING + i]
        here = dot_t(kv_ref[i * rows : (i + 1) * rows, :], wide)
        scores.append(jnp.where(within < limit, here, NEGATIVE))
    summit = jnp.max(reduce(jnp.maximum, scores), axis=0, keepdims=True)
    raised = [jnp.exp(here - summit) for here in scores]
    share = 1.0 / jnp.sum(reduce(jnp.add, raised), axis=0, keepdims=True)
    out = None
    for i in range(shards):
        here = slice(i * rows, (i + 1) * rows)
        probs = (raised[i] * share).astype(BF16)
        pg_ref[0, here, :] = probs
        term = t_dot(probs, kv_ref[here, :])
        out = term if out is None else out + term
    out_ref[rows : rows + extra, :] = jnp.where(
        low, out[:extra, :PAIR], out[extra:, PAIR:]
    ).astype(BF16)


def backward_kernel(
    starts,
    x_ref,
    q_ref,
    do_ref,
    kv_ref,
    p_ref,
    pg_ref,
    *rest,
    first,
    row_blocks,
    extra,
    shards,
    parts,
    waits,
):
    seen_refs = rest[:shards]
    dq_ref, dkv_ref, near_ref, away_ref, qsum_ref, vsum_ref, acc = rest[shards + waits :][:7]
    tokens = loader(seen_refs, rest[shards + waits + 7 :])
    core = starts[row_blocks * H * MOVING + 1]
    top = pl.multiple_of(starts[row_blocks * H * MOVING], BLOCK)
    pair = first + pl.program_id(0)
    rows = row_blocks * BLOCK
    low = lax.broadcasted_iota(jnp.int32, (1, PAIR), 1) < HD

    last = slice(rows, rows + extra)
    wide_do = by_head(do_ref[last, :], low, False)
    cuts = [slice(i * rows, (i + 1) * rows) for i in range(shards)]
    dps = [dot_t(kv_ref[here, :], wide_do) for here in cuts]
    terms = [pg_ref[0, here, :].astype(F32) * dp for here, dp in zip(cuts, dps)]
    delta = jnp.sum(reduce(jnp.add, terms), axis=0, keepdims=True)
    rows_in = jnp.concatenate([wide_do, by_head(q_ref[last, :], low, True)], axis=0)
    dq = None
    for here, dp in zip(cuts, dps):
        probs = pg_ref[0, here, :]
        ds = (probs.astype(F32) * (dp - delta)).astype(BF16)
        term = t_dot(ds, kv_ref[here, :])
        dq = term if dq is None else dq + term
        acc[here, :] = dot(jnp.concatenate([probs, ds], axis=1), rows_in)
    dq = jnp.where(low, dq[extra:, PAIR:], dq[:extra, :PAIR]) * FACTOR
    dq_ref[last, :] = dq.astype(BF16)

    def some_blocks(group, carry):
        blocks = [group * TOGETHER + i for i in range(TOGETHER)]
        ats = [pl.ds(pl.multiple_of(block * BLOCK, BLOCK), BLOCK) for block in blocks]
        listed = [
            listed_keys(starts, (block * H + 2 * pair) * MOVING, top, kv_ref) for block in blocks
        ]
        kvs = [kv for kv, _ in listed]
        dos = [by_head(do_ref[at, :], low, False) for at in ats]
        dps = [dot_t(kv, do) for kv, do in zip(kvs, dos)]
        probs = [p_ref[block, 0] for block in blocks]
        dss = []
        for some, dp in zip(probs, dps):
            wide = some.astype(F32)
            dss.append((wide * (dp - jnp.sum(wide * dp, axis=0, keepdims=True))).astype(BF16))
        dqs = [t_dot(ds, kv) for ds, kv in zip(dss, kvs)]
        dkvs = [
            dot(
                jnp.concatenate([some, ds], axis=1),
                jnp.concatenate([do, by_head(q_ref[at, :], low, True)], axis=0),
            )
            for some, ds, do, at in zip(probs, dss, dos, ats)
        ]
        for at, dq in zip(ats, dqs):
            dq = jnp.where(low, dq[BLOCK:, PAIR:], dq[:BLOCK, :PAIR]) * FACTOR
            dq_ref[at, :] = dq.astype(BF16)
        acc[pl.ds(top, GLOB * BLOCK), :] += reduce(jnp.add, [d[: GLOB * BLOCK] for d in dkvs])
        for dkv, (_, places) in zip(dkvs, listed):
            for i in range(MOVING):
                here = dkv[(GLOB + i) * BLOCK : (GLOB + i + 1) * BLOCK]
                if i < 3:
                    acc[pl.ds(places[0][i], BLOCK), :] += here
                else:
                    acc[pl.ds(places[0][i], BLOCK), :PAIR] += here[:, :PAIR]
                    acc[pl.ds(places[1][i], BLOCK), PAIR:] += here[:, PAIR:]
        return carry

    lax.fori_loop(0, row_blocks // TOGETHER, some_blocks, 0)
    dkv_ref[...] = acc[...].astype(BF16)
    total = jnp.sum(acc[...], axis=0, keepdims=True)
    vsum_ref[0] = jnp.where(low, total[:, :PAIR], total[:, PAIR:])
    total = jnp.sum(dq_ref[...].astype(F32), axis=0, keepdims=True)
    qsum_ref[0] = jnp.concatenate([total[:, HD:], total[:, :HD]], axis=1)
    near, away = by_core(t_dot(x_ref[...], dq_ref[...]), core, parts)
    near_ref[:, :PAIR], away_ref[:, :PAIR] = near.astype(BF16), away.astype(BF16)
    total = None
    for i in range(shards):
        term = t_dot(tokens(i), dkv_ref[i * rows : (i + 1) * rows, :])
        total = term if total is None else total + term
    near, away = by_core(total, core, parts)
    near_ref[:, PAIR:], away_ref[:, PAIR:] = near.astype(BF16), away.astype(BF16)


def piece_specs(rows, width, shards):
    if shards > PIECES:
        scratch = [pltpu.VMEM((rows, width), BF16), pltpu.SemaphoreType.DMA]
        return [pl.BlockSpec(memory_space=pl.ANY)] * shards, scratch
    spec = pl.BlockSpec((rows, width), lambda p, *_: (0, 0), pipeline_mode=pl.Buffered(1))
    return [spec] * shards, []


def long_spec(shape, place, shards):
    if shards > PIECES:
        return pl.BlockSpec(shape, place, pipeline_mode=pl.Buffered(1))
    return pl.BlockSpec(shape, place)


def attention_forward(starts, limits, x, pieces, weights, b_qkv, waits, first, count, extra):
    rows, width, shards = x.shape[0], x.shape[1], len(pieces)
    seq = shards * (rows - extra)
    row_blocks = (rows - extra) // BLOCK
    specs, scratch = piece_specs(rows - extra, width, shards)
    return pl.pallas_call(
        partial(
            forward_kernel,
            first=first,
            row_blocks=row_blocks,
            extra=extra,
            shards=shards,
            waits=len(waits),
        ),
        grid_spec=pltpu.PrefetchScalarGridSpec(
            num_scalar_prefetch=2,
            grid=(count,),
            in_specs=[
                pl.BlockSpec((rows, width), lambda p, *_: (0, 0)),
                pl.BlockSpec((width, 3 * PAIR), lambda p, *_: (0, p)),
                pl.BlockSpec((1, 1, 3 * PAIR), lambda p, *_: (first + p, 0, 0)),
            ]
            + specs
            + [pl.BlockSpec(memory_space=pl.ANY)] * len(waits),
            out_specs=[
                pl.BlockSpec((rows, PAIR), lambda p, *_: (0, p)),
                long_spec((seq, 2 * PAIR), lambda p, *_: (0, p), shards),
                pl.BlockSpec((rows, PAIR), lambda p, *_: (0, p)),
                pl.BlockSpec((row_blocks, 1, LISTED, PAIR), lambda p, *_: (0, p, 0, 0)),
                long_spec((1, seq, 2 * extra), lambda p, *_: (p, 0, 0), shards),
            ],
            scratch_shapes=scratch,
        ),
        out_shape=[
            jax.ShapeDtypeStruct((rows, count * PAIR), BF16),
            jax.ShapeDtypeStruct((seq, 2 * count * PAIR), BF16),
            jax.ShapeDtypeStruct((rows, count * PAIR), BF16),
            jax.ShapeDtypeStruct((row_blocks, count, LISTED, PAIR), BF16),
            jax.ShapeDtypeStruct((count, seq, 2 * extra), BF16),
        ],
        compiler_params=pltpu.CompilerParams(vmem_limit_bytes=58 * MIB),
        cost_estimate=taking(10 * count),
        name="attention_forward",
    )(starts, limits, x, weights, b_qkv, *pieces, *waits)


def attention_backward(
    starts, x, pieces, q, do, kv, probs, global_probs, waits, first, offset, count, cost, extra
):
    rows, seq, width, shards = q.shape[0], kv.shape[0], x.shape[1], len(pieces)
    parts = lax.axis_size("wt")
    row_blocks = (rows - extra) // BLOCK
    specs, scratch = piece_specs(rows - extra, width, shards)
    return pl.pallas_call(
        partial(
            backward_kernel,
            first=first,
            row_blocks=row_blocks,
            extra=extra,
            shards=shards,
            parts=parts,
            waits=len(waits),
        ),
        grid_spec=pltpu.PrefetchScalarGridSpec(
            num_scalar_prefetch=1,
            grid=(count,),
            in_specs=[
                pl.BlockSpec((rows, width), lambda p, *_: (0, 0)),
                pl.BlockSpec((rows, PAIR), lambda p, *_: (0, offset + p)),
                pl.BlockSpec((rows, PAIR), lambda p, *_: (0, first + p)),
                long_spec((seq, 2 * PAIR), lambda p, *_: (0, offset + p), shards),
                pl.BlockSpec((row_blocks, 1, LISTED, PAIR), lambda p, *_: (0, offset + p, 0, 0)),
                long_spec((1, seq, 2 * extra), lambda p, *_: (offset + p, 0, 0), shards),
            ]
            + specs
            + [pl.BlockSpec(memory_space=pl.ANY)] * len(waits),
            out_specs=[
                pl.BlockSpec((rows, PAIR), lambda p, *_: (0, p)),
                long_spec((seq, 2 * PAIR), lambda p, *_: (0, p), shards),
                pl.BlockSpec((width // 2, 3 * PAIR), lambda p, *_: (0, p)),
                pl.BlockSpec((width // 2, 3 * PAIR), lambda p, *_: (0, p)),
                pl.BlockSpec((1, 1, PAIR), lambda p, *_: (p, 0, 0)),
                pl.BlockSpec((1, 1, PAIR), lambda p, *_: (p, 0, 0)),
            ],
            scratch_shapes=[pltpu.VMEM((seq, 2 * PAIR), F32), *scratch],
        ),
        out_shape=[
            jax.ShapeDtypeStruct((rows, count * PAIR), BF16),
            jax.ShapeDtypeStruct((seq, 2 * count * PAIR), BF16),
            jax.ShapeDtypeStruct((width // 2, 3 * count * PAIR), BF16),
            jax.ShapeDtypeStruct((width // 2, 3 * count * PAIR), BF16),
            jax.ShapeDtypeStruct((count, 1, PAIR), F32),
            jax.ShapeDtypeStruct((count, 1, PAIR), F32),
        ],
        compiler_params=pltpu.CompilerParams(vmem_limit_bytes=60 * MIB),
        cost_estimate=taking(cost),
        name="attention_backward",
    )(starts, x, q, do, kv, probs, global_probs, *pieces, *waits)


def centered_root(value):
    centered = value - jnp.mean(value, axis=1, keepdims=True)
    root = lax.rsqrt(jnp.mean(centered * centered, axis=1, keepdims=True) + EPSILON)
    return centered * root, root


def norm_back(grad, normed, root):
    mean = jnp.mean(grad, axis=1, keepdims=True)
    return root * (grad - mean - normed * jnp.mean(grad * normed, axis=1, keepdims=True))


def both_pieces(ref, core, columns):
    half = ref.shape[3] // 2
    pieces = []
    for piece in (core, 1 - core):
        blocks = [ref[piece, part] for part in range(ref.shape[1])]
        if columns:
            blocks = [b for block in blocks for b in (block[:, :half], block[:, half:])]
        pieces.append(jnp.concatenate(blocks, axis=0))
    return jnp.concatenate(pieces, axis=1 if columns else 0)


def layer_kernel(
    me,
    x_ref,
    att0_ref,
    att1_ref,
    cot_ref,
    keep_ref,
    wo_ref,
    we_ref,
    wc_ref,
    be_ref,
    vec_ref,
    out_ref,
    one_ref,
    do_ref,
    wok_ref,
    woa_ref,
    ck_ref,
    ca_ref,
    ek_ref,
    ea_ref,
    beg_ref,
    vecg_ref,
    norm_ref,
    root_ref,
    low_ref,
    slope_ref,
    hid_ref,
    acc_ref,
    two_ref,
):
    step = pl.program_id(0)
    core = me[0] % 2
    row = lambda i: vec_ref[i : i + 1, :]

    @pl.when(step == 0)
    def _():
        cut = att0_ref.shape[1]
        branch = dot(att0_ref[...], wo_ref[:cut]) + dot(att1_ref[...], wo_ref[cut:])
        normed, root = centered_root(x_ref[...].astype(F32) + branch + row(0))
        norm_ref[...] = normed
        root_ref[...] = root
        normed = normed * row(1) + row(2)
        low_ref[...] = normed.astype(BF16)
        acc_ref[...] = normed + row(3)

    @pl.when(step < 4)
    def _():
        bias = jnp.concatenate([be_ref[core], be_ref[1 - core]], axis=1)
        u = dot(low_ref[...], both_pieces(we_ref, core, True)) + bias
        square = u * u
        t = jnp.tanh(SLOPE * u * (1.0 + CUBIC * square))
        half = 0.5 * (1.0 + t)
        hidden = (u * half).astype(BF16)
        slope_ref[step] = half + (0.5 * SLOPE) * u * (1.0 - t * t) * (
            1.0 + (3.0 * CUBIC) * square
        )
        hid_ref[step] = hidden
        acc_ref[...] += dot(hidden, both_pieces(wc_ref, core, False))

    @pl.when(step == 4)
    def _():
        normed, root = centered_root(acc_ref[...])
        out_ref[...] = (keep_ref[...] * (normed * row(4) + row(5))).astype(BF16)
        cot = cot_ref[...].astype(F32)
        vecg_ref[4:5, :] = jnp.sum(cot * normed, axis=0, keepdims=True)
        vecg_ref[5:6, :] = jnp.sum(cot, axis=0, keepdims=True)
        two = norm_back(cot * row(4), normed, root)
        acc_ref[...] = two
        two = two.astype(BF16)
        two_ref[...] = two
        vecg_ref[3:4, :] = jnp.sum(two.astype(F32), axis=0, keepdims=True)

    @pl.when(step >= 4)
    def _():
        at = step - 4
        piece = ck_ref.shape[1]
        grad = t_dot(hid_ref[at], two_ref[...]).astype(BF16)
        ck_ref[0], ca_ref[0] = grad[:piece], grad[piece:]
        grad = dot_t(two_ref[...], both_pieces(wc_ref, core, False)) * slope_ref[at]
        grad = grad.astype(BF16)
        total = jnp.sum(grad.astype(F32), axis=0, keepdims=True)
        beg_ref[core], beg_ref[1 - core] = total[:, :piece], total[:, piece:]
        acc_ref[...] += dot_t(grad, both_pieces(we_ref, core, True))
        grad = t_dot(low_ref[...], grad).astype(BF16)
        ek_ref[0], ea_ref[0] = grad[:, :piece], grad[:, piece:]

    @pl.when(step == 7)
    def _():
        first = acc_ref[...]
        normed = norm_ref[...]
        vecg_ref[1:2, :] = jnp.sum(first * normed, axis=0, keepdims=True)
        vecg_ref[2:3, :] = jnp.sum(first, axis=0, keepdims=True)
        one = norm_back(first * row(1), normed, root_ref[...])
        one_ref[...] = one
        one = one.astype(BF16)
        vecg_ref[0:1, :] = jnp.sum(one.astype(F32), axis=0, keepdims=True)
        vecg_ref[6:8, :] = jnp.zeros((2, one.shape[1]), F32)
        grad = [t_dot(att_ref[...], one) for att_ref in (att0_ref, att1_ref)]
        near, away = by_core(jnp.concatenate(grad, axis=0), core, we_ref.shape[1])
        wok_ref[...], woa_ref[...] = near.astype(BF16), away.astype(BF16)
        do_ref[...] = dot_t(one, wo_ref[...]).astype(BF16)


def layer(c, x, attended, cot, keep, w_output, w_hidden, b_expand, vectors):
    rows, width = x.shape
    parts, piece = w_hidden.shape[1], b_expand.shape[2]
    each = piece // parts
    steps = PIECES // 2
    whole = lambda *shape: pl.BlockSpec(shape, lambda s, me: (0,) * len(shape))
    chip = lambda s, me: (s % steps) ^ ((me[0] % PIECES) // 2)
    sent = lambda *shape: pl.BlockSpec((1, *shape), lambda s, me: (jnp.maximum(s - steps, 0), 0, 0))
    return pl.pallas_call(
        layer_kernel,
        grid_spec=pltpu.PrefetchScalarGridSpec(
            num_scalar_prefetch=1,
            grid=(2 * steps,),
            in_specs=[
                whole(rows, width),
                *[whole(*a.shape) for a in attended],
                whole(rows, width),
                whole(rows, 1),
                whole(width, width),
                pl.BlockSpec((2, parts, each, width), lambda s, me: (chip(s, me), 0, 0, 0)),
                pl.BlockSpec((2, parts, each, width), lambda s, me: (chip(s, me), 0, 1, 0)),
                pl.BlockSpec((2, 1, piece), lambda s, me: (chip(s, me), 0, 0)),
                whole(8, width),
            ],
            out_specs=[
                whole(rows, width),
                whole(rows, width),
                whole(rows, width),
                whole(width // 2, width),
                whole(width // 2, width),
                sent(piece, width),
                sent(piece, width),
                sent(width, piece),
                sent(width, piece),
                pl.BlockSpec((2, 1, piece), lambda s, me: (chip(jnp.maximum(s - steps, 0), me), 0, 0)),
                whole(8, width),
            ],
            scratch_shapes=[
                pltpu.VMEM((rows, width), F32),
                pltpu.VMEM((rows, 1), F32),
                pltpu.VMEM((rows, width), BF16),
                pltpu.VMEM((steps, rows, 2 * piece), F32),
                pltpu.VMEM((steps, rows, 2 * piece), BF16),
                pltpu.VMEM((rows, width), F32),
                pltpu.VMEM((rows, width), BF16),
            ],
        ),
        out_shape=[
            jax.ShapeDtypeStruct((rows, width), BF16),
            jax.ShapeDtypeStruct((rows, width), F32),
            jax.ShapeDtypeStruct((rows, width), BF16),
            jax.ShapeDtypeStruct((width // 2, width), BF16),
            jax.ShapeDtypeStruct((width // 2, width), BF16),
            jax.ShapeDtypeStruct((steps, piece, width), BF16),
            jax.ShapeDtypeStruct((steps, piece, width), BF16),
            jax.ShapeDtypeStruct((steps, width, piece), BF16),
            jax.ShapeDtypeStruct((steps, width, piece), BF16),
            jax.ShapeDtypeStruct((PIECES, 1, piece), F32),
            jax.ShapeDtypeStruct((8, width), F32),
        ],
        compiler_params=pltpu.CompilerParams(vmem_limit_bytes=58 * MIB),
        cost_estimate=taking(35),
        name="layer",
    )(
        jnp.reshape(c, (1,)).astype(jnp.int32),
        x,
        *attended,
        cot,
        keep,
        w_output,
        w_hidden,
        w_hidden,
        b_expand,
        vectors,
    )


def pair_sum(grad_refs, weight_refs, columns, at):
    grads = jnp.concatenate([ref[...] for ref in grad_refs], axis=1)
    weights = []
    for group, offset, count in BACK:
        for pair in range(offset, offset + count):
            start = 3 * PAIR * pair + at
            weights.append(weight_refs[group][:, start : start + columns])
    return dot_t(grads, jnp.concatenate(weights, axis=1))


def token_kernel(me, *refs, away, extra, count):
    sides = len(BACK)
    dkv_refs, w_refs = refs[:sides], refs[sides : sides + 2]
    c, step = me[0], pl.program_id(0)
    piece = 2 * step + (1 if away else 0)
    half = dkv_refs[0].shape[0] // 2
    if away:
        dq_refs, one_ref = refs[sides + 2 : 2 * sides + 2], refs[2 * sides + 2]
        out_ref, share_ref = refs[-2:]

        @pl.when(step == 0)
        def _():
            share_ref[...] = one_ref[...] + pair_sum(dq_refs, w_refs, PAIR, 0)

        share = lambda: share_ref[2 * half : 2 * half + extra, :]
    else:
        share_ref, out_ref = refs[sides + 2], refs[-1]
        share = lambda: share_ref[...]
    total = pair_sum(dkv_refs, w_refs, 2 * PAIR, PAIR).astype(BF16)
    out_ref[0, 0], out_ref[1, 0] = total[:half], total[half:]

    @pl.when((piece == c) & (c < count))
    def _():
        at = pl.ds(pl.multiple_of(c * extra, extra), extra)
        out_ref[0, 0, at, :] = (out_ref[0, 0, at, :].astype(F32) + share()).astype(BF16)


def token_share(c, dkvs, weights, more, away, waits, rows, extra, count):
    seq, width = dkvs[0].shape[0], weights[0].shape[0]
    chips = seq // rows // 2
    other = 1 if away else 0
    full = lambda a: pl.BlockSpec(a.shape, lambda j, me: (0,) * a.ndim)
    out_specs = [pl.BlockSpec((2, 1, rows // 2, width), lambda j, me: (0, j, 0, 0))]
    out_shape = [jax.ShapeDtypeStruct((2, chips, rows // 2, width), BF16)]
    if away:
        out_specs.append(pl.BlockSpec((rows + extra, width), lambda j, me: (0, 0)))
        out_shape.append(jax.ShapeDtypeStruct((rows + extra, width), F32))
    return pl.pallas_call(
        partial(token_kernel, away=away, extra=extra, count=count),
        grid_spec=pltpu.PrefetchScalarGridSpec(
            num_scalar_prefetch=1,
            grid=(chips,),
            in_specs=[
                pl.BlockSpec((rows, a.shape[1]), lambda j, me: (2 * j + other, 0))
                for a in dkvs
            ]
            + [full(a) for a in (*weights, *more)]
            + [pl.BlockSpec(memory_space=pl.ANY)] * len(waits),
            out_specs=out_specs,
        ),
        out_shape=out_shape,
        compiler_params=pltpu.CompilerParams(vmem_limit_bytes=48 * MIB),
        cost_estimate=taking(3),
        name="token_share",
    )(jnp.reshape(c, (1,)).astype(jnp.int32), *dkvs, *weights, *more, *waits)


def by_pair(queries, keys, values):
    count = queries.shape[0]
    together = [a.reshape(count, PAIRS, PAIR) for a in (queries, keys, values)]
    together = jnp.concatenate(together, axis=2).reshape(count * PAIRS, 3 * PAIR)
    places = jnp.arange(3 * PAIR, dtype=jnp.int32)
    source = jnp.array((1, 0, 4, 2, 3, 5), jnp.int32)[places // HD] * HD + places % HD
    return ordered(together, source).astype(BF16).reshape(count, PAIRS * 3 * PAIR)


def column_places(pairs):
    start = jnp.arange(pairs, dtype=jnp.int32)[:, None, None] * (3 * PAIR)
    inner = jnp.arange(HD, dtype=jnp.int32)
    for spots in ((1, 0), (3, 4), (2, 5)):
        yield (start + jnp.array(spots, jnp.int32)[:, None] * HD + inner).reshape(-1)


def swapped(value, bit):
    shards = lax.axis_size("ctx")
    return lax.ppermute(value, "ctx", [(i, i ^ bit) for i in range(shards)])


def own_bit(bit):
    return (lax.axis_index("ctx") // bit) % 2


def added(keep, came):
    return (keep.astype(F32) + came.astype(F32)).astype(BF16)


def halved(value, axis, bit):
    mine = own_bit(bit)
    away = lax.dynamic_index_in_dim(value, 1 - mine, axis, keepdims=False)
    keep = lax.dynamic_index_in_dim(value, mine, axis, keepdims=False)
    return added(keep, swapped(away, bit))


def doubled(value, bit):
    other = swapped(value, bit)
    mine = own_bit(bit) == 0
    return jnp.stack([jnp.where(mine, value, other), jnp.where(mine, other, value)])


def plane_gather(value):
    value = value[None]
    for bit in (1, 2, 4):
        value = doubled(value, bit)
        value = value.reshape(-1, *value.shape[2:])
    return value


def line_step(value, bit):
    parts = lax.axis_size("wt")
    other = lax.ppermute(value, "wt", [(i, i ^ bit) for i in range(parts)])
    mine = lax.axis_index("wt") // bit % 2 == 0
    return jnp.concatenate([jnp.where(mine, value, other), jnp.where(mine, other, value)])


def line_gather(value, bit=1):
    while bit < lax.axis_size("wt"):
        value = line_step(value, bit)
        bit *= 2
    return value


def token_gather(own):
    shards, half = lax.axis_size("ctx"), own.shape[0] // 2
    along_x, along_y = swapped(own, 2), swapped(own, 4)
    far = jnp.concatenate([swapped(along_y[:half], 2), swapped(along_x[half:], 4)], axis=0)
    pieces = []
    for piece in (own, along_x, along_y, far):
        pieces += [piece, swapped(piece, 1)]
    bit = PIECES
    while bit < shards:
        pieces += [swapped(piece, bit) for piece in pieces]
        bit *= 2
    return pieces


def far_sum(value, shards):
    if shards == PIECES:
        return value
    return lax.psum(value, "ctx", axis_index_groups=across_groups(shards))


def same_core(shards, block):
    return [list(range(s + k, s + block, 2)) for s in range(0, shards, block) for k in range(2)]


def rows_start(near, came):
    parts, columns = lax.axis_size("wt"), near.shape[1]
    near, came = (a.reshape(parts, PIECES // 2, -1, columns) for a in (near, came))
    return jnp.transpose(added(near, came), (1, 0, 2, 3)).reshape(parts * PIECES // 2, -1, columns)


def rows_send(sums):
    shards, parts = lax.axis_size("ctx"), lax.axis_size("wt")
    sums = far_sum(sums, shards)
    groups = [[i * parts + w for i in g for w in range(parts)] for g in same_core(shards, PIECES)]
    return lax.all_to_all(
        sums, ("ctx", "wt"), split_axis=0, concat_axis=0, axis_index_groups=groups, tiled=True
    )


def rows_add(sums):
    return jnp.sum(sums.astype(F32), axis=0).astype(BF16)


def rows_sum(sums):
    return rows_add(rows_send(sums))


def ordered(value, source):
    rows = jnp.arange(value.shape[1], dtype=jnp.int32)
    return dot(value, (rows[:, None] == source[None, :]).astype(BF16))


def start_kernel(me, q_ref, k_ref, v_ref, o_ref, e_ref, c_ref, *rest, parts):
    vectors, (lead_ref, more_ref) = rest[:-2], rest[-2:]
    c = me[0]
    half, width = lead_ref.shape[0] - 8, lead_ref.shape[1]
    piece = c % PIECES
    own = pl.ds(pl.multiple_of(c % 2 * half, 16), half)
    low = lax.broadcasted_iota(jnp.int32, (1, PAIR), 1) < HD
    flip = lambda a: jnp.concatenate([a[:, HD:], a[:, :HD]], axis=1)
    columns = []
    for pair in range(PAIRS):
        at = slice(pair * PAIR, (pair + 1) * PAIR)
        q, k, v = (ref[own, at].astype(F32) for ref in (q_ref, k_ref, v_ref))
        k = flip(k)
        columns += [flip(q), jnp.where(low, v, k), jnp.where(low, k, v)]
    ahead = 3 * AHEAD
    small = [r[...].astype(F32).reshape(1, -1) for r in vectors]
    some = [jnp.concatenate(small[i : i + parts], axis=1) for i in range(0, 2 * parts, parts)]
    some += small[2 * parts :]
    small = jnp.concatenate(some + [jnp.zeros((8 - len(some), width), F32)], axis=0)
    lead = jnp.concatenate([jnp.concatenate(columns[:ahead], axis=1), small], axis=0)
    lead_ref[...] = lead.astype(BF16)

    run = e_ref.shape[1] // parts // PIECES
    block = e_ref.shape[1] // parts
    runs = []
    for part in range(parts):
        here = e_ref[:, part * block : (part + 1) * block].astype(F32)
        runs.append(pltpu.roll(here, block - piece * run, 1)[:, :run])
    runs = jnp.concatenate(runs, axis=1)
    count = runs.shape[0] // 2
    more_ref[:count] = jnp.concatenate([runs[:count], runs[count:]], axis=1).astype(BF16)
    rows = c_ref.shape[0] // PIECES
    more_ref[count : count + rows] = c_ref[pl.ds(pl.multiple_of(piece * rows, 16), rows), :]
    at = count + rows
    left = (PAIRS - AHEAD) * 3 * PAIR // width
    for i in range(left):
        some = columns[ahead + i * width // PAIR : ahead + (i + 1) * width // PAIR]
        more_ref[at : at + half] = jnp.concatenate(some, axis=1).astype(BF16)
        at += half
    rows = o_ref.shape[0] // PIECES
    whole = o_ref[...].astype(F32)
    turned = pltpu.roll(whole, whole.shape[0] - piece * rows, 0)
    more_ref[at:] = turned[: more_ref.shape[0] - at].astype(BF16)


def start_arrays(c, weights, vectors, parts):
    half, width = weights[0].shape[0] // 2, weights[0].shape[1]
    count = weights[4].shape[0] // 2 + weights[5].shape[0] // PIECES
    count += (PAIRS - AHEAD) * 3 * PAIR // width * half
    count += -(-weights[3].shape[0] // PIECES // 16) * 16
    full = lambda shape: pl.BlockSpec(shape, lambda i: (0,) * len(shape))
    shapes = [(half + 8, width), (count, width)]
    return pl.pallas_call(
        partial(start_kernel, parts=parts),
        grid=(1,),
        in_specs=[pl.BlockSpec(memory_space=pltpu.SMEM)] + [full(a.shape) for a in (*weights, *vectors)],
        out_specs=[full(shape) for shape in shapes],
        out_shape=[jax.ShapeDtypeStruct(shape, BF16) for shape in shapes],
        compiler_params=pltpu.CompilerParams(vmem_limit_bytes=60 * MIB),
        cost_estimate=taking(3),
        name="start_arrays",
    )(jnp.reshape(c, (1,)).astype(jnp.int32), *weights, *vectors)


def vector_kernel(*refs, parts):
    sides = len(BACK)
    joined = lambda some: jnp.concatenate([r[i] for r in some for i in range(r.shape[0])], axis=1)
    grads_ref, expand_ref, _, out_ref = refs[2 * sides :]
    rows = [joined(refs[:sides]), joined(refs[sides : 2 * sides])]
    rows += [grads_ref[i : i + 1, :] for i in (0, 3, 1, 2, 4, 5)]
    width = out_ref.shape[1]
    share, run = width // parts, expand_ref.shape[2] // parts
    out = []
    for part in range(parts):
        cuts = [row[:, part * share : (part + 1) * share] for row in rows]
        out += [jnp.concatenate(cuts[i : i + parts], axis=1) for i in range(0, len(cuts), parts)]
        cuts = [expand_ref[p, :, part * run : (part + 1) * run] for p in range(PIECES)]
        out.append(jnp.concatenate(cuts, axis=1))
        out.append(jnp.zeros((PIECES - len(rows) // parts - 1, width), F32))
    out_ref[...] = jnp.concatenate(out, axis=0).astype(BF16)


def vector_rows(q_sums, v_sums, grads, expand_grads, wait, parts):
    return pl.pallas_call(
        partial(vector_kernel, parts=parts),
        in_specs=[pl.BlockSpec(memory_space=pltpu.VMEM)] * (2 * len(BACK) + 2)
        + [pl.BlockSpec(memory_space=pl.ANY)],
        out_shape=jax.ShapeDtypeStruct((parts * PIECES, grads.shape[1]), BF16),
        cost_estimate=taking(1),
        name="vector_rows",
    )(*q_sums, *v_sums, grads, expand_grads, wait)


def expand_kernel(in_ref, out_ref):
    pieces, half, run = in_ref.shape[0], in_ref.shape[1], in_ref.shape[2] // 2
    parts = out_ref.shape[1] // in_ref.shape[2]
    count = run // parts
    for lower in range(2):
        for part in range(parts):
            at = lower * run + part * count
            runs = [in_ref[p, :, at : at + count].astype(F32) for p in range(pieces)]
            out_ref[
                lower * half : (lower + 1) * half, part * 2 * run : (part + 1) * 2 * run
            ] = jnp.concatenate(runs, axis=1)


def expand_columns(gathered, each_piece, parts):
    width = gathered.shape[2]
    return pl.pallas_call(
        expand_kernel,
        grid=(1,),
        in_specs=[pl.BlockSpec((PIECES, each_piece, width), lambda i: (0, 1, 0))],
        out_specs=pl.BlockSpec((2 * each_piece, parts * width), lambda i: (0, 0)),
        out_shape=jax.ShapeDtypeStruct((2 * each_piece, parts * width), F32),
        compiler_params=pltpu.CompilerParams(vmem_limit_bytes=24 * MIB),
        cost_estimate=taking(2),
        name="expand_columns",
    )(gathered)


def body(
    tokens,
    cotangent,
    lengths,
    rand_blocks,
    query_weight,
    key_weight,
    value_weight,
    output_weight,
    expand_weight,
    contract_weight,
    query_bias,
    value_bias,
    output_bias,
    expand_bias,
    contract_bias,
    attn_gain,
    attn_shift,
    ffn_gain,
    ffn_shift,
):
    shards = lax.axis_size("ctx")
    parts = lax.axis_size("wt")
    c = lax.axis_index("ctx")
    rows, width = tokens.shape[1], tokens.shape[2]
    row_blocks = rows // BLOCK
    seq = shards * rows
    global_count = GLOB * BLOCK
    extra = 16 * (-(-global_count // (16 * shards)))
    hidden_width = expand_weight.shape[1]
    part = expand_weight.shape[0]
    piece = hidden_width // PIECES
    length = lengths[0]
    inputs = tokens[0]

    pieces = token_gather(inputs)
    half = part // 2
    leading, behind = start_arrays(
        c,
        (query_weight, key_weight, value_weight, output_weight, expand_weight, contract_weight),
        (
            query_bias,
            value_bias,
            output_bias,
            contract_bias,
            attn_gain,
            attn_shift,
            ffn_gain,
            ffn_shift,
            expand_bias,
        ),
        parts,
    )
    early_lead = line_step(leading[None], 1)
    leading = line_gather(after(early_lead, pieces[2], pieces[4]), 2)
    vectors = leading[:, half:].reshape(parts, -1)
    leading = leading[:, :half]

    def joined(bundle):
        return jnp.transpose(doubled(bundle, 1), (1, 0, 2, 3)).reshape(width, -1)

    weights = [joined(leading)]
    each = width // parts
    b_query, b_value, b_output, b_contract, g_attn, s_attn, g_ffn, s_ffn = (
        vectors[:, i * each : (i + 1) * each].reshape(-1).astype(F32) for i in range(8)
    )
    b_expand = vectors[:, 8 * each : 8 * each + hidden_width // parts].reshape(parts, PIECES, -1)
    b_expand = jnp.transpose(b_expand, (1, 0, 2)).reshape(PIECES, 1, piece).astype(F32)

    each_piece = piece // parts
    o_rows = part // PIECES
    mixed = 2 * each_piece
    w_hidden = lax.all_gather(behind, "wt")
    following = w_hidden[:, mixed : mixed + 2 * half].reshape(parts, 2, half, width)
    following = jnp.concatenate([following[:, 0], following[:, 1]], axis=2)
    w_hidden = jnp.concatenate(
        [w_hidden[:, :mixed], w_hidden[:, mixed + 2 * half : mixed + 2 * half + o_rows]], axis=1
    )

    start = jnp.minimum(c * extra, global_count - extra)
    more = lax.dynamic_slice_in_dim(pieces[0], start, extra, 0)
    for i in range(1, shards):
        other = lax.dynamic_slice_in_dim(pieces[i], start, extra, 0)
        more = jnp.where(c == i, other, more)
    x = jnp.concatenate([inputs, more], axis=0)
    index = jnp.arange(rows + extra, dtype=jnp.int32)
    position = jnp.where(index < rows, c * rows + index, c * extra + index - rows)
    is_global = position < global_count
    usable = ((position < length) & (is_global == (index >= rows)))[:, None]
    own = c * row_blocks + jnp.arange(row_blocks, dtype=jnp.int32)
    beside = own[:, None, None] + jnp.arange(-1, 2, dtype=jnp.int32)
    listed = jnp.concatenate(
        [jnp.broadcast_to(beside, (row_blocks, H, 3)), rand_blocks[0]], axis=2
    )
    blocks = seq // BLOCK
    inside = (listed >= 0) & (listed < blocks)
    listed = jnp.clip(listed, 0, blocks - 1)
    limits = jnp.where(inside, length - listed * BLOCK, 0).reshape(-1)
    order = jnp.arange(shards, dtype=jnp.int32) ^ c
    limits = jnp.concatenate([limits, length - order * rows])
    starts = (listed // row_blocks ^ c) * rows + listed % row_blocks * BLOCK
    starts = jnp.concatenate([starts.reshape(-1), jnp.stack([c * rows, c % 2])])

    given = jnp.where(c == 0, cotangent[0, :global_count], jnp.zeros((), BF16))
    given = jnp.pad(given, ((0, shards * extra - global_count), (0, 0)))
    given = after(given.reshape(shards, extra, width), pieces[4])
    given = lax.all_to_all(given, "ctx", split_axis=0, concat_axis=0, tiled=True)
    cot = jnp.concatenate([cotangent[0], given[0]], axis=0)
    cot = jnp.where(usable, cot, jnp.zeros((), BF16))

    b_qkv = by_pair(*(b.astype(BF16)[None] for b in (b_query, jnp.zeros_like(b_value), b_value)))
    b_qkv = b_qkv.astype(F32).reshape(PAIRS, 1, 3 * PAIR)
    zero = jnp.zeros_like(b_output)
    vectors = jnp.stack([b_output, g_attn, s_attn, b_contract, g_ffn, s_ffn, zero, zero])
    keep = usable.astype(F32)
    w_hidden = after(
        w_hidden, *pieces, weights[0], cot, starts, limits, b_qkv, vectors, b_expand, keep, x
    )
    w_hidden = lax.all_gather(w_hidden, "ctx", axis_index_groups=groups_of(shards))
    w_output = jnp.transpose(w_hidden[:, :, 2 * each_piece :], (1, 0, 2, 3)).reshape(width, width)
    forward = partial(attention_forward, starts, limits, x, pieces)
    kept = [forward(weights[0], b_qkv, (cot,), *GROUPS[0], extra)]
    weights.append(joined(following))
    kept.append(forward(weights[1], b_qkv, (), *GROUPS[1], extra))

    (
        layer_out,
        grad_one,
        grad_attended,
        o_keep,
        o_away,
        c_keep,
        c_away,
        e_keep,
        e_away,
        expand_bgrad,
        vector_grads,
    ) = layer(
        c,
        x,
        [k[2] for k in kept],
        cot,
        keep,
        w_output,
        w_hidden,
        b_expand,
        vectors,
    )

    def attention_back(side, *waits):
        group, offset, count = BACK[side]
        q, kv, _, probs, global_probs = kept[group]
        first = GROUPS[group][0] + offset
        return attention_backward(
            starts,
            x,
            pieces,
            q,
            grad_attended,
            kv,
            probs,
            global_probs,
            waits,
            first,
            offset,
            count,
            BACK_COST[side],
            extra,
        )

    c_came, e_came = swapped(c_away, 1), swapped(e_away, 1)
    early = [rows_start(o_keep, swapped(o_away, 1))]
    backs = [attention_back(0)]
    steps = PIECES // 2
    c_keep, c_came = (a.reshape(2, 2, piece, width) for a in (c_keep, c_came))
    e_keep, e_came = (a.reshape(2, 2, width, piece) for a in (e_keep, e_came))
    c_away = added(c_keep[:, 1], c_came[:, 1])
    e_away = added(e_keep[1], e_came[1])
    c_came_on, e_came_on = swapped(c_away, 2), swapped(e_away, 4)
    c_keep = added(c_keep[:, 0], c_came[:, 0])
    e_keep = added(e_keep[0], e_came[0])

    early.append(rows_start(backs[0][2], swapped(backs[0][3], 1)))
    early = jnp.concatenate(early, axis=1)
    backs.append(attention_back(1, c_away, e_away, early))
    early = rows_sum(early)
    c_away, e_away = added(c_keep[1], c_came_on[1]), added(e_keep[1], e_came_on[1])
    c_last, e_last = swapped(c_away, 4), swapped(e_away, 2)
    c_keep, e_keep = added(c_keep[0], c_came_on[0]), added(e_keep[0], e_came_on[0])

    middle = rows_start(backs[1][2], swapped(backs[1][3], 1))
    backs.append(attention_back(2, c_away, e_away, early, middle))
    middle = rows_sum(middle)
    c_mine = far_sum(added(c_keep, c_last), shards).reshape(parts, -1, width)
    e_mine = far_sum(added(e_keep, e_last), shards).reshape(parts, 2, -1, piece)
    e_mine = jnp.concatenate([e_mine[:, 0], e_mine[:, 1]], axis=2)
    hidden_sums = jnp.concatenate([c_mine, e_mine], axis=1)
    both = lax.all_to_all(hidden_sums, "wt", split_axis=0, concat_axis=0, tiled=True)
    backs.append(attention_back(3, hidden_sums, middle))

    small = vector_rows([b[4] for b in backs], [b[5] for b in backs], vector_grads, expand_bgrad, backs[3][0], parts)
    small = small.reshape(parts, 2, -1, width)
    near = jnp.concatenate([backs[2][2], backs[3][2]], axis=1).reshape(parts, PIECES // 2, -1, width)
    near = jnp.concatenate(
        [near, lax.dynamic_index_in_dim(small, own_bit(1), 1, keepdims=False)[:, :, None]], axis=2
    )
    far = jnp.concatenate([backs[2][3], backs[3][3]], axis=1).reshape(parts, PIECES // 2, -1, width)
    far = jnp.concatenate(
        [far, lax.dynamic_index_in_dim(small, 1 - own_bit(1), 1, keepdims=False)[:, :, None]], axis=2
    )
    late = rows_start(near.reshape(-1, width), swapped(far, 1))

    share = partial(token_share, c, [b[1] for b in backs], weights)
    count = global_count // extra
    away, own = share(
        [b[0] for b in backs] + [grad_one], True, (late,), rows, extra, count
    )
    both = jnp.sum(after(both, away).astype(F32), axis=0).astype(BF16)
    both = jnp.concatenate([both, early, middle, layer_out[rows:]], axis=0)
    (keep,) = share([own[rows:]], False, (away, both, late), rows, extra, count)
    late = rows_send(late)
    came = swapped(away, 1)
    chips = shards // 2
    if chips > 4:
        keep = added(keep, came)
        while chips > 4:
            keep = added(keep[:, : chips // 2], swapped(keep[:, chips // 2 :], chips))
            chips //= 2
        came = jnp.zeros_like(keep)
    keep, came = (a.reshape(2, 2, 2, rows // 2, width) for a in (keep, came))
    above, below = (keep[0], came[0]), (keep[1], came[1])
    above_sent = added(above[0][:, 1], above[1][:, 1])
    below_sent = added(below[0][1], below[1][1])
    late = rows_add(after(late, above_sent, below_sent))
    above_came, below_came = swapped(above_sent, 2), swapped(below_sent, 4)
    above = added(above[0][:, 0], above[1][:, 0])
    below = added(below[0][0], below[1][0])
    rows_late = late.shape[0]
    late = jnp.pad(late, ((0, -rows_late % 8), (0, 0)))
    late = doubled(late, 1)
    late = doubled(late, 2).reshape(4, -1, width)

    def carried(sent, more, bit):
        count = sent.shape[0]
        flat = swapped(jnp.concatenate([sent, more.reshape(-1, width)], axis=0), bit)
        other = flat[count:].reshape(more.shape)
        mine = own_bit(bit) == 0
        more = jnp.concatenate([jnp.where(mine, more, other), jnp.where(mine, other, more)])
        return flat[:count], more

    hidden_rows = 2 * each_piece
    gathered = lax.all_gather(both, "ctx", axis_index_groups=groups_of(shards))

    contract_wgrad = gathered[:, :each_piece].reshape(-1, width).astype(F32)
    expand_wgrad = expand_columns(gathered, each_piece, parts)
    finished = gathered[:, -extra:].reshape(-1, width)
    on_first = (c == 0) & (index[:rows] < global_count)
    finished = jnp.pad(finished[:global_count], ((0, rows - global_count), (0, 0)))
    layer_out = jnp.where(on_first[:, None], finished, layer_out[:rows])

    above_came = after(above_came, contract_wgrad, expand_wgrad, layer_out)
    below_came = after(below_came, contract_wgrad, expand_wgrad, layer_out)

    above_sent = added(above[1], above_came[1])
    below_sent = added(below[1], below_came[1])
    above_last, late = carried(above_sent, late, 4)
    below_last = swapped(below_sent, 2)
    late = late[:, : rows_late]
    above = above[0].astype(F32) + above_came[0].astype(F32) + above_last.astype(F32)
    below = below[0].astype(F32) + below_came[0].astype(F32) + below_last.astype(F32)
    input_grad = own[:rows] + jnp.concatenate([above, below], axis=0)

    kinds = [gathered[:, hidden_rows:-extra].reshape(PIECES, 3, -1, width)]
    kinds.append(late[:, None, :-1])
    mine = jnp.concatenate(kinds, axis=1).reshape(PIECES // 2, 2, 4, -1, width)
    mine = jnp.transpose(mine, (2, 1, 0, 3, 4)).reshape(4, part, width)
    small = jnp.transpose(late[:, -1].reshape(PIECES // 2, 2, width), (1, 0, 2)).reshape(-1, width)
    small = small.astype(F32)
    small_grads = [small[i // parts, i % parts * each :][:each] for i in range(8)]
    expand_bias_grad = small[2]
    output_wgrad = mine[0].astype(F32)
    query_wgrad, key_wgrad, value_wgrad = (
        jnp.concatenate([ordered(g, places) for g in (mine[1], mine[2], mine[3])], axis=1)
        for places in column_places(AHEAD)
    )

    return (
        layer_out[None],
        input_grad[None],
        query_wgrad,
        key_wgrad,
        value_wgrad,
        output_wgrad,
        expand_wgrad,
        contract_wgrad,
        small_grads[0],
        small_grads[1],
        small_grads[2],
        expand_bias_grad,
        small_grads[3],
        small_grads[4],
        small_grads[5],
        small_grads[6],
        small_grads[7],
    )


def solution(mesh):
    tokens, weight, vector = P("wt", "ctx", None), P("wt", None), P("wt")
    return jax.shard_map(
        body,
        mesh=mesh,
        in_specs=(tokens, tokens, vector, P("wt", "ctx", None, None)) + (weight,) * 6 + (vector,) * 9,
        out_specs=(tokens, tokens) + (weight,) * 6 + (vector,) * 9,
        check_vma=False,
    )
```

```python
from functools import partial, reduce

import jax
import jax.numpy as jnp
from jax import lax
from jax.experimental import pallas as pl
from jax.experimental.pallas import tpu as pltpu
from jax.sharding import PartitionSpec as P

H = 12
HD = 64
BLOCK = 64
GLOB = 2
RAND = 3
PAIR = 2 * HD
PAIRS = H // 2
AHEAD = 2
GROUPS = ((0, AHEAD), (AHEAD, PAIRS - AHEAD))
BACK = ((0, 0, 2), (1, 0, 2), (1, 2, 1), (1, 3, 1))
BACK_COST = (8, 8, 8, 20)
MOVING = 3 + RAND
TOGETHER = 8
LISTED = (GLOB + MOVING) * BLOCK
PIECES = 8
NEGATIVE = -1e30
EPSILON = 1e-12
FACTOR = HD ** (-0.5)
SLOPE = (2.0 / jnp.pi) ** 0.5
CUBIC = 0.044715
F32 = jnp.float32
BF16 = jnp.bfloat16
MIB = 2**20


def taking(microseconds):
    return pl.CostEstimate(
        flops=int(microseconds * 10**9), bytes_accessed=10**6, transcendentals=0
    )


def groups_of(shards):
    return [list(range(s, s + PIECES)) for s in range(0, shards, PIECES)]


def across_groups(shards):
    return [list(range(s, shards, PIECES)) for s in range(PIECES)]


def dot(a, b):
    return jnp.dot(a, b, preferred_element_type=F32)


def dot_t(a, b):
    return lax.dot_general(a, b, (((1,), (1,)), ((), ())), preferred_element_type=F32)


def t_dot(a, b):
    return lax.dot_general(a, b, (((0,), (0,)), ((), ())), preferred_element_type=F32)


def after(value, *earlier):
    return pl.pallas_call(
        lambda *refs: None,
        in_specs=[pl.BlockSpec(memory_space=pl.ANY)] * (1 + len(earlier)),
        out_specs=pl.BlockSpec(memory_space=pl.ANY),
        out_shape=jax.ShapeDtypeStruct(value.shape, value.dtype),
        input_output_aliases={0: 0},
        name="after",
    )(value, *earlier)


def by_head(both, low, inner):
    zero = jnp.zeros_like(both)
    first, second = jnp.where(low, both, zero), jnp.where(low, zero, both)
    if inner:
        first, second = second, first
    return jnp.concatenate(
        [jnp.concatenate([first, zero], axis=1), jnp.concatenate([zero, second], axis=1)], axis=0
    )


def listed_keys(starts, spot, top, kv_ref):
    rows = [
        [pl.multiple_of(starts[spot + head * MOVING + i], BLOCK) for i in range(MOVING)]
        for head in range(2)
    ]
    parts = [kv_ref[pl.ds(top, GLOB * BLOCK), :]]
    parts += [kv_ref[pl.ds(at, BLOCK), :] for at in rows[0][:3]]
    parts += [
        jnp.concatenate(
            [kv_ref[pl.ds(first, BLOCK), :PAIR], kv_ref[pl.ds(second, BLOCK), PAIR:]], axis=1
        )
        for first, second in zip(rows[0][3:], rows[1][3:])
    ]
    return jnp.concatenate(parts, axis=0), rows


def loader(refs, streamed):
    if not streamed:
        return lambda i: refs[i][...]
    buffer, semaphore = streamed

    def load(i):
        copy = pltpu.make_async_copy(refs[i], buffer, semaphore)
        copy.start()
        copy.wait()
        return buffer[...]

    return load


def softmax(scores):
    raised = jnp.exp(scores - jnp.max(scores, axis=0, keepdims=True))
    return (raised * (1.0 / jnp.sum(raised, axis=0, keepdims=True))).astype(BF16)


def by_core(grad, core, parts):
    half = grad.shape[0] // parts // 2
    halves = [
        jnp.concatenate([grad[at : at + half] for at in range(i * half, grad.shape[0], 2 * half)])
        for i in range(2)
    ]
    first = core == 0
    return jnp.where(first, halves[0], halves[1]), jnp.where(first, halves[1], halves[0])


def forward_kernel(
    starts, limits, x_ref, w_ref, b_ref, *rest, first, row_blocks, extra, shards, waits
):
    seen_refs = rest[:shards]
    q_ref, kv_ref, out_ref, p_ref, pg_ref = rest[shards + waits :][:5]
    tokens = loader(seen_refs, rest[shards + waits + 5 :])
    top = pl.multiple_of(starts[row_blocks * H * MOVING], BLOCK)
    pair = first + pl.program_id(0)
    rows = row_blocks * BLOCK
    low = lax.broadcasted_iota(jnp.int32, (1, PAIR), 1) < HD
    within = lax.broadcasted_iota(jnp.int32, (BLOCK, PAIR), 0)

    queries = dot(x_ref[...], w_ref[:, :PAIR]) + b_ref[0, :, :PAIR]
    q_ref[...] = (queries.astype(BF16).astype(F32) * FACTOR).astype(BF16)

    for i in range(shards):
        kv = dot(tokens(i), w_ref[:, PAIR:]) + b_ref[0, :, PAIR:]
        kv_ref[i * rows : (i + 1) * rows, :] = kv.astype(BF16)

    def some_blocks(group, carry):
        blocks = [group * TOGETHER + i for i in range(TOGETHER)]
        ats = [pl.ds(pl.multiple_of(block * BLOCK, BLOCK), BLOCK) for block in blocks]
        spots = [(block * H + 2 * pair) * MOVING for block in blocks]
        kvs = [listed_keys(starts, spot, top, kv_ref)[0] for spot in spots]
        scores = [dot_t(kv, by_head(q_ref[at, :], low, True)) for kv, at in zip(kvs, ats)]
        probs = []
        for some, spot in zip(scores, spots):
            masked = [some[: GLOB * BLOCK]]
            for i in range(MOVING):
                limit = jnp.where(low, limits[spot + i], limits[spot + MOVING + i])
                here = some[(GLOB + i) * BLOCK : (GLOB + i + 1) * BLOCK]
                masked.append(jnp.where(within < limit, here, NEGATIVE))
            probs.append(softmax(jnp.concatenate(masked, axis=0)))
        outs = [t_dot(some, kv) for some, kv in zip(probs, kvs)]
        for block, at, some, out in zip(blocks, ats, probs, outs):
            p_ref[block, 0] = some
            out_ref[at, :] = jnp.where(low, out[:BLOCK, :PAIR], out[BLOCK:, PAIR:]).astype(BF16)
        return carry

    lax.fori_loop(0, row_blocks // TOGETHER, some_blocks, 0)

    wide = by_head(q_ref[rows : rows + extra, :], low, True)
    within = lax.broadcasted_iota(jnp.int32, (rows, 2 * extra), 0)
    scores = []
    for i in range(shards):
        limit = limits[row_blocks * H * MOVING + i]
        here = dot_t(kv_ref[i * rows : (i + 1) * rows, :], wide)
        scores.append(jnp.where(within < limit, here, NEGATIVE))
    summit = jnp.max(reduce(jnp.maximum, scores), axis=0, keepdims=True)
    raised = [jnp.exp(here - summit) for here in scores]
    share = 1.0 / jnp.sum(reduce(jnp.add, raised), axis=0, keepdims=True)
    out = None
    for i in range(shards):
        here = slice(i * rows, (i + 1) * rows)
        probs = (raised[i] * share).astype(BF16)
        pg_ref[0, here, :] = probs
        term = t_dot(probs, kv_ref[here, :])
        out = term if out is None else out + term
    out_ref[rows : rows + extra, :] = jnp.where(
        low, out[:extra, :PAIR], out[extra:, PAIR:]
    ).astype(BF16)


def backward_kernel(
    starts,
    x_ref,
    q_ref,
    do_ref,
    kv_ref,
    p_ref,
    pg_ref,
    *rest,
    first,
    row_blocks,
    extra,
    shards,
    parts,
    waits,
):
    seen_refs = rest[:shards]
    dq_ref, dkv_ref, near_ref, away_ref, qsum_ref, vsum_ref, acc = rest[shards + waits :][:7]
    tokens = loader(seen_refs, rest[shards + waits + 7 :])
    core = starts[row_blocks * H * MOVING + 1]
    top = pl.multiple_of(starts[row_blocks * H * MOVING], BLOCK)
    pair = first + pl.program_id(0)
    rows = row_blocks * BLOCK
    low = lax.broadcasted_iota(jnp.int32, (1, PAIR), 1) < HD

    last = slice(rows, rows + extra)
    wide_do = by_head(do_ref[last, :], low, False)
    cuts = [slice(i * rows, (i + 1) * rows) for i in range(shards)]
    dps = [dot_t(kv_ref[here, :], wide_do) for here in cuts]
    terms = [pg_ref[0, here, :].astype(F32) * dp for here, dp in zip(cuts, dps)]
    delta = jnp.sum(reduce(jnp.add, terms), axis=0, keepdims=True)
    rows_in = jnp.concatenate([wide_do, by_head(q_ref[last, :], low, True)], axis=0)
    dq = None
    for here, dp in zip(cuts, dps):
        probs = pg_ref[0, here, :]
        ds = (probs.astype(F32) * (dp - delta)).astype(BF16)
        term = t_dot(ds, kv_ref[here, :])
        dq = term if dq is None else dq + term
        acc[here, :] = dot(jnp.concatenate([probs, ds], axis=1), rows_in)
    dq = jnp.where(low, dq[extra:, PAIR:], dq[:extra, :PAIR]) * FACTOR
    dq_ref[last, :] = dq.astype(BF16)

    def some_blocks(group, carry):
        blocks = [group * TOGETHER + i for i in range(TOGETHER)]
        ats = [pl.ds(pl.multiple_of(block * BLOCK, BLOCK), BLOCK) for block in blocks]
        listed = [
            listed_keys(starts, (block * H + 2 * pair) * MOVING, top, kv_ref) for block in blocks
        ]
        kvs = [kv for kv, _ in listed]
        dos = [by_head(do_ref[at, :], low, False) for at in ats]
        dps = [dot_t(kv, do) for kv, do in zip(kvs, dos)]
        probs = [p_ref[block, 0] for block in blocks]
        dss = []
        for some, dp in zip(probs, dps):
            wide = some.astype(F32)
            dss.append((wide * (dp - jnp.sum(wide * dp, axis=0, keepdims=True))).astype(BF16))
        dqs = [t_dot(ds, kv) for ds, kv in zip(dss, kvs)]
        dkvs = [
            dot(
                jnp.concatenate([some, ds], axis=1),
                jnp.concatenate([do, by_head(q_ref[at, :], low, True)], axis=0),
            )
            for some, ds, do, at in zip(probs, dss, dos, ats)
        ]
        for at, dq in zip(ats, dqs):
            dq = jnp.where(low, dq[BLOCK:, PAIR:], dq[:BLOCK, :PAIR]) * FACTOR
            dq_ref[at, :] = dq.astype(BF16)
        acc[pl.ds(top, GLOB * BLOCK), :] += reduce(jnp.add, [d[: GLOB * BLOCK] for d in dkvs])
        for dkv, (_, places) in zip(dkvs, listed):
            for i in range(MOVING):
                here = dkv[(GLOB + i) * BLOCK : (GLOB + i + 1) * BLOCK]
                if i < 3:
                    acc[pl.ds(places[0][i], BLOCK), :] += here
                else:
                    acc[pl.ds(places[0][i], BLOCK), :PAIR] += here[:, :PAIR]
                    acc[pl.ds(places[1][i], BLOCK), PAIR:] += here[:, PAIR:]
        return carry

    lax.fori_loop(0, row_blocks // TOGETHER, some_blocks, 0)
    dkv_ref[...] = acc[...].astype(BF16)
    total = jnp.sum(acc[...], axis=0, keepdims=True)
    vsum_ref[0] = jnp.where(low, total[:, :PAIR], total[:, PAIR:])
    total = jnp.sum(dq_ref[...].astype(F32), axis=0, keepdims=True)
    qsum_ref[0] = jnp.concatenate([total[:, HD:], total[:, :HD]], axis=1)
    near, away = by_core(t_dot(x_ref[...], dq_ref[...]), core, parts)
    near_ref[:, :PAIR], away_ref[:, :PAIR] = near.astype(BF16), away.astype(BF16)
    total = None
    for i in range(shards):
        term = t_dot(tokens(i), dkv_ref[i * rows : (i + 1) * rows, :])
        total = term if total is None else total + term
    near, away = by_core(total, core, parts)
    near_ref[:, PAIR:], away_ref[:, PAIR:] = near.astype(BF16), away.astype(BF16)


def piece_specs(rows, width, shards):
    if shards > PIECES:
        scratch = [pltpu.VMEM((rows, width), BF16), pltpu.SemaphoreType.DMA]
        return [pl.BlockSpec(memory_space=pl.ANY)] * shards, scratch
    spec = pl.BlockSpec((rows, width), lambda p, *_: (0, 0), pipeline_mode=pl.Buffered(1))
    return [spec] * shards, []


def long_spec(shape, place, shards):
    if shards > PIECES:
        return pl.BlockSpec(shape, place, pipeline_mode=pl.Buffered(1))
    return pl.BlockSpec(shape, place)


def attention_forward(starts, limits, x, pieces, weights, b_qkv, waits, first, count, extra):
    rows, width, shards = x.shape[0], x.shape[1], len(pieces)
    seq = shards * (rows - extra)
    row_blocks = (rows - extra) // BLOCK
    specs, scratch = piece_specs(rows - extra, width, shards)
    return pl.pallas_call(
        partial(
            forward_kernel,
            first=first,
            row_blocks=row_blocks,
            extra=extra,
            shards=shards,
            waits=len(waits),
        ),
        grid_spec=pltpu.PrefetchScalarGridSpec(
            num_scalar_prefetch=2,
            grid=(count,),
            in_specs=[
                pl.BlockSpec((rows, width), lambda p, *_: (0, 0)),
                pl.BlockSpec((width, 3 * PAIR), lambda p, *_: (0, p)),
                pl.BlockSpec((1, 1, 3 * PAIR), lambda p, *_: (first + p, 0, 0)),
            ]
            + specs
            + [pl.BlockSpec(memory_space=pl.ANY)] * len(waits),
            out_specs=[
                pl.BlockSpec((rows, PAIR), lambda p, *_: (0, p)),
                long_spec((seq, 2 * PAIR), lambda p, *_: (0, p), shards),
                pl.BlockSpec((rows, PAIR), lambda p, *_: (0, p)),
                pl.BlockSpec((row_blocks, 1, LISTED, PAIR), lambda p, *_: (0, p, 0, 0)),
                long_spec((1, seq, 2 * extra), lambda p, *_: (p, 0, 0), shards),
            ],
            scratch_shapes=scratch,
        ),
        out_shape=[
            jax.ShapeDtypeStruct((rows, count * PAIR), BF16),
            jax.ShapeDtypeStruct((seq, 2 * count * PAIR), BF16),
            jax.ShapeDtypeStruct((rows, count * PAIR), BF16),
            jax.ShapeDtypeStruct((row_blocks, count, LISTED, PAIR), BF16),
            jax.ShapeDtypeStruct((count, seq, 2 * extra), BF16),
        ],
        compiler_params=pltpu.CompilerParams(vmem_limit_bytes=58 * MIB),
        cost_estimate=taking(10 * count),
        name="attention_forward",
    )(starts, limits, x, weights, b_qkv, *pieces, *waits)


def attention_backward(
    starts, x, pieces, q, do, kv, probs, global_probs, waits, first, offset, count, cost, extra
):
    rows, seq, width, shards = q.shape[0], kv.shape[0], x.shape[1], len(pieces)
    parts = lax.axis_size("wt")
    row_blocks = (rows - extra) // BLOCK
    specs, scratch = piece_specs(rows - extra, width, shards)
    return pl.pallas_call(
        partial(
            backward_kernel,
            first=first,
            row_blocks=row_blocks,
            extra=extra,
            shards=shards,
            parts=parts,
            waits=len(waits),
        ),
        grid_spec=pltpu.PrefetchScalarGridSpec(
            num_scalar_prefetch=1,
            grid=(count,),
            in_specs=[
                pl.BlockSpec((rows, width), lambda p, *_: (0, 0)),
                pl.BlockSpec((rows, PAIR), lambda p, *_: (0, offset + p)),
                pl.BlockSpec((rows, PAIR), lambda p, *_: (0, first + p)),
                long_spec((seq, 2 * PAIR), lambda p, *_: (0, offset + p), shards),
                pl.BlockSpec((row_blocks, 1, LISTED, PAIR), lambda p, *_: (0, offset + p, 0, 0)),
                long_spec((1, seq, 2 * extra), lambda p, *_: (offset + p, 0, 0), shards),
            ]
            + specs
            + [pl.BlockSpec(memory_space=pl.ANY)] * len(waits),
            out_specs=[
                pl.BlockSpec((rows, PAIR), lambda p, *_: (0, p)),
                long_spec((seq, 2 * PAIR), lambda p, *_: (0, p), shards),
                pl.BlockSpec((width // 2, 3 * PAIR), lambda p, *_: (0, p)),
                pl.BlockSpec((width // 2, 3 * PAIR), lambda p, *_: (0, p)),
                pl.BlockSpec((1, 1, PAIR), lambda p, *_: (p, 0, 0)),
                pl.BlockSpec((1, 1, PAIR), lambda p, *_: (p, 0, 0)),
            ],
            scratch_shapes=[pltpu.VMEM((seq, 2 * PAIR), F32), *scratch],
        ),
        out_shape=[
            jax.ShapeDtypeStruct((rows, count * PAIR), BF16),
            jax.ShapeDtypeStruct((seq, 2 * count * PAIR), BF16),
            jax.ShapeDtypeStruct((width // 2, 3 * count * PAIR), BF16),
            jax.ShapeDtypeStruct((width // 2, 3 * count * PAIR), BF16),
            jax.ShapeDtypeStruct((count, 1, PAIR), F32),
            jax.ShapeDtypeStruct((count, 1, PAIR), F32),
        ],
        compiler_params=pltpu.CompilerParams(vmem_limit_bytes=60 * MIB),
        cost_estimate=taking(cost),
        name="attention_backward",
    )(starts, x, q, do, kv, probs, global_probs, *pieces, *waits)


def centered_root(value):
    centered = value - jnp.mean(value, axis=1, keepdims=True)
    root = lax.rsqrt(jnp.mean(centered * centered, axis=1, keepdims=True) + EPSILON)
    return centered * root, root


def norm_back(grad, normed, root):
    mean = jnp.mean(grad, axis=1, keepdims=True)
    return root * (grad - mean - normed * jnp.mean(grad * normed, axis=1, keepdims=True))


def both_pieces(ref, core, columns):
    half = ref.shape[3] // 2
    pieces = []
    for piece in (core, 1 - core):
        blocks = [ref[piece, part] for part in range(ref.shape[1])]
        if columns:
            blocks = [b for block in blocks for b in (block[:, :half], block[:, half:])]
        pieces.append(jnp.concatenate(blocks, axis=0))
    return jnp.concatenate(pieces, axis=1 if columns else 0)


def layer_kernel(
    me,
    x_ref,
    att0_ref,
    att1_ref,
    cot_ref,
    keep_ref,
    wo_ref,
    we_ref,
    wc_ref,
    be_ref,
    vec_ref,
    out_ref,
    one_ref,
    do_ref,
    wok_ref,
    woa_ref,
    ck_ref,
    ca_ref,
    ek_ref,
    ea_ref,
    beg_ref,
    vecg_ref,
    norm_ref,
    root_ref,
    low_ref,
    slope_ref,
    hid_ref,
    acc_ref,
    two_ref,
):
    step = pl.program_id(0)
    core = me[0] % 2
    row = lambda i: vec_ref[i : i + 1, :]

    @pl.when(step == 0)
    def _():
        cut = att0_ref.shape[1]
        branch = dot(att0_ref[...], wo_ref[:cut]) + dot(att1_ref[...], wo_ref[cut:])
        normed, root = centered_root(x_ref[...].astype(F32) + branch + row(0))
        norm_ref[...] = normed
        root_ref[...] = root
        normed = normed * row(1) + row(2)
        low_ref[...] = normed.astype(BF16)
        acc_ref[...] = normed + row(3)

    @pl.when(step < 4)
    def _():
        bias = jnp.concatenate([be_ref[core], be_ref[1 - core]], axis=1)
        u = dot(low_ref[...], both_pieces(we_ref, core, True)) + bias
        square = u * u
        t = jnp.tanh(SLOPE * u * (1.0 + CUBIC * square))
        half = 0.5 * (1.0 + t)
        hidden = (u * half).astype(BF16)
        slope_ref[step] = half + (0.5 * SLOPE) * u * (1.0 - t * t) * (
            1.0 + (3.0 * CUBIC) * square
        )
        hid_ref[step] = hidden
        acc_ref[...] += dot(hidden, both_pieces(wc_ref, core, False))

    @pl.when(step == 4)
    def _():
        normed, root = centered_root(acc_ref[...])
        out_ref[...] = (keep_ref[...] * (normed * row(4) + row(5))).astype(BF16)
        cot = cot_ref[...].astype(F32)
        vecg_ref[4:5, :] = jnp.sum(cot * normed, axis=0, keepdims=True)
        vecg_ref[5:6, :] = jnp.sum(cot, axis=0, keepdims=True)
        two = norm_back(cot * row(4), normed, root)
        acc_ref[...] = two
        two = two.astype(BF16)
        two_ref[...] = two
        vecg_ref[3:4, :] = jnp.sum(two.astype(F32), axis=0, keepdims=True)

    @pl.when(step >= 4)
    def _():
        at = step - 4
        piece = ck_ref.shape[1]
        grad = t_dot(hid_ref[at], two_ref[...]).astype(BF16)
        ck_ref[0], ca_ref[0] = grad[:piece], grad[piece:]
        grad = dot_t(two_ref[...], both_pieces(wc_ref, core, False)) * slope_ref[at]
        grad = grad.astype(BF16)
        total = jnp.sum(grad.astype(F32), axis=0, keepdims=True)
        beg_ref[core], beg_ref[1 - core] = total[:, :piece], total[:, piece:]
        acc_ref[...] += dot_t(grad, both_pieces(we_ref, core, True))
        grad = t_dot(low_ref[...], grad).astype(BF16)
        ek_ref[0], ea_ref[0] = grad[:, :piece], grad[:, piece:]

    @pl.when(step == 7)
    def _():
        first = acc_ref[...]
        normed = norm_ref[...]
        vecg_ref[1:2, :] = jnp.sum(first * normed, axis=0, keepdims=True)
        vecg_ref[2:3, :] = jnp.sum(first, axis=0, keepdims=True)
        one = norm_back(first * row(1), normed, root_ref[...])
        one_ref[...] = one
        one = one.astype(BF16)
        vecg_ref[0:1, :] = jnp.sum(one.astype(F32), axis=0, keepdims=True)
        vecg_ref[6:8, :] = jnp.zeros((2, one.shape[1]), F32)
        grad = [t_dot(att_ref[...], one) for att_ref in (att0_ref, att1_ref)]
        near, away = by_core(jnp.concatenate(grad, axis=0), core, we_ref.shape[1])
        wok_ref[...], woa_ref[...] = near.astype(BF16), away.astype(BF16)
        do_ref[...] = dot_t(one, wo_ref[...]).astype(BF16)


def layer(c, x, attended, cot, keep, w_output, w_hidden, b_expand, vectors):
    rows, width = x.shape
    parts, piece = w_hidden.shape[1], b_expand.shape[2]
    each = piece // parts
    steps = PIECES // 2
    whole = lambda *shape: pl.BlockSpec(shape, lambda s, me: (0,) * len(shape))
    chip = lambda s, me: (s % steps) ^ ((me[0] % PIECES) // 2)
    sent = lambda *shape: pl.BlockSpec((1, *shape), lambda s, me: (jnp.maximum(s - steps, 0), 0, 0))
    return pl.pallas_call(
        layer_kernel,
        grid_spec=pltpu.PrefetchScalarGridSpec(
            num_scalar_prefetch=1,
            grid=(2 * steps,),
            in_specs=[
                whole(rows, width),
                *[whole(*a.shape) for a in attended],
                whole(rows, width),
                whole(rows, 1),
                whole(width, width),
                pl.BlockSpec((2, parts, each, width), lambda s, me: (chip(s, me), 0, 0, 0)),
                pl.BlockSpec((2, parts, each, width), lambda s, me: (chip(s, me), 0, 1, 0)),
                pl.BlockSpec((2, 1, piece), lambda s, me: (chip(s, me), 0, 0)),
                whole(8, width),
            ],
            out_specs=[
                whole(rows, width),
                whole(rows, width),
                whole(rows, width),
                whole(width // 2, width),
                whole(width // 2, width),
                sent(piece, width),
                sent(piece, width),
                sent(width, piece),
                sent(width, piece),
                pl.BlockSpec((2, 1, piece), lambda s, me: (chip(jnp.maximum(s - steps, 0), me), 0, 0)),
                whole(8, width),
            ],
            scratch_shapes=[
                pltpu.VMEM((rows, width), F32),
                pltpu.VMEM((rows, 1), F32),
                pltpu.VMEM((rows, width), BF16),
                pltpu.VMEM((steps, rows, 2 * piece), F32),
                pltpu.VMEM((steps, rows, 2 * piece), BF16),
                pltpu.VMEM((rows, width), F32),
                pltpu.VMEM((rows, width), BF16),
            ],
        ),
        out_shape=[
            jax.ShapeDtypeStruct((rows, width), BF16),
            jax.ShapeDtypeStruct((rows, width), F32),
            jax.ShapeDtypeStruct((rows, width), BF16),
            jax.ShapeDtypeStruct((width // 2, width), BF16),
            jax.ShapeDtypeStruct((width // 2, width), BF16),
            jax.ShapeDtypeStruct((steps, piece, width), BF16),
            jax.ShapeDtypeStruct((steps, piece, width), BF16),
            jax.ShapeDtypeStruct((steps, width, piece), BF16),
            jax.ShapeDtypeStruct((steps, width, piece), BF16),
            jax.ShapeDtypeStruct((PIECES, 1, piece), F32),
            jax.ShapeDtypeStruct((8, width), F32),
        ],
        compiler_params=pltpu.CompilerParams(vmem_limit_bytes=58 * MIB),
        cost_estimate=taking(35),
        name="layer",
    )(
        jnp.reshape(c, (1,)).astype(jnp.int32),
        x,
        *attended,
        cot,
        keep,
        w_output,
        w_hidden,
        w_hidden,
        b_expand,
        vectors,
    )


def pair_sum(grad_refs, weight_refs, columns, at):
    grads = jnp.concatenate([ref[...] for ref in grad_refs], axis=1)
    weights = []
    for group, offset, count in BACK:
        for pair in range(offset, offset + count):
            start = 3 * PAIR * pair + at
            weights.append(weight_refs[group][:, start : start + columns])
    return dot_t(grads, jnp.concatenate(weights, axis=1))


def token_kernel(me, *refs, away, extra, count):
    sides = len(BACK)
    dkv_refs, w_refs = refs[:sides], refs[sides : sides + 2]
    c, step = me[0], pl.program_id(0)
    piece = 2 * step + (1 if away else 0)
    half = dkv_refs[0].shape[0] // 2
    if away:
        dq_refs, one_ref = refs[sides + 2 : 2 * sides + 2], refs[2 * sides + 2]
        out_ref, share_ref = refs[-2:]

        @pl.when(step == 0)
        def _():
            share_ref[...] = one_ref[...] + pair_sum(dq_refs, w_refs, PAIR, 0)

        share = lambda: share_ref[2 * half : 2 * half + extra, :]
    else:
        share_ref, out_ref = refs[sides + 2], refs[-1]
        share = lambda: share_ref[...]
    total = pair_sum(dkv_refs, w_refs, 2 * PAIR, PAIR).astype(BF16)
    out_ref[0, 0], out_ref[1, 0] = total[:half], total[half:]

    @pl.when((piece == c) & (c < count))
    def _():
        at = pl.ds(pl.multiple_of(c * extra, extra), extra)
        out_ref[0, 0, at, :] = (out_ref[0, 0, at, :].astype(F32) + share()).astype(BF16)


def token_share(c, dkvs, weights, more, away, waits, rows, extra, count):
    seq, width = dkvs[0].shape[0], weights[0].shape[0]
    chips = seq // rows // 2
    other = 1 if away else 0
    full = lambda a: pl.BlockSpec(a.shape, lambda j, me: (0,) * a.ndim)
    out_specs = [pl.BlockSpec((2, 1, rows // 2, width), lambda j, me: (0, j, 0, 0))]
    out_shape = [jax.ShapeDtypeStruct((2, chips, rows // 2, width), BF16)]
    if away:
        out_specs.append(pl.BlockSpec((rows + extra, width), lambda j, me: (0, 0)))
        out_shape.append(jax.ShapeDtypeStruct((rows + extra, width), F32))
    return pl.pallas_call(
        partial(token_kernel, away=away, extra=extra, count=count),
        grid_spec=pltpu.PrefetchScalarGridSpec(
            num_scalar_prefetch=1,
            grid=(chips,),
            in_specs=[
                pl.BlockSpec((rows, a.shape[1]), lambda j, me: (2 * j + other, 0))
                for a in dkvs
            ]
            + [full(a) for a in (*weights, *more)]
            + [pl.BlockSpec(memory_space=pl.ANY)] * len(waits),
            out_specs=out_specs,
        ),
        out_shape=out_shape,
        compiler_params=pltpu.CompilerParams(vmem_limit_bytes=48 * MIB),
        cost_estimate=taking(0.5),
        name="token_share",
    )(jnp.reshape(c, (1,)).astype(jnp.int32), *dkvs, *weights, *more, *waits)


def by_pair(queries, keys, values):
    count = queries.shape[0]
    together = [a.reshape(count, PAIRS, PAIR) for a in (queries, keys, values)]
    together = jnp.concatenate(together, axis=2).reshape(count * PAIRS, 3 * PAIR)
    places = jnp.arange(3 * PAIR, dtype=jnp.int32)
    source = jnp.array((1, 0, 4, 2, 3, 5), jnp.int32)[places // HD] * HD + places % HD
    return ordered(together, source).astype(BF16).reshape(count, PAIRS * 3 * PAIR)


def column_places(pairs):
    start = jnp.arange(pairs, dtype=jnp.int32)[:, None, None] * (3 * PAIR)
    inner = jnp.arange(HD, dtype=jnp.int32)
    for spots in ((1, 0), (3, 4), (2, 5)):
        yield (start + jnp.array(spots, jnp.int32)[:, None] * HD + inner).reshape(-1)


def swapped(value, bit):
    shards = lax.axis_size("ctx")
    return lax.ppermute(value, "ctx", [(i, i ^ bit) for i in range(shards)])


def own_bit(bit):
    return (lax.axis_index("ctx") // bit) % 2


def added(keep, came):
    return (keep.astype(F32) + came.astype(F32)).astype(BF16)


def halved(value, axis, bit):
    mine = own_bit(bit)
    away = lax.dynamic_index_in_dim(value, 1 - mine, axis, keepdims=False)
    keep = lax.dynamic_index_in_dim(value, mine, axis, keepdims=False)
    return added(keep, swapped(away, bit))


def doubled(value, bit):
    other = swapped(value, bit)
    mine = own_bit(bit) == 0
    return jnp.stack([jnp.where(mine, value, other), jnp.where(mine, other, value)])


def plane_gather(value):
    value = value[None]
    for bit in (1, 2, 4):
        value = doubled(value, bit)
        value = value.reshape(-1, *value.shape[2:])
    return value


def line_step(value, bit):
    parts = lax.axis_size("wt")
    other = lax.ppermute(value, "wt", [(i, i ^ bit) for i in range(parts)])
    mine = lax.axis_index("wt") // bit % 2 == 0
    return jnp.concatenate([jnp.where(mine, value, other), jnp.where(mine, other, value)])


def line_gather(value, bit=1):
    while bit < lax.axis_size("wt"):
        value = line_step(value, bit)
        bit *= 2
    return value


def token_gather(own):
    shards, half = lax.axis_size("ctx"), own.shape[0] // 2
    along_x, along_y = swapped(own, 2), swapped(own, 4)
    far = jnp.concatenate([swapped(along_y[:half], 2), swapped(along_x[half:], 4)], axis=0)
    pieces = []
    for piece in (own, along_x, along_y, far):
        pieces += [piece, swapped(piece, 1)]
    bit = PIECES
    while bit < shards:
        pieces += [swapped(piece, bit) for piece in pieces]
        bit *= 2
    return pieces


def far_sum(value, shards):
    if shards == PIECES:
        return value
    return lax.psum(value, "ctx", axis_index_groups=across_groups(shards))


def same_core(shards, block):
    return [list(range(s + k, s + block, 2)) for s in range(0, shards, block) for k in range(2)]


def rows_start(near, came):
    parts, columns = lax.axis_size("wt"), near.shape[1]
    near, came = (a.reshape(parts, PIECES // 2, -1, columns) for a in (near, came))
    return jnp.transpose(added(near, came), (1, 0, 2, 3)).reshape(parts * PIECES // 2, -1, columns)


def rows_send(sums):
    shards, parts = lax.axis_size("ctx"), lax.axis_size("wt")
    sums = far_sum(sums, shards)
    groups = [[i * parts + w for i in g for w in range(parts)] for g in same_core(shards, PIECES)]
    return lax.all_to_all(
        sums, ("ctx", "wt"), split_axis=0, concat_axis=0, axis_index_groups=groups, tiled=True
    )


def rows_add(sums):
    return jnp.sum(sums.astype(F32), axis=0).astype(BF16)


def rows_sum(sums):
    return rows_add(rows_send(sums))


def ordered(value, source):
    rows = jnp.arange(value.shape[1], dtype=jnp.int32)
    return dot(value, (rows[:, None] == source[None, :]).astype(BF16))


def start_kernel(me, q_ref, k_ref, v_ref, o_ref, e_ref, c_ref, *rest, parts):
    vectors, (lead_ref, more_ref) = rest[:-2], rest[-2:]
    c = me[0]
    half, width = lead_ref.shape[0] - 8, lead_ref.shape[1]
    piece = c % PIECES
    own = pl.ds(pl.multiple_of(c % 2 * half, 16), half)
    low = lax.broadcasted_iota(jnp.int32, (1, PAIR), 1) < HD
    flip = lambda a: jnp.concatenate([a[:, HD:], a[:, :HD]], axis=1)
    columns = []
    for pair in range(PAIRS):
        at = slice(pair * PAIR, (pair + 1) * PAIR)
        q, k, v = (ref[own, at].astype(F32) for ref in (q_ref, k_ref, v_ref))
        k = flip(k)
        columns += [flip(q), jnp.where(low, v, k), jnp.where(low, k, v)]
    ahead = 3 * AHEAD
    small = [r[...].astype(F32).reshape(1, -1) for r in vectors]
    some = [jnp.concatenate(small[i : i + parts], axis=1) for i in range(0, 2 * parts, parts)]
    some += small[2 * parts :]
    small = jnp.concatenate(some + [jnp.zeros((8 - len(some), width), F32)], axis=0)
    lead = jnp.concatenate([jnp.concatenate(columns[:ahead], axis=1), small], axis=0)
    lead_ref[...] = lead.astype(BF16)

    run = e_ref.shape[1] // parts // PIECES
    block = e_ref.shape[1] // parts
    runs = []
    for part in range(parts):
        here = e_ref[:, part * block : (part + 1) * block].astype(F32)
        runs.append(pltpu.roll(here, block - piece * run, 1)[:, :run])
    runs = jnp.concatenate(runs, axis=1)
    count = runs.shape[0] // 2
    more_ref[:count] = jnp.concatenate([runs[:count], runs[count:]], axis=1).astype(BF16)
    rows = c_ref.shape[0] // PIECES
    more_ref[count : count + rows] = c_ref[pl.ds(pl.multiple_of(piece * rows, 16), rows), :]
    at = count + rows
    rows = o_ref.shape[0] // PIECES
    whole = o_ref[...].astype(F32)
    turned = pltpu.roll(whole, whole.shape[0] - piece * rows, 0)
    rows = -(-rows // 16) * 16
    more_ref[at : at + rows] = turned[:rows].astype(BF16)
    at += rows
    left = (PAIRS - AHEAD) * 3 * PAIR // width
    for i in range(left):
        some = columns[ahead + i * width // PAIR : ahead + (i + 1) * width // PAIR]
        some = jnp.concatenate(some, axis=1)
        some = jnp.where(c // (2 << i) % 2 == 0, some[: half // 2], some[half // 2 :])
        more_ref[at : at + half // 2] = some.astype(BF16)
        at += half // 2


def start_arrays(c, weights, vectors, parts):
    half, width = weights[0].shape[0] // 2, weights[0].shape[1]
    count = weights[4].shape[0] // 2 + weights[5].shape[0] // PIECES
    count += (PAIRS - AHEAD) * 3 * PAIR // width * half // 2
    count += -(-weights[3].shape[0] // PIECES // 16) * 16
    full = lambda shape: pl.BlockSpec(shape, lambda i: (0,) * len(shape))
    shapes = [(half + 8, width), (count, width)]
    return pl.pallas_call(
        partial(start_kernel, parts=parts),
        grid=(1,),
        in_specs=[pl.BlockSpec(memory_space=pltpu.SMEM)] + [full(a.shape) for a in (*weights, *vectors)],
        out_specs=[full(shape) for shape in shapes],
        out_shape=[jax.ShapeDtypeStruct(shape, BF16) for shape in shapes],
        compiler_params=pltpu.CompilerParams(vmem_limit_bytes=60 * MIB),
        cost_estimate=taking(3),
        name="start_arrays",
    )(jnp.reshape(c, (1,)).astype(jnp.int32), *weights, *vectors)


def vector_kernel(*refs, parts):
    sides = len(BACK)
    joined = lambda some: jnp.concatenate([r[i] for r in some for i in range(r.shape[0])], axis=1)
    grads_ref, expand_ref, _, out_ref = refs[2 * sides :]
    rows = [joined(refs[:sides]), joined(refs[sides : 2 * sides])]
    rows += [grads_ref[i : i + 1, :] for i in (0, 3, 1, 2, 4, 5)]
    width = out_ref.shape[1]
    share, run = width // parts, expand_ref.shape[2] // parts
    out = []
    for part in range(parts):
        cuts = [row[:, part * share : (part + 1) * share] for row in rows]
        out += [jnp.concatenate(cuts[i : i + parts], axis=1) for i in range(0, len(cuts), parts)]
        cuts = [expand_ref[p, :, part * run : (part + 1) * run] for p in range(PIECES)]
        out.append(jnp.concatenate(cuts, axis=1))
        out.append(jnp.zeros((PIECES - len(rows) // parts - 1, width), F32))
    out_ref[...] = jnp.concatenate(out, axis=0).astype(BF16)


def vector_rows(q_sums, v_sums, grads, expand_grads, wait, parts):
    return pl.pallas_call(
        partial(vector_kernel, parts=parts),
        in_specs=[pl.BlockSpec(memory_space=pltpu.VMEM)] * (2 * len(BACK) + 2)
        + [pl.BlockSpec(memory_space=pl.ANY)],
        out_shape=jax.ShapeDtypeStruct((parts * PIECES, grads.shape[1]), BF16),
        cost_estimate=taking(1),
        name="vector_rows",
    )(*q_sums, *v_sums, grads, expand_grads, wait)


def expand_kernel(in_ref, out_ref):
    pieces, half, run = in_ref.shape[0], in_ref.shape[1], in_ref.shape[2] // 2
    parts = out_ref.shape[1] // in_ref.shape[2]
    count = run // parts
    for lower in range(2):
        for part in range(parts):
            at = lower * run + part * count
            runs = [in_ref[p, :, at : at + count].astype(F32) for p in range(pieces)]
            out_ref[
                lower * half : (lower + 1) * half, part * 2 * run : (part + 1) * 2 * run
            ] = jnp.concatenate(runs, axis=1)


def expand_columns(gathered, each_piece, parts):
    width = gathered.shape[2]
    return pl.pallas_call(
        expand_kernel,
        grid=(1,),
        in_specs=[pl.BlockSpec((PIECES, each_piece, width), lambda i: (0, 1, 0))],
        out_specs=pl.BlockSpec((2 * each_piece, parts * width), lambda i: (0, 0)),
        out_shape=jax.ShapeDtypeStruct((2 * each_piece, parts * width), F32),
        compiler_params=pltpu.CompilerParams(vmem_limit_bytes=24 * MIB),
        cost_estimate=taking(2),
        name="expand_columns",
    )(gathered)


def body(
    tokens,
    cotangent,
    lengths,
    rand_blocks,
    query_weight,
    key_weight,
    value_weight,
    output_weight,
    expand_weight,
    contract_weight,
    query_bias,
    value_bias,
    output_bias,
    expand_bias,
    contract_bias,
    attn_gain,
    attn_shift,
    ffn_gain,
    ffn_shift,
):
    shards = lax.axis_size("ctx")
    parts = lax.axis_size("wt")
    c = lax.axis_index("ctx")
    rows, width = tokens.shape[1], tokens.shape[2]
    row_blocks = rows // BLOCK
    seq = shards * rows
    global_count = GLOB * BLOCK
    extra = 16 * (-(-global_count // (16 * shards)))
    hidden_width = expand_weight.shape[1]
    part = expand_weight.shape[0]
    piece = hidden_width // PIECES
    length = lengths[0]
    inputs = tokens[0]

    pieces = token_gather(inputs)
    half = part // 2
    leading, behind = start_arrays(
        c,
        (query_weight, key_weight, value_weight, output_weight, expand_weight, contract_weight),
        (
            query_bias,
            value_bias,
            output_bias,
            contract_bias,
            attn_gain,
            attn_shift,
            ffn_gain,
            ffn_shift,
            expand_bias,
        ),
        parts,
    )
    early_lead = line_step(leading[None], 1)
    leading = line_gather(after(early_lead, pieces[2], pieces[4]), 2)
    vectors = leading[:, half:].reshape(parts, -1)
    leading = leading[:, :half]

    def joined(bundle):
        return jnp.transpose(doubled(bundle, 1), (1, 0, 2, 3)).reshape(width, -1)

    weights = [joined(leading)]
    each = width // parts
    b_query, b_value, b_output, b_contract, g_attn, s_attn, g_ffn, s_ffn = (
        vectors[:, i * each : (i + 1) * each].reshape(-1).astype(F32) for i in range(8)
    )
    b_expand = vectors[:, 8 * each : 8 * each + hidden_width // parts].reshape(parts, PIECES, -1)
    b_expand = jnp.transpose(b_expand, (1, 0, 2)).reshape(PIECES, 1, piece).astype(F32)

    each_piece = piece // parts
    o_rows = part // PIECES
    mixed = 2 * each_piece
    w_hidden = lax.all_gather(behind, "wt")
    mixed += -(-o_rows // 16) * 16
    following = w_hidden[:, mixed:].reshape(parts, 2, half // 2, width)
    following = [
        jnp.transpose(doubled(following[:, i], 2 << i), (1, 0, 2, 3)).reshape(parts, half, width)
        for i in range(2)
    ]
    following = jnp.concatenate(following, axis=2)
    w_hidden = w_hidden[:, :mixed]

    start = jnp.minimum(c * extra, global_count - extra)
    more = lax.dynamic_slice_in_dim(pieces[0], start, extra, 0)
    for i in range(1, shards):
        other = lax.dynamic_slice_in_dim(pieces[i], start, extra, 0)
        more = jnp.where(c == i, other, more)
    x = jnp.concatenate([inputs, more], axis=0)
    index = jnp.arange(rows + extra, dtype=jnp.int32)
    position = jnp.where(index < rows, c * rows + index, c * extra + index - rows)
    is_global = position < global_count
    usable = ((position < length) & (is_global == (index >= rows)))[:, None]
    own = c * row_blocks + jnp.arange(row_blocks, dtype=jnp.int32)
    beside = own[:, None, None] + jnp.arange(-1, 2, dtype=jnp.int32)
    listed = jnp.concatenate(
        [jnp.broadcast_to(beside, (row_blocks, H, 3)), rand_blocks[0]], axis=2
    )
    blocks = seq // BLOCK
    inside = (listed >= 0) & (listed < blocks)
    listed = jnp.clip(listed, 0, blocks - 1)
    limits = jnp.where(inside, length - listed * BLOCK, 0).reshape(-1)
    order = jnp.arange(shards, dtype=jnp.int32) ^ c
    limits = jnp.concatenate([limits, length - order * rows])
    starts = (listed // row_blocks ^ c) * rows + listed % row_blocks * BLOCK
    starts = jnp.concatenate([starts.reshape(-1), jnp.stack([c * rows, c % 2])])

    given = jnp.where(c == 0, cotangent[0, :global_count], jnp.zeros((), BF16))
    given = jnp.pad(given, ((0, shards * extra - global_count), (0, 0)))
    given = after(given.reshape(shards, extra, width), pieces[4])
    given = lax.all_to_all(given, "ctx", split_axis=0, concat_axis=0, tiled=True)
    cot = jnp.concatenate([cotangent[0], given[0]], axis=0)
    cot = jnp.where(usable, cot, jnp.zeros((), BF16))

    b_qkv = by_pair(*(b.astype(BF16)[None] for b in (b_query, jnp.zeros_like(b_value), b_value)))
    b_qkv = b_qkv.astype(F32).reshape(PAIRS, 1, 3 * PAIR)
    zero = jnp.zeros_like(b_output)
    vectors = jnp.stack([b_output, g_attn, s_attn, b_contract, g_ffn, s_ffn, zero, zero])
    keep = usable.astype(F32)
    w_hidden = after(
        w_hidden, *pieces[:PIECES:2], leading, cot, starts, limits, b_qkv, vectors, b_expand, keep
    )
    w_hidden = lax.all_gather(w_hidden, "ctx", axis_index_groups=groups_of(shards))
    w_output = w_hidden[:, :, 2 * each_piece : 2 * each_piece + o_rows]
    w_output = jnp.transpose(w_output, (1, 0, 2, 3)).reshape(width, width)
    forward = partial(attention_forward, starts, limits, x, pieces)
    kept = [forward(weights[0], b_qkv, (cot,), *GROUPS[0], extra)]
    weights.append(joined(following))
    kept.append(forward(weights[1], b_qkv, (), *GROUPS[1], extra))

    (
        layer_out,
        grad_one,
        grad_attended,
        o_keep,
        o_away,
        c_keep,
        c_away,
        e_keep,
        e_away,
        expand_bgrad,
        vector_grads,
    ) = layer(
        c,
        x,
        [k[2] for k in kept],
        cot,
        keep,
        w_output,
        w_hidden,
        b_expand,
        vectors,
    )

    def attention_back(side, *waits):
        group, offset, count = BACK[side]
        q, kv, _, probs, global_probs = kept[group]
        first = GROUPS[group][0] + offset
        return attention_backward(
            starts,
            x,
            pieces,
            q,
            grad_attended,
            kv,
            probs,
            global_probs,
            waits,
            first,
            offset,
            count,
            BACK_COST[side],
            extra,
        )

    c_came, e_came = swapped(c_away, 1), swapped(e_away, 1)
    early = [rows_start(o_keep, swapped(o_away, 1))]
    backs = [attention_back(0)]
    steps = PIECES // 2
    c_keep, c_came = (a.reshape(2, 2, piece, width) for a in (c_keep, c_came))
    e_keep, e_came = (a.reshape(2, 2, width, piece) for a in (e_keep, e_came))
    c_away = added(c_keep[:, 1], c_came[:, 1])
    e_away = added(e_keep[1], e_came[1])
    c_came_on, e_came_on = swapped(c_away, 2), swapped(e_away, 4)
    c_keep = added(c_keep[:, 0], c_came[:, 0])
    e_keep = added(e_keep[0], e_came[0])

    early.append(rows_start(backs[0][2], swapped(backs[0][3], 1)))
    early = jnp.concatenate(early, axis=1)
    backs.append(attention_back(1, c_away, e_away, early))
    early = rows_sum(early)
    c_away, e_away = added(c_keep[1], c_came_on[1]), added(e_keep[1], e_came_on[1])
    c_last, e_last = swapped(c_away, 4), swapped(e_away, 2)
    c_keep, e_keep = added(c_keep[0], c_came_on[0]), added(e_keep[0], e_came_on[0])

    middle = rows_start(backs[1][2], swapped(backs[1][3], 1))
    backs.append(attention_back(2, c_away, e_away, early, middle))
    middle = rows_sum(middle)
    c_mine = far_sum(added(c_keep, c_last), shards).reshape(parts, -1, width)
    e_mine = far_sum(added(e_keep, e_last), shards).reshape(parts, 2, -1, piece)
    e_mine = jnp.concatenate([e_mine[:, 0], e_mine[:, 1]], axis=2)
    hidden_sums = jnp.concatenate([c_mine, e_mine], axis=1)
    both = lax.all_to_all(hidden_sums, "wt", split_axis=0, concat_axis=0, tiled=True)
    backs.append(attention_back(3, hidden_sums, middle))

    small = vector_rows([b[4] for b in backs], [b[5] for b in backs], vector_grads, expand_bgrad, backs[3][0], parts)
    small = small.reshape(parts, 2, -1, width)
    near = jnp.concatenate([backs[2][2], backs[3][2]], axis=1).reshape(parts, PIECES // 2, -1, width)
    near = jnp.concatenate(
        [near, lax.dynamic_index_in_dim(small, own_bit(1), 1, keepdims=False)[:, :, None]], axis=2
    )
    far = jnp.concatenate([backs[2][3], backs[3][3]], axis=1).reshape(parts, PIECES // 2, -1, width)
    far = jnp.concatenate(
        [far, lax.dynamic_index_in_dim(small, 1 - own_bit(1), 1, keepdims=False)[:, :, None]], axis=2
    )
    late = rows_start(near.reshape(-1, width), swapped(far, 1))

    share = partial(token_share, c, [b[1] for b in backs], weights)
    count = global_count // extra
    away, own = share(
        [b[0] for b in backs] + [grad_one], True, (late,), rows, extra, count
    )
    both = jnp.sum(after(both, away).astype(F32), axis=0).astype(BF16)
    both = jnp.concatenate([both, early, middle, layer_out[rows:]], axis=0)
    (keep,) = share([own[rows:]], False, (away, both, late), rows, extra, count)
    late = rows_send(late)
    came = swapped(away, 1)
    chips = shards // 2
    if chips > 4:
        keep = added(keep, came)
        while chips > 4:
            keep = added(keep[:, : chips // 2], swapped(keep[:, chips // 2 :], chips))
            chips //= 2
        came = jnp.zeros_like(keep)
    keep, came = (a.reshape(2, 2, 2, rows // 2, width) for a in (keep, came))
    above, below = (keep[0], came[0]), (keep[1], came[1])
    above_sent = added(above[0][:, 1], above[1][:, 1])
    below_sent = added(below[0][1], below[1][1])
    late = rows_add(after(late, above_sent, below_sent))
    above_came, below_came = swapped(above_sent, 2), swapped(below_sent, 4)
    above = added(above[0][:, 0], above[1][:, 0])
    below = added(below[0][0], below[1][0])
    rows_late = late.shape[0]
    late = jnp.pad(late, ((0, -rows_late % 8), (0, 0)))
    late = doubled(late, 1)
    late = doubled(late, 2).reshape(4, -1, width)

    def carried(sent, more, bit):
        count = sent.shape[0]
        flat = swapped(jnp.concatenate([sent, more.reshape(-1, width)], axis=0), bit)
        other = flat[count:].reshape(more.shape)
        mine = own_bit(bit) == 0
        more = jnp.concatenate([jnp.where(mine, more, other), jnp.where(mine, other, more)])
        return flat[:count], more

    hidden_rows = 2 * each_piece
    gathered = lax.all_gather(both, "ctx", axis_index_groups=groups_of(shards))

    contract_wgrad = gathered[:, :each_piece].reshape(-1, width).astype(F32)
    expand_wgrad = expand_columns(gathered, each_piece, parts)
    finished = gathered[:, -extra:].reshape(-1, width)
    on_first = (c == 0) & (index[:rows] < global_count)
    finished = jnp.pad(finished[:global_count], ((0, rows - global_count), (0, 0)))
    layer_out = jnp.where(on_first[:, None], finished, layer_out[:rows])

    above_came = after(above_came, contract_wgrad, expand_wgrad, layer_out)
    below_came = after(below_came, contract_wgrad, expand_wgrad, layer_out)

    above_sent = added(above[1], above_came[1])
    below_sent = added(below[1], below_came[1])
    above_last, late = carried(above_sent, late, 4)
    below_last = swapped(below_sent, 2)
    late = late[:, : rows_late]
    above = above[0].astype(F32) + above_came[0].astype(F32) + above_last.astype(F32)
    below = below[0].astype(F32) + below_came[0].astype(F32) + below_last.astype(F32)
    input_grad = own[:rows] + jnp.concatenate([above, below], axis=0)

    kinds = [gathered[:, hidden_rows:-extra].reshape(PIECES, 3, -1, width)]
    kinds.append(late[:, None, :-1])
    mine = jnp.concatenate(kinds, axis=1).reshape(PIECES // 2, 2, 4, -1, width)
    mine = jnp.transpose(mine, (2, 1, 0, 3, 4)).reshape(4, part, width)
    small = jnp.transpose(late[:, -1].reshape(PIECES // 2, 2, width), (1, 0, 2)).reshape(-1, width)
    small = small.astype(F32)
    small_grads = [small[i // parts, i % parts * each :][:each] for i in range(8)]
    expand_bias_grad = small[2]
    output_wgrad = mine[0].astype(F32)
    query_wgrad, key_wgrad, value_wgrad = (
        jnp.concatenate([ordered(g, places) for g in (mine[1], mine[2], mine[3])], axis=1)
        for places in column_places(AHEAD)
    )

    return (
        layer_out[None],
        input_grad[None],
        query_wgrad,
        key_wgrad,
        value_wgrad,
        output_wgrad,
        expand_wgrad,
        contract_wgrad,
        small_grads[0],
        small_grads[1],
        small_grads[2],
        expand_bias_grad,
        small_grads[3],
        small_grads[4],
        small_grads[5],
        small_grads[6],
        small_grads[7],
    )


def solution(mesh):
    tokens, weight, vector = P("wt", "ctx", None), P("wt", None), P("wt")
    return jax.shard_map(
        body,
        mesh=mesh,
        in_specs=(tokens, tokens, vector, P("wt", "ctx", None, None)) + (weight,) * 6 + (vector,) * 9,
        out_specs=(tokens, tokens) + (weight,) * 6 + (vector,) * 9,
        check_vma=False,
    )
```

```python
from functools import partial, reduce

import jax
import jax.numpy as jnp
from jax import lax
from jax.experimental import pallas as pl
from jax.experimental.pallas import tpu as pltpu
from jax.sharding import PartitionSpec as P

H = 12
HD = 64
BLOCK = 64
GLOB = 2
RAND = 3
PAIR = 2 * HD
PAIRS = H // 2
AHEAD = 2
GROUPS = ((0, AHEAD), (AHEAD, PAIRS - AHEAD))
BACK = ((0, 0, 2), (1, 0, 2), (1, 2, 1), (1, 3, 1))
BACK_COST = (8, 8, 8, 20)
MOVING = 3 + RAND
TOGETHER = 8
LISTED = (GLOB + MOVING) * BLOCK
PIECES = 8
NEGATIVE = -1e30
EPSILON = 1e-12
FACTOR = HD ** (-0.5)
SLOPE = (2.0 / jnp.pi) ** 0.5
CUBIC = 0.044715
F32 = jnp.float32
BF16 = jnp.bfloat16
MIB = 2**20


def taking(microseconds):
    return pl.CostEstimate(
        flops=int(microseconds * 10**9), bytes_accessed=10**6, transcendentals=0
    )


def groups_of(shards):
    return [list(range(s, s + PIECES)) for s in range(0, shards, PIECES)]


def across_groups(shards):
    return [list(range(s, shards, PIECES)) for s in range(PIECES)]


def dot(a, b):
    return jnp.dot(a, b, preferred_element_type=F32)


def dot_t(a, b):
    return lax.dot_general(a, b, (((1,), (1,)), ((), ())), preferred_element_type=F32)


def t_dot(a, b):
    return lax.dot_general(a, b, (((0,), (0,)), ((), ())), preferred_element_type=F32)


def after(value, *earlier):
    return pl.pallas_call(
        lambda *refs: None,
        in_specs=[pl.BlockSpec(memory_space=pl.ANY)] * (1 + len(earlier)),
        out_specs=pl.BlockSpec(memory_space=pl.ANY),
        out_shape=jax.ShapeDtypeStruct(value.shape, value.dtype),
        input_output_aliases={0: 0},
        name="after",
    )(value, *earlier)


def by_head(both, low, inner):
    zero = jnp.zeros_like(both)
    first, second = jnp.where(low, both, zero), jnp.where(low, zero, both)
    if inner:
        first, second = second, first
    return jnp.concatenate(
        [jnp.concatenate([first, zero], axis=1), jnp.concatenate([zero, second], axis=1)], axis=0
    )


def listed_keys(starts, spot, top, kv_ref):
    rows = [
        [pl.multiple_of(starts[spot + head * MOVING + i], BLOCK) for i in range(MOVING)]
        for head in range(2)
    ]
    parts = [kv_ref[pl.ds(top, GLOB * BLOCK), :]]
    parts += [kv_ref[pl.ds(at, BLOCK), :] for at in rows[0][:3]]
    parts += [
        jnp.concatenate(
            [kv_ref[pl.ds(first, BLOCK), :PAIR], kv_ref[pl.ds(second, BLOCK), PAIR:]], axis=1
        )
        for first, second in zip(rows[0][3:], rows[1][3:])
    ]
    return jnp.concatenate(parts, axis=0), rows


def loader(refs, streamed):
    if not streamed:
        return lambda i: refs[i][...]
    buffer, semaphore = streamed

    def load(i):
        copy = pltpu.make_async_copy(refs[i], buffer, semaphore)
        copy.start()
        copy.wait()
        return buffer[...]

    return load


def softmax(scores):
    raised = jnp.exp(scores - jnp.max(scores, axis=0, keepdims=True))
    return (raised * (1.0 / jnp.sum(raised, axis=0, keepdims=True))).astype(BF16)


def by_core(grad, core, parts):
    half = grad.shape[0] // parts // 2
    halves = [
        jnp.concatenate([grad[at : at + half] for at in range(i * half, grad.shape[0], 2 * half)])
        for i in range(2)
    ]
    first = core == 0
    return jnp.where(first, halves[0], halves[1]), jnp.where(first, halves[1], halves[0])


def forward_kernel(
    starts, limits, x_ref, w_ref, b_ref, *rest, first, row_blocks, extra, shards, waits
):
    seen_refs = rest[:shards]
    q_ref, kv_ref, out_ref, p_ref, pg_ref = rest[shards + waits :][:5]
    tokens = loader(seen_refs, rest[shards + waits + 5 :])
    top = pl.multiple_of(starts[row_blocks * H * MOVING], BLOCK)
    pair = first + pl.program_id(0)
    rows = row_blocks * BLOCK
    low = lax.broadcasted_iota(jnp.int32, (1, PAIR), 1) < HD
    within = lax.broadcasted_iota(jnp.int32, (BLOCK, PAIR), 0)

    queries = dot(x_ref[...], w_ref[:, :PAIR]) + b_ref[0, :, :PAIR]
    q_ref[...] = (queries.astype(BF16).astype(F32) * FACTOR).astype(BF16)

    for i in range(shards):
        kv = dot(tokens(i), w_ref[:, PAIR:]) + b_ref[0, :, PAIR:]
        kv_ref[i * rows : (i + 1) * rows, :] = kv.astype(BF16)

    def some_blocks(group, carry):
        blocks = [group * TOGETHER + i for i in range(TOGETHER)]
        ats = [pl.ds(pl.multiple_of(block * BLOCK, BLOCK), BLOCK) for block in blocks]
        spots = [(block * H + 2 * pair) * MOVING for block in blocks]
        kvs = [listed_keys(starts, spot, top, kv_ref)[0] for spot in spots]
        scores = [dot_t(kv, by_head(q_ref[at, :], low, True)) for kv, at in zip(kvs, ats)]
        probs = []
        for some, spot in zip(scores, spots):
            masked = [some[: GLOB * BLOCK]]
            for i in range(MOVING):
                limit = jnp.where(low, limits[spot + i], limits[spot + MOVING + i])
                here = some[(GLOB + i) * BLOCK : (GLOB + i + 1) * BLOCK]
                masked.append(jnp.where(within < limit, here, NEGATIVE))
            probs.append(softmax(jnp.concatenate(masked, axis=0)))
        outs = [t_dot(some, kv) for some, kv in zip(probs, kvs)]
        for block, at, some, out in zip(blocks, ats, probs, outs):
            p_ref[block, 0] = some
            out_ref[at, :] = jnp.where(low, out[:BLOCK, :PAIR], out[BLOCK:, PAIR:]).astype(BF16)
        return carry

    lax.fori_loop(0, row_blocks // TOGETHER, some_blocks, 0)

    wide = by_head(q_ref[rows : rows + extra, :], low, True)
    within = lax.broadcasted_iota(jnp.int32, (rows, 2 * extra), 0)
    scores = []
    for i in range(shards):
        limit = limits[row_blocks * H * MOVING + i]
        here = dot_t(kv_ref[i * rows : (i + 1) * rows, :], wide)
        scores.append(jnp.where(within < limit, here, NEGATIVE))
    summit = jnp.max(reduce(jnp.maximum, scores), axis=0, keepdims=True)
    raised = [jnp.exp(here - summit) for here in scores]
    share = 1.0 / jnp.sum(reduce(jnp.add, raised), axis=0, keepdims=True)
    out = None
    for i in range(shards):
        here = slice(i * rows, (i + 1) * rows)
        probs = (raised[i] * share).astype(BF16)
        pg_ref[0, here, :] = probs
        term = t_dot(probs, kv_ref[here, :])
        out = term if out is None else out + term
    out_ref[rows : rows + extra, :] = jnp.where(
        low, out[:extra, :PAIR], out[extra:, PAIR:]
    ).astype(BF16)


def backward_kernel(
    starts,
    x_ref,
    q_ref,
    do_ref,
    kv_ref,
    p_ref,
    pg_ref,
    *rest,
    first,
    row_blocks,
    extra,
    shards,
    parts,
    waits,
):
    seen_refs = rest[:shards]
    dq_ref, dkv_ref, near_ref, away_ref, qsum_ref, vsum_ref, acc = rest[shards + waits :][:7]
    tokens = loader(seen_refs, rest[shards + waits + 7 :])
    core = starts[row_blocks * H * MOVING + 1]
    top = pl.multiple_of(starts[row_blocks * H * MOVING], BLOCK)
    pair = first + pl.program_id(0)
    rows = row_blocks * BLOCK
    low = lax.broadcasted_iota(jnp.int32, (1, PAIR), 1) < HD

    last = slice(rows, rows + extra)
    wide_do = by_head(do_ref[last, :], low, False)
    cuts = [slice(i * rows, (i + 1) * rows) for i in range(shards)]
    dps = [dot_t(kv_ref[here, :], wide_do) for here in cuts]
    terms = [pg_ref[0, here, :].astype(F32) * dp for here, dp in zip(cuts, dps)]
    delta = jnp.sum(reduce(jnp.add, terms), axis=0, keepdims=True)
    rows_in = jnp.concatenate([wide_do, by_head(q_ref[last, :], low, True)], axis=0)
    dq = None
    for here, dp in zip(cuts, dps):
        probs = pg_ref[0, here, :]
        ds = (probs.astype(F32) * (dp - delta)).astype(BF16)
        term = t_dot(ds, kv_ref[here, :])
        dq = term if dq is None else dq + term
        acc[here, :] = dot(jnp.concatenate([probs, ds], axis=1), rows_in)
    dq = jnp.where(low, dq[extra:, PAIR:], dq[:extra, :PAIR]) * FACTOR
    dq_ref[last, :] = dq.astype(BF16)

    def some_blocks(group, carry):
        blocks = [group * TOGETHER + i for i in range(TOGETHER)]
        ats = [pl.ds(pl.multiple_of(block * BLOCK, BLOCK), BLOCK) for block in blocks]
        listed = [
            listed_keys(starts, (block * H + 2 * pair) * MOVING, top, kv_ref) for block in blocks
        ]
        kvs = [kv for kv, _ in listed]
        dos = [by_head(do_ref[at, :], low, False) for at in ats]
        dps = [dot_t(kv, do) for kv, do in zip(kvs, dos)]
        probs = [p_ref[block, 0] for block in blocks]
        dss = []
        for some, dp in zip(probs, dps):
            wide = some.astype(F32)
            dss.append((wide * (dp - jnp.sum(wide * dp, axis=0, keepdims=True))).astype(BF16))
        dqs = [t_dot(ds, kv) for ds, kv in zip(dss, kvs)]
        dkvs = [
            dot(
                jnp.concatenate([some, ds], axis=1),
                jnp.concatenate([do, by_head(q_ref[at, :], low, True)], axis=0),
            )
            for some, ds, do, at in zip(probs, dss, dos, ats)
        ]
        for at, dq in zip(ats, dqs):
            dq = jnp.where(low, dq[BLOCK:, PAIR:], dq[:BLOCK, :PAIR]) * FACTOR
            dq_ref[at, :] = dq.astype(BF16)
        acc[pl.ds(top, GLOB * BLOCK), :] += reduce(jnp.add, [d[: GLOB * BLOCK] for d in dkvs])
        for dkv, (_, places) in zip(dkvs, listed):
            for i in range(MOVING):
                here = dkv[(GLOB + i) * BLOCK : (GLOB + i + 1) * BLOCK]
                if i < 3:
                    acc[pl.ds(places[0][i], BLOCK), :] += here
                else:
                    acc[pl.ds(places[0][i], BLOCK), :PAIR] += here[:, :PAIR]
                    acc[pl.ds(places[1][i], BLOCK), PAIR:] += here[:, PAIR:]
        return carry

    lax.fori_loop(0, row_blocks // TOGETHER, some_blocks, 0)
    dkv_ref[...] = acc[...].astype(BF16)
    total = jnp.sum(acc[...], axis=0, keepdims=True)
    vsum_ref[0] = jnp.where(low, total[:, :PAIR], total[:, PAIR:])
    total = jnp.sum(dq_ref[...].astype(F32), axis=0, keepdims=True)
    qsum_ref[0] = jnp.concatenate([total[:, HD:], total[:, :HD]], axis=1)
    near, away = by_core(t_dot(x_ref[...], dq_ref[...]), core, parts)
    near_ref[:, :PAIR], away_ref[:, :PAIR] = near.astype(BF16), away.astype(BF16)
    total = None
    for i in range(shards):
        term = t_dot(tokens(i), dkv_ref[i * rows : (i + 1) * rows, :])
        total = term if total is None else total + term
    near, away = by_core(total, core, parts)
    near_ref[:, PAIR:], away_ref[:, PAIR:] = near.astype(BF16), away.astype(BF16)


def piece_specs(rows, width, shards):
    if shards > PIECES:
        scratch = [pltpu.VMEM((rows, width), BF16), pltpu.SemaphoreType.DMA]
        return [pl.BlockSpec(memory_space=pl.ANY)] * shards, scratch
    spec = pl.BlockSpec((rows, width), lambda p, *_: (0, 0), pipeline_mode=pl.Buffered(1))
    return [spec] * shards, []


def long_spec(shape, place, shards):
    if shards > PIECES:
        return pl.BlockSpec(shape, place, pipeline_mode=pl.Buffered(1))
    return pl.BlockSpec(shape, place)


def attention_forward(starts, limits, x, pieces, weights, b_qkv, waits, first, count, extra):
    rows, width, shards = x.shape[0], x.shape[1], len(pieces)
    seq = shards * (rows - extra)
    row_blocks = (rows - extra) // BLOCK
    specs, scratch = piece_specs(rows - extra, width, shards)
    return pl.pallas_call(
        partial(
            forward_kernel,
            first=first,
            row_blocks=row_blocks,
            extra=extra,
            shards=shards,
            waits=len(waits),
        ),
        grid_spec=pltpu.PrefetchScalarGridSpec(
            num_scalar_prefetch=2,
            grid=(count,),
            in_specs=[
                pl.BlockSpec((rows, width), lambda p, *_: (0, 0)),
                pl.BlockSpec((width, 3 * PAIR), lambda p, *_: (0, p)),
                pl.BlockSpec((1, 1, 3 * PAIR), lambda p, *_: (first + p, 0, 0)),
            ]
            + specs
            + [pl.BlockSpec(memory_space=pl.ANY)] * len(waits),
            out_specs=[
                pl.BlockSpec((rows, PAIR), lambda p, *_: (0, p)),
                long_spec((seq, 2 * PAIR), lambda p, *_: (0, p), shards),
                pl.BlockSpec((rows, PAIR), lambda p, *_: (0, p)),
                pl.BlockSpec((row_blocks, 1, LISTED, PAIR), lambda p, *_: (0, p, 0, 0)),
                long_spec((1, seq, 2 * extra), lambda p, *_: (p, 0, 0), shards),
            ],
            scratch_shapes=scratch,
        ),
        out_shape=[
            jax.ShapeDtypeStruct((rows, count * PAIR), BF16),
            jax.ShapeDtypeStruct((seq, 2 * count * PAIR), BF16),
            jax.ShapeDtypeStruct((rows, count * PAIR), BF16),
            jax.ShapeDtypeStruct((row_blocks, count, LISTED, PAIR), BF16),
            jax.ShapeDtypeStruct((count, seq, 2 * extra), BF16),
        ],
        compiler_params=pltpu.CompilerParams(vmem_limit_bytes=58 * MIB),
        cost_estimate=taking(10 * count),
        name="attention_forward",
    )(starts, limits, x, weights, b_qkv, *pieces, *waits)


def attention_backward(
    starts, x, pieces, q, do, kv, probs, global_probs, waits, first, offset, count, cost, extra
):
    rows, seq, width, shards = q.shape[0], kv.shape[0], x.shape[1], len(pieces)
    parts = lax.axis_size("wt")
    row_blocks = (rows - extra) // BLOCK
    specs, scratch = piece_specs(rows - extra, width, shards)
    return pl.pallas_call(
        partial(
            backward_kernel,
            first=first,
            row_blocks=row_blocks,
            extra=extra,
            shards=shards,
            parts=parts,
            waits=len(waits),
        ),
        grid_spec=pltpu.PrefetchScalarGridSpec(
            num_scalar_prefetch=1,
            grid=(count,),
            in_specs=[
                pl.BlockSpec((rows, width), lambda p, *_: (0, 0)),
                pl.BlockSpec((rows, PAIR), lambda p, *_: (0, offset + p)),
                pl.BlockSpec((rows, PAIR), lambda p, *_: (0, first + p)),
                long_spec((seq, 2 * PAIR), lambda p, *_: (0, offset + p), shards),
                pl.BlockSpec((row_blocks, 1, LISTED, PAIR), lambda p, *_: (0, offset + p, 0, 0)),
                long_spec((1, seq, 2 * extra), lambda p, *_: (offset + p, 0, 0), shards),
            ]
            + specs
            + [pl.BlockSpec(memory_space=pl.ANY)] * len(waits),
            out_specs=[
                pl.BlockSpec((rows, PAIR), lambda p, *_: (0, p)),
                long_spec((seq, 2 * PAIR), lambda p, *_: (0, p), shards),
                pl.BlockSpec((width // 2, 3 * PAIR), lambda p, *_: (0, p)),
                pl.BlockSpec((width // 2, 3 * PAIR), lambda p, *_: (0, p)),
                pl.BlockSpec((1, 1, PAIR), lambda p, *_: (p, 0, 0)),
                pl.BlockSpec((1, 1, PAIR), lambda p, *_: (p, 0, 0)),
            ],
            scratch_shapes=[pltpu.VMEM((seq, 2 * PAIR), F32), *scratch],
        ),
        out_shape=[
            jax.ShapeDtypeStruct((rows, count * PAIR), BF16),
            jax.ShapeDtypeStruct((seq, 2 * count * PAIR), BF16),
            jax.ShapeDtypeStruct((width // 2, 3 * count * PAIR), BF16),
            jax.ShapeDtypeStruct((width // 2, 3 * count * PAIR), BF16),
            jax.ShapeDtypeStruct((count, 1, PAIR), F32),
            jax.ShapeDtypeStruct((count, 1, PAIR), F32),
        ],
        compiler_params=pltpu.CompilerParams(vmem_limit_bytes=60 * MIB),
        cost_estimate=taking(cost),
        name="attention_backward",
    )(starts, x, q, do, kv, probs, global_probs, *pieces, *waits)


def centered_root(value):
    centered = value - jnp.mean(value, axis=1, keepdims=True)
    root = lax.rsqrt(jnp.mean(centered * centered, axis=1, keepdims=True) + EPSILON)
    return centered * root, root


def norm_back(grad, normed, root):
    mean = jnp.mean(grad, axis=1, keepdims=True)
    return root * (grad - mean - normed * jnp.mean(grad * normed, axis=1, keepdims=True))


def both_pieces(ref, core, columns):
    half = ref.shape[3] // 2
    pieces = []
    for piece in (core, 1 - core):
        blocks = [ref[piece, part] for part in range(ref.shape[1])]
        if columns:
            blocks = [b for block in blocks for b in (block[:, :half], block[:, half:])]
        pieces.append(jnp.concatenate(blocks, axis=0))
    return jnp.concatenate(pieces, axis=1 if columns else 0)


def layer_kernel(
    me,
    x_ref,
    att0_ref,
    att1_ref,
    cot_ref,
    keep_ref,
    wo_ref,
    we_ref,
    wc_ref,
    be_ref,
    vec_ref,
    out_ref,
    one_ref,
    do_ref,
    wok_ref,
    woa_ref,
    ck_ref,
    ca_ref,
    ek_ref,
    ea_ref,
    beg_ref,
    vecg_ref,
    norm_ref,
    root_ref,
    low_ref,
    slope_ref,
    hid_ref,
    acc_ref,
    two_ref,
):
    step = pl.program_id(0)
    core = me[0] % 2
    row = lambda i: vec_ref[i : i + 1, :]

    @pl.when(step == 0)
    def _():
        cut = att0_ref.shape[1]
        branch = dot(att0_ref[...], wo_ref[:cut]) + dot(att1_ref[...], wo_ref[cut:])
        normed, root = centered_root(x_ref[...].astype(F32) + branch + row(0))
        norm_ref[...] = normed
        root_ref[...] = root
        normed = normed * row(1) + row(2)
        low_ref[...] = normed.astype(BF16)
        acc_ref[...] = normed + row(3)

    @pl.when(step < 4)
    def _():
        bias = jnp.concatenate([be_ref[core], be_ref[1 - core]], axis=1)
        u = dot(low_ref[...], both_pieces(we_ref, core, True)) + bias
        square = u * u
        t = jnp.tanh(SLOPE * u * (1.0 + CUBIC * square))
        half = 0.5 * (1.0 + t)
        hidden = (u * half).astype(BF16)
        slope_ref[step] = half + (0.5 * SLOPE) * u * (1.0 - t * t) * (
            1.0 + (3.0 * CUBIC) * square
        )
        hid_ref[step] = hidden
        acc_ref[...] += dot(hidden, both_pieces(wc_ref, core, False))

    @pl.when(step == 4)
    def _():
        normed, root = centered_root(acc_ref[...])
        out_ref[...] = (keep_ref[...] * (normed * row(4) + row(5))).astype(BF16)
        cot = cot_ref[...].astype(F32)
        vecg_ref[4:5, :] = jnp.sum(cot * normed, axis=0, keepdims=True)
        vecg_ref[5:6, :] = jnp.sum(cot, axis=0, keepdims=True)
        two = norm_back(cot * row(4), normed, root)
        acc_ref[...] = two
        two = two.astype(BF16)
        two_ref[...] = two
        vecg_ref[3:4, :] = jnp.sum(two.astype(F32), axis=0, keepdims=True)

    @pl.when(step >= 4)
    def _():
        at = step - 4
        piece = ck_ref.shape[1]
        grad = t_dot(hid_ref[at], two_ref[...]).astype(BF16)
        ck_ref[0], ca_ref[0] = grad[:piece], grad[piece:]
        grad = dot_t(two_ref[...], both_pieces(wc_ref, core, False)) * slope_ref[at]
        grad = grad.astype(BF16)
        total = jnp.sum(grad.astype(F32), axis=0, keepdims=True)
        beg_ref[core], beg_ref[1 - core] = total[:, :piece], total[:, piece:]
        acc_ref[...] += dot_t(grad, both_pieces(we_ref, core, True))
        grad = t_dot(low_ref[...], grad).astype(BF16)
        ek_ref[0], ea_ref[0] = grad[:, :piece], grad[:, piece:]

    @pl.when(step == 7)
    def _():
        first = acc_ref[...]
        normed = norm_ref[...]
        vecg_ref[1:2, :] = jnp.sum(first * normed, axis=0, keepdims=True)
        vecg_ref[2:3, :] = jnp.sum(first, axis=0, keepdims=True)
        one = norm_back(first * row(1), normed, root_ref[...])
        one_ref[...] = one
        one = one.astype(BF16)
        vecg_ref[0:1, :] = jnp.sum(one.astype(F32), axis=0, keepdims=True)
        vecg_ref[6:8, :] = jnp.zeros((2, one.shape[1]), F32)
        grad = [t_dot(att_ref[...], one) for att_ref in (att0_ref, att1_ref)]
        near, away = by_core(jnp.concatenate(grad, axis=0), core, we_ref.shape[1])
        wok_ref[...], woa_ref[...] = near.astype(BF16), away.astype(BF16)
        do_ref[...] = dot_t(one, wo_ref[...]).astype(BF16)


def layer(c, x, attended, cot, keep, w_output, w_hidden, b_expand, vectors):
    rows, width = x.shape
    parts, piece = w_hidden.shape[1], b_expand.shape[2]
    each = piece // parts
    steps = PIECES // 2
    whole = lambda *shape: pl.BlockSpec(shape, lambda s, me: (0,) * len(shape))
    chip = lambda s, me: (s % steps) ^ ((me[0] % PIECES) // 2)
    sent = lambda *shape: pl.BlockSpec((1, *shape), lambda s, me: (jnp.maximum(s - steps, 0), 0, 0))
    return pl.pallas_call(
        layer_kernel,
        grid_spec=pltpu.PrefetchScalarGridSpec(
            num_scalar_prefetch=1,
            grid=(2 * steps,),
            in_specs=[
                whole(rows, width),
                *[whole(*a.shape) for a in attended],
                whole(rows, width),
                whole(rows, 1),
                whole(width, width),
                pl.BlockSpec((2, parts, each, width), lambda s, me: (chip(s, me), 0, 0, 0)),
                pl.BlockSpec((2, parts, each, width), lambda s, me: (chip(s, me), 0, 1, 0)),
                pl.BlockSpec((2, 1, piece), lambda s, me: (chip(s, me), 0, 0)),
                whole(8, width),
            ],
            out_specs=[
                whole(rows, width),
                whole(rows, width),
                whole(rows, width),
                whole(width // 2, width),
                whole(width // 2, width),
                sent(piece, width),
                sent(piece, width),
                sent(width, piece),
                sent(width, piece),
                pl.BlockSpec((2, 1, piece), lambda s, me: (chip(jnp.maximum(s - steps, 0), me), 0, 0)),
                whole(8, width),
            ],
            scratch_shapes=[
                pltpu.VMEM((rows, width), F32),
                pltpu.VMEM((rows, 1), F32),
                pltpu.VMEM((rows, width), BF16),
                pltpu.VMEM((steps, rows, 2 * piece), F32),
                pltpu.VMEM((steps, rows, 2 * piece), BF16),
                pltpu.VMEM((rows, width), F32),
                pltpu.VMEM((rows, width), BF16),
            ],
        ),
        out_shape=[
            jax.ShapeDtypeStruct((rows, width), BF16),
            jax.ShapeDtypeStruct((rows, width), F32),
            jax.ShapeDtypeStruct((rows, width), BF16),
            jax.ShapeDtypeStruct((width // 2, width), BF16),
            jax.ShapeDtypeStruct((width // 2, width), BF16),
            jax.ShapeDtypeStruct((steps, piece, width), BF16),
            jax.ShapeDtypeStruct((steps, piece, width), BF16),
            jax.ShapeDtypeStruct((steps, width, piece), BF16),
            jax.ShapeDtypeStruct((steps, width, piece), BF16),
            jax.ShapeDtypeStruct((PIECES, 1, piece), F32),
            jax.ShapeDtypeStruct((8, width), F32),
        ],
        compiler_params=pltpu.CompilerParams(vmem_limit_bytes=58 * MIB),
        cost_estimate=taking(35),
        name="layer",
    )(
        jnp.reshape(c, (1,)).astype(jnp.int32),
        x,
        *attended,
        cot,
        keep,
        w_output,
        w_hidden,
        w_hidden,
        b_expand,
        vectors,
    )


def pair_sum(grad_refs, weight_refs, columns, at):
    grads = jnp.concatenate([ref[...] for ref in grad_refs], axis=1)
    weights = []
    for group, offset, count in BACK:
        for pair in range(offset, offset + count):
            start = 3 * PAIR * pair + at
            weights.append(weight_refs[group][:, start : start + columns])
    return dot_t(grads, jnp.concatenate(weights, axis=1))


def token_kernel(me, *refs, away, extra, count):
    sides = len(BACK)
    dkv_refs, w_refs = refs[:sides], refs[sides : sides + 2]
    c, step = me[0], pl.program_id(0)
    piece = 2 * step + (1 if away else 0)
    half = dkv_refs[0].shape[0] // 2
    if away:
        dq_refs, one_ref = refs[sides + 2 : 2 * sides + 2], refs[2 * sides + 2]
        out_ref, share_ref = refs[-2:]

        @pl.when(step == 0)
        def _():
            share_ref[...] = one_ref[...] + pair_sum(dq_refs, w_refs, PAIR, 0)

        share = lambda: share_ref[2 * half : 2 * half + extra, :]
    else:
        share_ref, out_ref = refs[sides + 2], refs[-1]
        share = lambda: share_ref[...]
    total = pair_sum(dkv_refs, w_refs, 2 * PAIR, PAIR).astype(BF16)
    out_ref[0, 0], out_ref[1, 0] = total[:half], total[half:]

    @pl.when((piece == c) & (c < count))
    def _():
        at = pl.ds(pl.multiple_of(c * extra, extra), extra)
        out_ref[0, 0, at, :] = (out_ref[0, 0, at, :].astype(F32) + share()).astype(BF16)


def token_share(c, dkvs, weights, more, away, waits, rows, extra, count):
    seq, width = dkvs[0].shape[0], weights[0].shape[0]
    chips = seq // rows // 2
    other = 1 if away else 0
    full = lambda a: pl.BlockSpec(a.shape, lambda j, me: (0,) * a.ndim)
    out_specs = [pl.BlockSpec((2, 1, rows // 2, width), lambda j, me: (0, j, 0, 0))]
    out_shape = [jax.ShapeDtypeStruct((2, chips, rows // 2, width), BF16)]
    if away:
        out_specs.append(pl.BlockSpec((rows + extra, width), lambda j, me: (0, 0)))
        out_shape.append(jax.ShapeDtypeStruct((rows + extra, width), F32))
    return pl.pallas_call(
        partial(token_kernel, away=away, extra=extra, count=count),
        grid_spec=pltpu.PrefetchScalarGridSpec(
            num_scalar_prefetch=1,
            grid=(chips,),
            in_specs=[
                pl.BlockSpec((rows, a.shape[1]), lambda j, me: (2 * j + other, 0))
                for a in dkvs
            ]
            + [full(a) for a in (*weights, *more)]
            + [pl.BlockSpec(memory_space=pl.ANY)] * len(waits),
            out_specs=out_specs,
        ),
        out_shape=out_shape,
        compiler_params=pltpu.CompilerParams(vmem_limit_bytes=48 * MIB),
        cost_estimate=taking(0.5),
        name="token_share",
    )(jnp.reshape(c, (1,)).astype(jnp.int32), *dkvs, *weights, *more, *waits)


def by_pair(queries, keys, values):
    count = queries.shape[0]
    together = [a.reshape(count, PAIRS, PAIR) for a in (queries, keys, values)]
    together = jnp.concatenate(together, axis=2).reshape(count * PAIRS, 3 * PAIR)
    places = jnp.arange(3 * PAIR, dtype=jnp.int32)
    source = jnp.array((1, 0, 4, 2, 3, 5), jnp.int32)[places // HD] * HD + places % HD
    return ordered(together, source).astype(BF16).reshape(count, PAIRS * 3 * PAIR)


def column_places(pairs):
    start = jnp.arange(pairs, dtype=jnp.int32)[:, None, None] * (3 * PAIR)
    inner = jnp.arange(HD, dtype=jnp.int32)
    for spots in ((1, 0), (3, 4), (2, 5)):
        yield (start + jnp.array(spots, jnp.int32)[:, None] * HD + inner).reshape(-1)


def swapped(value, bit):
    shards = lax.axis_size("ctx")
    return lax.ppermute(value, "ctx", [(i, i ^ bit) for i in range(shards)])


def own_bit(bit):
    return (lax.axis_index("ctx") // bit) % 2


def added(keep, came):
    return (keep.astype(F32) + came.astype(F32)).astype(BF16)


def halved(value, axis, bit):
    mine = own_bit(bit)
    away = lax.dynamic_index_in_dim(value, 1 - mine, axis, keepdims=False)
    keep = lax.dynamic_index_in_dim(value, mine, axis, keepdims=False)
    return added(keep, swapped(away, bit))


def doubled(value, bit):
    other = swapped(value, bit)
    mine = own_bit(bit) == 0
    return jnp.stack([jnp.where(mine, value, other), jnp.where(mine, other, value)])


def plane_gather(value):
    value = value[None]
    for bit in (1, 2, 4):
        value = doubled(value, bit)
        value = value.reshape(-1, *value.shape[2:])
    return value


def line_step(value, bit):
    parts = lax.axis_size("wt")
    other = lax.ppermute(value, "wt", [(i, i ^ bit) for i in range(parts)])
    mine = lax.axis_index("wt") // bit % 2 == 0
    return jnp.concatenate([jnp.where(mine, value, other), jnp.where(mine, other, value)])


def line_gather(value, bit=1):
    while bit < lax.axis_size("wt"):
        value = line_step(value, bit)
        bit *= 2
    return value


def token_gather(own):
    shards, half = lax.axis_size("ctx"), own.shape[0] // 2
    along_x, along_y = swapped(own, 2), swapped(own, 4)
    far = jnp.concatenate([swapped(along_y[:half], 2), swapped(along_x[half:], 4)], axis=0)
    pieces = []
    for piece in (own, along_x, along_y, far):
        pieces += [piece, swapped(piece, 1)]
    bit = PIECES
    while bit < shards:
        pieces += [swapped(piece, bit) for piece in pieces]
        bit *= 2
    return pieces


def far_sum(value, shards):
    if shards == PIECES:
        return value
    return lax.psum(value, "ctx", axis_index_groups=across_groups(shards))


def same_core(shards, block):
    return [list(range(s + k, s + block, 2)) for s in range(0, shards, block) for k in range(2)]


def rows_start(near, came):
    parts, columns = lax.axis_size("wt"), near.shape[1]
    near, came = (a.reshape(parts, PIECES // 2, -1, columns) for a in (near, came))
    return jnp.transpose(added(near, came), (1, 0, 2, 3)).reshape(parts * PIECES // 2, -1, columns)


def rows_send(sums):
    shards, parts = lax.axis_size("ctx"), lax.axis_size("wt")
    sums = far_sum(sums, shards)
    groups = [[i * parts + w for i in g for w in range(parts)] for g in same_core(shards, PIECES)]
    return lax.all_to_all(
        sums, ("ctx", "wt"), split_axis=0, concat_axis=0, axis_index_groups=groups, tiled=True
    )


def rows_add(sums):
    return jnp.sum(sums.astype(F32), axis=0).astype(BF16)


def rows_sum(sums):
    return rows_add(rows_send(sums))


def ordered(value, source):
    rows = jnp.arange(value.shape[1], dtype=jnp.int32)
    return dot(value, (rows[:, None] == source[None, :]).astype(BF16))


def start_kernel(me, q_ref, k_ref, v_ref, o_ref, e_ref, c_ref, *rest, parts):
    vectors, (lead_ref, more_ref) = rest[:-2], rest[-2:]
    c = me[0]
    half, width = lead_ref.shape[0] - 8, lead_ref.shape[1]
    piece = c % PIECES
    own = pl.ds(pl.multiple_of(c % 2 * half, 16), half)
    low = lax.broadcasted_iota(jnp.int32, (1, PAIR), 1) < HD
    flip = lambda a: jnp.concatenate([a[:, HD:], a[:, :HD]], axis=1)
    columns = []
    for pair in range(PAIRS):
        at = slice(pair * PAIR, (pair + 1) * PAIR)
        q, k, v = (ref[own, at].astype(F32) for ref in (q_ref, k_ref, v_ref))
        k = flip(k)
        columns += [flip(q), jnp.where(low, v, k), jnp.where(low, k, v)]
    ahead = 3 * AHEAD
    small = [r[...].astype(F32).reshape(1, -1) for r in vectors]
    some = [jnp.concatenate(small[i : i + parts], axis=1) for i in range(0, 2 * parts, parts)]
    some += small[2 * parts :]
    small = jnp.concatenate(some + [jnp.zeros((8 - len(some), width), F32)], axis=0)
    lead = jnp.concatenate([jnp.concatenate(columns[:ahead], axis=1), small], axis=0)
    lead_ref[...] = lead.astype(BF16)

    run = e_ref.shape[1] // parts // PIECES
    block = e_ref.shape[1] // parts
    runs = []
    for part in range(parts):
        here = e_ref[:, part * block : (part + 1) * block].astype(F32)
        runs.append(pltpu.roll(here, block - piece * run, 1)[:, :run])
    runs = jnp.concatenate(runs, axis=1)
    count = runs.shape[0] // 2
    more_ref[:count] = jnp.concatenate([runs[:count], runs[count:]], axis=1).astype(BF16)
    rows = c_ref.shape[0] // PIECES
    more_ref[count : count + rows] = c_ref[pl.ds(pl.multiple_of(piece * rows, 16), rows), :]
    at = count + rows
    rows = o_ref.shape[0] // PIECES
    whole = o_ref[...].astype(F32)
    turned = pltpu.roll(whole, whole.shape[0] - piece * rows, 0)
    rows = -(-rows // 16) * 16
    more_ref[at : at + rows] = turned[:rows].astype(BF16)
    at += rows
    left = (PAIRS - AHEAD) * 3 * PAIR // width
    for i in range(left):
        some = columns[ahead + i * width // PAIR : ahead + (i + 1) * width // PAIR]
        some = jnp.concatenate(some, axis=1)
        some = jnp.where(c // (2 << i) % 2 == 0, some[: half // 2], some[half // 2 :])
        more_ref[at : at + half // 2] = some.astype(BF16)
        at += half // 2


def start_arrays(c, weights, vectors, parts):
    half, width = weights[0].shape[0] // 2, weights[0].shape[1]
    count = weights[4].shape[0] // 2 + weights[5].shape[0] // PIECES
    count += (PAIRS - AHEAD) * 3 * PAIR // width * half // 2
    count += -(-weights[3].shape[0] // PIECES // 16) * 16
    full = lambda shape: pl.BlockSpec(shape, lambda i: (0,) * len(shape))
    shapes = [(half + 8, width), (count, width)]
    return pl.pallas_call(
        partial(start_kernel, parts=parts),
        grid=(1,),
        in_specs=[pl.BlockSpec(memory_space=pltpu.SMEM)] + [full(a.shape) for a in (*weights, *vectors)],
        out_specs=[full(shape) for shape in shapes],
        out_shape=[jax.ShapeDtypeStruct(shape, BF16) for shape in shapes],
        compiler_params=pltpu.CompilerParams(vmem_limit_bytes=60 * MIB),
        cost_estimate=taking(3),
        name="start_arrays",
    )(jnp.reshape(c, (1,)).astype(jnp.int32), *weights, *vectors)


def vector_kernel(*refs, parts):
    sides = len(BACK)
    joined = lambda some: jnp.concatenate([r[i] for r in some for i in range(r.shape[0])], axis=1)
    grads_ref, expand_ref, _, out_ref = refs[2 * sides :]
    rows = [joined(refs[:sides]), joined(refs[sides : 2 * sides])]
    rows += [grads_ref[i : i + 1, :] for i in (0, 3, 1, 2, 4, 5)]
    width = out_ref.shape[1]
    share, run = width // parts, expand_ref.shape[2] // parts
    out = []
    for part in range(parts):
        cuts = [row[:, part * share : (part + 1) * share] for row in rows]
        out += [jnp.concatenate(cuts[i : i + parts], axis=1) for i in range(0, len(cuts), parts)]
        cuts = [expand_ref[p, :, part * run : (part + 1) * run] for p in range(PIECES)]
        out.append(jnp.concatenate(cuts, axis=1))
        out.append(jnp.zeros((PIECES - len(rows) // parts - 1, width), F32))
    out_ref[...] = jnp.concatenate(out, axis=0).astype(BF16)


def vector_rows(q_sums, v_sums, grads, expand_grads, wait, parts):
    return pl.pallas_call(
        partial(vector_kernel, parts=parts),
        in_specs=[pl.BlockSpec(memory_space=pltpu.VMEM)] * (2 * len(BACK) + 2)
        + [pl.BlockSpec(memory_space=pl.ANY)],
        out_shape=jax.ShapeDtypeStruct((parts * PIECES, grads.shape[1]), BF16),
        cost_estimate=taking(1),
        name="vector_rows",
    )(*q_sums, *v_sums, grads, expand_grads, wait)


def expand_kernel(in_ref, out_ref):
    pieces, half, run = in_ref.shape[0], in_ref.shape[1], in_ref.shape[2] // 2
    parts = out_ref.shape[1] // in_ref.shape[2]
    count = run // parts
    for lower in range(2):
        for part in range(parts):
            at = lower * run + part * count
            runs = [in_ref[p, :, at : at + count].astype(F32) for p in range(pieces)]
            out_ref[
                lower * half : (lower + 1) * half, part * 2 * run : (part + 1) * 2 * run
            ] = jnp.concatenate(runs, axis=1)


def expand_columns(gathered, each_piece, parts):
    width = gathered.shape[2]
    return pl.pallas_call(
        expand_kernel,
        grid=(1,),
        in_specs=[pl.BlockSpec((PIECES, each_piece, width), lambda i: (0, 1, 0))],
        out_specs=pl.BlockSpec((2 * each_piece, parts * width), lambda i: (0, 0)),
        out_shape=jax.ShapeDtypeStruct((2 * each_piece, parts * width), F32),
        compiler_params=pltpu.CompilerParams(vmem_limit_bytes=24 * MIB),
        cost_estimate=taking(2),
        name="expand_columns",
    )(gathered)


def body(
    tokens,
    cotangent,
    lengths,
    rand_blocks,
    query_weight,
    key_weight,
    value_weight,
    output_weight,
    expand_weight,
    contract_weight,
    query_bias,
    value_bias,
    output_bias,
    expand_bias,
    contract_bias,
    attn_gain,
    attn_shift,
    ffn_gain,
    ffn_shift,
):
    shards = lax.axis_size("ctx")
    parts = lax.axis_size("wt")
    c = lax.axis_index("ctx")
    rows, width = tokens.shape[1], tokens.shape[2]
    row_blocks = rows // BLOCK
    seq = shards * rows
    global_count = GLOB * BLOCK
    extra = 16 * (-(-global_count // (16 * shards)))
    hidden_width = expand_weight.shape[1]
    part = expand_weight.shape[0]
    piece = hidden_width // PIECES
    length = lengths[0]
    inputs = tokens[0]

    pieces = token_gather(inputs)
    half = part // 2
    leading, behind = start_arrays(
        c,
        (query_weight, key_weight, value_weight, output_weight, expand_weight, contract_weight),
        (
            query_bias,
            value_bias,
            output_bias,
            contract_bias,
            attn_gain,
            attn_shift,
            ffn_gain,
            ffn_shift,
            expand_bias,
        ),
        parts,
    )
    early_lead = line_step(leading[None], 1)
    leading = line_gather(after(early_lead, pieces[2], pieces[4]), 2)
    vectors = leading[:, half:].reshape(parts, -1)
    leading = leading[:, :half]

    def joined(bundle):
        return jnp.transpose(doubled(bundle, 1), (1, 0, 2, 3)).reshape(width, -1)

    weights = [joined(leading)]
    each = width // parts
    b_query, b_value, b_output, b_contract, g_attn, s_attn, g_ffn, s_ffn = (
        vectors[:, i * each : (i + 1) * each].reshape(-1).astype(F32) for i in range(8)
    )
    b_expand = vectors[:, 8 * each : 8 * each + hidden_width // parts].reshape(parts, PIECES, -1)
    b_expand = jnp.transpose(b_expand, (1, 0, 2)).reshape(PIECES, 1, piece).astype(F32)

    each_piece = piece // parts
    o_rows = part // PIECES
    mixed = 2 * each_piece
    w_hidden = lax.all_gather(behind, "wt")
    mixed += -(-o_rows // 16) * 16
    following = w_hidden[:, mixed:].reshape(parts, 2, half // 2, width)
    following = [
        jnp.transpose(doubled(following[:, i], 2 << i), (1, 0, 2, 3)).reshape(parts, half, width)
        for i in range(2)
    ]
    following = jnp.concatenate(following, axis=2)
    w_hidden = w_hidden[:, :mixed]

    start = jnp.minimum(c * extra, global_count - extra)
    more = lax.dynamic_slice_in_dim(pieces[0], start, extra, 0)
    for i in range(1, shards):
        other = lax.dynamic_slice_in_dim(pieces[i], start, extra, 0)
        more = jnp.where(c == i, other, more)
    x = jnp.concatenate([inputs, more], axis=0)
    index = jnp.arange(rows + extra, dtype=jnp.int32)
    position = jnp.where(index < rows, c * rows + index, c * extra + index - rows)
    is_global = position < global_count
    usable = ((position < length) & (is_global == (index >= rows)))[:, None]
    own = c * row_blocks + jnp.arange(row_blocks, dtype=jnp.int32)
    beside = own[:, None, None] + jnp.arange(-1, 2, dtype=jnp.int32)
    listed = jnp.concatenate(
        [jnp.broadcast_to(beside, (row_blocks, H, 3)), rand_blocks[0]], axis=2
    )
    blocks = seq // BLOCK
    inside = (listed >= 0) & (listed < blocks)
    listed = jnp.clip(listed, 0, blocks - 1)
    limits = jnp.where(inside, length - listed * BLOCK, 0).reshape(-1)
    order = jnp.arange(shards, dtype=jnp.int32) ^ c
    limits = jnp.concatenate([limits, length - order * rows])
    starts = (listed // row_blocks ^ c) * rows + listed % row_blocks * BLOCK
    starts = jnp.concatenate([starts.reshape(-1), jnp.stack([c * rows, c % 2])])

    given = jnp.where(c == 0, cotangent[0, :global_count], jnp.zeros((), BF16))
    given = jnp.pad(given, ((0, shards * extra - global_count), (0, 0)))
    given = after(given.reshape(shards, extra, width), pieces[4])
    given = lax.all_to_all(given, "ctx", split_axis=0, concat_axis=0, tiled=True)
    cot = jnp.concatenate([cotangent[0], given[0]], axis=0)
    cot = jnp.where(usable, cot, jnp.zeros((), BF16))

    b_qkv = by_pair(*(b.astype(BF16)[None] for b in (b_query, jnp.zeros_like(b_value), b_value)))
    b_qkv = b_qkv.astype(F32).reshape(PAIRS, 1, 3 * PAIR)
    zero = jnp.zeros_like(b_output)
    vectors = jnp.stack([b_output, g_attn, s_attn, b_contract, g_ffn, s_ffn, zero, zero])
    keep = usable.astype(F32)
    w_hidden = after(
        w_hidden, *pieces[:PIECES:2], leading, cot, starts, limits, b_qkv, vectors, b_expand, keep
    )
    w_hidden = lax.all_gather(w_hidden, "ctx", axis_index_groups=groups_of(shards))
    w_output = w_hidden[:, :, 2 * each_piece : 2 * each_piece + o_rows]
    w_output = jnp.transpose(w_output, (1, 0, 2, 3)).reshape(width, width)
    forward = partial(attention_forward, starts, limits, x, pieces)
    kept = [forward(weights[0], b_qkv, (cot,), *GROUPS[0], extra)]
    weights.append(joined(following))
    kept.append(forward(weights[1], b_qkv, (), *GROUPS[1], extra))

    (
        layer_out,
        grad_one,
        grad_attended,
        o_keep,
        o_away,
        c_keep,
        c_away,
        e_keep,
        e_away,
        expand_bgrad,
        vector_grads,
    ) = layer(
        c,
        x,
        [k[2] for k in kept],
        cot,
        keep,
        w_output,
        w_hidden,
        b_expand,
        vectors,
    )

    def attention_back(side, *waits):
        group, offset, count = BACK[side]
        q, kv, _, probs, global_probs = kept[group]
        first = GROUPS[group][0] + offset
        return attention_backward(
            starts,
            x,
            pieces,
            q,
            grad_attended,
            kv,
            probs,
            global_probs,
            waits,
            first,
            offset,
            count,
            BACK_COST[side],
            extra,
        )

    c_came, e_came = swapped(c_away, 1), swapped(e_away, 1)
    early = [rows_start(o_keep, swapped(o_away, 1))]
    backs = [attention_back(0)]
    steps = PIECES // 2
    c_keep, c_came = (a.reshape(2, 2, piece, width) for a in (c_keep, c_came))
    e_keep, e_came = (a.reshape(2, 2, width, piece) for a in (e_keep, e_came))
    c_away = added(c_keep[:, 1], c_came[:, 1])
    e_away = added(e_keep[1], e_came[1])
    c_came_on, e_came_on = swapped(c_away, 2), swapped(e_away, 4)
    c_keep = added(c_keep[:, 0], c_came[:, 0])
    e_keep = added(e_keep[0], e_came[0])

    early.append(rows_start(backs[0][2], swapped(backs[0][3], 1)))
    early = jnp.concatenate(early, axis=1)
    backs.append(attention_back(1, c_away, e_away, early))
    early = rows_sum(early)
    c_away, e_away = added(c_keep[1], c_came_on[1]), added(e_keep[1], e_came_on[1])
    c_last, e_last = swapped(c_away, 4), swapped(e_away, 2)
    c_keep, e_keep = added(c_keep[0], c_came_on[0]), added(e_keep[0], e_came_on[0])

    middle = rows_start(backs[1][2], swapped(backs[1][3], 1))
    backs.append(attention_back(2, c_away, e_away, early, middle))
    middle = rows_sum(middle)
    c_mine = far_sum(added(c_keep, c_last), shards).reshape(parts, -1, width)
    e_mine = far_sum(added(e_keep, e_last), shards).reshape(parts, 2, -1, piece)
    e_mine = jnp.concatenate([e_mine[:, 0], e_mine[:, 1]], axis=2)
    hidden_sums = jnp.concatenate([c_mine, e_mine], axis=1)
    both = lax.all_to_all(hidden_sums, "wt", split_axis=0, concat_axis=0, tiled=True)
    backs.append(attention_back(3, hidden_sums, middle))

    small = vector_rows([b[4] for b in backs], [b[5] for b in backs], vector_grads, expand_bgrad, backs[3][0], parts)
    small = small.reshape(parts, 2, -1, width)
    near = jnp.concatenate([backs[2][2], backs[3][2]], axis=1).reshape(parts, PIECES // 2, -1, width)
    near = jnp.concatenate(
        [near, lax.dynamic_index_in_dim(small, own_bit(1), 1, keepdims=False)[:, :, None]], axis=2
    )
    far = jnp.concatenate([backs[2][3], backs[3][3]], axis=1).reshape(parts, PIECES // 2, -1, width)
    far = jnp.concatenate(
        [far, lax.dynamic_index_in_dim(small, 1 - own_bit(1), 1, keepdims=False)[:, :, None]], axis=2
    )
    late = rows_start(near.reshape(-1, width), swapped(far, 1))

    share = partial(token_share, c, [b[1] for b in backs], weights)
    count = global_count // extra
    away, own = share(
        [b[0] for b in backs] + [grad_one], True, (late,), rows, extra, count
    )
    both = jnp.sum(after(both, away).astype(F32), axis=0).astype(BF16)
    both = jnp.concatenate([both, early, middle, layer_out[rows:]], axis=0)
    (keep,) = share([own[rows:]], False, (away, both, late), rows, extra, count)
    late = rows_send(late)
    came = swapped(away, 1)
    chips = shards // 2
    if chips > 4:
        keep = added(keep, came)
        while chips > 4:
            keep = added(keep[:, : chips // 2], swapped(keep[:, chips // 2 :], chips))
            chips //= 2
        came = jnp.zeros_like(keep)
    keep, came = (a.reshape(2, 2, 2, rows // 2, width) for a in (keep, came))
    above, below = (keep[0], came[0]), (keep[1], came[1])
    above_sent = added(above[0][:, 1], above[1][:, 1])
    below_sent = added(below[0][1], below[1][1])
    late = rows_add(after(late, above_sent, below_sent))
    above_came, below_came = swapped(above_sent, 2), swapped(below_sent, 4)
    above = added(above[0][:, 0], above[1][:, 0])
    below = added(below[0][0], below[1][0])
    rows_late = late.shape[0]
    late = jnp.pad(late, ((0, -rows_late % 8), (0, 0)))
    late = doubled(late, 1)
    late = doubled(late, 2).reshape(4, -1, width)

    def carried(sent, more, bit):
        count = sent.shape[0]
        flat = swapped(jnp.concatenate([sent, more.reshape(-1, width)], axis=0), bit)
        other = flat[count:].reshape(more.shape)
        mine = own_bit(bit) == 0
        more = jnp.concatenate([jnp.where(mine, more, other), jnp.where(mine, other, more)])
        return flat[:count], more

    hidden_rows = 2 * each_piece
    gathered = lax.all_gather(both, "ctx", axis_index_groups=groups_of(shards))

    contract_wgrad = gathered[:, :each_piece].reshape(-1, width).astype(F32)
    expand_wgrad = expand_columns(gathered, each_piece, parts)
    finished = gathered[:, -extra:].reshape(-1, width)
    on_first = (c == 0) & (index[:rows] < global_count)
    finished = jnp.pad(finished[:global_count], ((0, rows - global_count), (0, 0)))
    layer_out = jnp.where(on_first[:, None], finished, layer_out[:rows])

    above_came = after(above_came, contract_wgrad, expand_wgrad, layer_out)
    below_came = after(below_came, contract_wgrad, expand_wgrad, layer_out)

    above_sent = added(above[1], above_came[1])
    below_sent = added(below[1], below_came[1])
    above_last, late = carried(above_sent, late, 4)
    below_last = swapped(below_sent, 2)
    late = late[:, : rows_late]
    above = above[0].astype(F32) + above_came[0].astype(F32) + above_last.astype(F32)
    below = below[0].astype(F32) + below_came[0].astype(F32) + below_last.astype(F32)
    input_grad = own[:rows] + jnp.concatenate([above, below], axis=0)

    mine = gathered[:, hidden_rows:-extra].reshape(PIECES // 2, 2, 3, -1, width)
    mine = jnp.transpose(mine, (2, 1, 0, 3, 4)).reshape(3, part, width)
    last = late[:, :-1].reshape(PIECES // 2, 2, -1, width)
    last = jnp.transpose(last, (1, 0, 2, 3)).reshape(part, width)
    small = jnp.transpose(late[:, -1].reshape(PIECES // 2, 2, width), (1, 0, 2)).reshape(-1, width)
    small = small.astype(F32)
    small_grads = [small[i // parts, i % parts * each :][:each] for i in range(8)]
    expand_bias_grad = small[2]
    output_wgrad = mine[0].astype(F32)
    places = jnp.concatenate(list(column_places(AHEAD)))
    sides = [ordered(g, places) for g in (mine[1], mine[2], last)]
    query_wgrad, key_wgrad, value_wgrad = (
        jnp.concatenate([g[:, at : at + width // 3] for g in sides], axis=1)
        for at in range(0, width, width // 3)
    )

    return (
        layer_out[None],
        input_grad[None],
        query_wgrad,
        key_wgrad,
        value_wgrad,
        output_wgrad,
        expand_wgrad,
        contract_wgrad,
        small_grads[0],
        small_grads[1],
        small_grads[2],
        expand_bias_grad,
        small_grads[3],
        small_grads[4],
        small_grads[5],
        small_grads[6],
        small_grads[7],
    )


def solution(mesh):
    tokens, weight, vector = P("wt", "ctx", None), P("wt", None), P("wt")
    return jax.shard_map(
        body,
        mesh=mesh,
        in_specs=(tokens, tokens, vector, P("wt", "ctx", None, None)) + (weight,) * 6 + (vector,) * 9,
        out_specs=(tokens, tokens) + (weight,) * 6 + (vector,) * 9,
        check_vma=False,
    )
```
